32 devices in a mesh: dp: 4 (over y, core), expert: 8 (over z, x).
Axes of the slice: x: 2, y: 2, z: 4, core: 2. Of those that a mesh axis runs over, the one named last changes fastest.
Arguments:
- tokens: bfloat16 [2, 2048, 1024], P(None, ('dp', 'expert')), may hold values from -6 to 6
- cotangent: bfloat16 [2, 2048, 1024], P(None, ('dp', 'expert')), may hold values from -6 to 6
- segments: int32 [2, 32, 64], P(None, ('dp', 'expert')), may hold values from 0 to 3, never falling along the last dimension, each value on 1 to 32 neighbouring positions
- value_picks: int32 [2, 2048, 4, 2], P(None, ('dp', 'expert')), may hold values from 0 to 4, all different within a row
- output_picks: int32 [2, 2048, 4, 2], P(None, ('dp', 'expert')), may hold values from 0 to 4, all different within a row
- expert_picks: int32 [2, 2048, 16], P(None, ('dp', 'expert')), may hold values from 0 to 127, all different within a row; in each aligned block of 64 rows (0 to 63, 64 to 127, ..., all dimensions but the last counted through in order) at most 16 rows name the same one
- attn_gain: bfloat16 [1024], P('dp'), may hold values from 0.5 to 2
- query_weight: bfloat16 [1024, 512], P('dp'), may hold values from -0.1875 to 0.1875
- key_weight: bfloat16 [1024, 512], P('dp'), may hold values from -0.1875 to 0.1875
- value_weight: bfloat16 [1024, 2560], P('dp'), may hold values from -0.1875 to 0.1875
- output_expert_weight: bfloat16 [1024, 2560], P('dp'), may hold values from -1 to 1
- value_select: bfloat16 [1024, 20], P('dp'), may hold values from -0.125 to 0.125
- output_select: bfloat16 [1024, 20], P('dp'), may hold values from -0.125 to 0.125
- moe_gain: bfloat16 [1024], P('dp'), may hold values from 0.5 to 2
- router_weight: bfloat16 [1024, 128], P('dp'), may hold values from -0.09375 to 0.09375
- up_weight: bfloat16 [128, 1024, 128], P('expert', 'dp'), may hold values from -0.1875 to 0.1875
- down_weight: bfloat16 [128, 128, 1024], P('expert', None, 'dp'), may hold values from -0.25 to 0.25
Outputs:
- output: float32 [2, 2048, 1024], P(None, ('dp', 'expert'))
- grad_tokens: float32 [2, 2048, 1024], P(None, ('dp', 'expert'))
- grad_attn_gain: float32 [1024], P(('dp', 'expert'))
- grad_query_weight: float32 [1024, 512], P(('dp', 'expert'))
- grad_key_weight: float32 [1024, 512], P(('dp', 'expert'))
- grad_value_weight: float32 [1024, 2560], P(('dp', 'expert'))
- grad_output_weight: float32 [1024, 2560], P(('dp', 'expert'))
- grad_value_select: float32 [1024, 20], P(('dp', 'expert'))
- grad_output_select: float32 [1024, 20], P(('dp', 'expert'))
- grad_moe_gain: float32 [1024], P(('dp', 'expert'))
- grad_router_weight: float32 [1024, 128], P(('dp', 'expert'))
- grad_up_weight: float32 [128, 1024, 128], P('expert', 'dp')
- grad_down_weight: float32 [128, 128, 1024], P('expert', None, 'dp')
The draws below stay inside these ranges and needn't reach their ends.
Inputs may be any that keep to these rules, and one draw needn't show every extreme that they name: `expert_picks`: each token names 16 different experts. Among the 64 tokens of one row of one micro-batch no expert is named more than 16 times, and in some rows an expert is named exactly 16 times. `value_picks`: for each token and head, 2 different experts. `output_picks`: for each token and head, 2 different experts. `segments`: along each row of 64 tokens the numbers never fall; a segment spans at most half a row.
All inputs are finite; a program needn't handle non-finite values.
Results may differ from the reference program's by a relative error of at most 0.013.
The reference program's roundings to bfloat16 on the way count: a program that leaves them out, or rounds other values in their place, can miss the bound.
Values may be sent and summed in bfloat16 or wider, within the bound.
No kernel may reach another device: no remote copies, remote signals or barrier semaphores. Data moves between devices by JAX's collectives and lax.ppermute only.
A program may use at most 192 MiB of HBM per device.

```python
import math
import jax
import jax.numpy as jnp
import numpy as np
from jax import lax

D = 1024
H = 4
DH = 128
EA = 5
ATT_TOP = 2
FF_E = 128
TOP = 16
EXPERTS = 128
ROW_LEN = 64
MICRO = 2
ROWS = 32
TOKENS = 2048
CAP = 16


def strengthened(values, own_key, source, target, parts, factor):
    owner, partner = [(jnp.arange(values.shape[dim]) // (values.shape[dim] // parts)).reshape([-1 if axis == dim else 1 for axis in range(values.ndim)]) for dim in (source, target)]
    chosen = jax.random.permutation(own_key, parts)[partner]
    strong = (owner == chosen) | (owner == (partner + parts // 2) % parts)
    return jnp.where(strong, factor * values, values)


def level_of(stream_key, shape, shards, low, largest):
    level, own = 1.0, jax.random.fold_in(stream_key, 6)
    for axis_at, parts in shards:
        steps = jnp.exp(jax.random.uniform(jax.random.fold_in(own, axis_at), (parts,), jnp.float32, low / len(shards), largest / len(shards)))
        level = level * jnp.repeat(steps, shape[axis_at] // parts).reshape([-1 if axis == axis_at else 1 for axis in range(len(shape))])
    return level


def distinct(stream_key, rows, count, top, lift):
    ranking = jax.random.permutation(jax.random.fold_in(stream_key, 1), count)
    favour = ranking
    for power in range(3):
        favour = favour * favour // count
    favour = favour * lift // count
    lots = jax.random.randint(jax.random.fold_in(stream_key, 2), (rows, count), 0, 4096) + favour
    sure = jax.random.permutation(jax.random.fold_in(stream_key, 3), rows)[jnp.arange(count) % rows]
    lots = jnp.where(jnp.arange(rows)[:, None] == sure[None, :], 1 << 14, lots)
    priority = lots * count + jnp.arange(count)
    return lax.top_k(priority.astype(jnp.int32), top)[1].astype(jnp.int32)


def split_up(count, total, reach, skew):
    loads = [(1 << 20) // math.isqrt(grade ** skew) + 1 for grade in range(2, count + 1)]
    surplus, counts = total - reach - (count - 1), [1] * (count - 1)
    while surplus > 0:
        movable = [i for i in range(count - 1) if counts[i] < reach]
        whole, remaining = sum([loads[i] for i in movable]), surplus
        for i in movable:
            addition = min(reach - counts[i], max(1, remaining * loads[i] // whole), surplus)
            counts[i] = counts[i] + addition
            surplus = surplus - addition
    return np.array([reach] + counts)


def uneven_parts(stream_key, amount, total, most, slope):
    if amount == 2:
        one = jax.random.randint(stream_key, (), max(1, total - most), min(most, total - 1) + 1)
        return jnp.stack([one, total - one])
    lengths = jnp.asarray(split_up(amount, total, most, slope), jnp.int32)
    pairs = (amount - 1) // 2
    giver, sink = lengths[1:1 + 2 * pairs:2], lengths[2:2 + 2 * pairs:2]
    margin = jnp.minimum(giver - 1, most - sink)
    moved = jax.random.randint(jax.random.fold_in(stream_key, 1), (pairs,), 0, 1 << 20) % (margin + 1)
    lengths = lengths.at[1:1 + 2 * pairs:2].set(giver - moved).at[2:2 + 2 * pairs:2].set(sink + moved)
    return lengths[jax.random.permutation(jax.random.fold_in(stream_key, 2), amount)]


def deal_out(own_key, own, number, rows, count, top, most, skew):
    sequence = jax.random.permutation(own_key, count)
    heavy_load, ordinary = load_shares(count, rows * top, most, skew, True), load_shares(count, rows * top, most, skew, False)
    places = jnp.arange(count)

    def named(sizes, rotation):
        used = int((sizes > 0).sum())
        fixed = max(1, used // 4)
        moved = fixed + (places - fixed + rotation * (used - fixed)) % max(1, count - fixed)
        return jnp.zeros((count,), jnp.int32).at[sequence[jnp.where(places < fixed, places, moved)]].set(jnp.asarray(sizes, jnp.int32))

    sizes = jnp.where(number % 4 == 0, named(heavy_load, number // 4), named(ordinary, number - number // 4 - 1))
    mixed = jax.random.permutation(jax.random.fold_in(own, 3), count)
    donor, sink = mixed[0:count // 2 * 2:2], mixed[1:count // 2 * 2:2]
    margin = jnp.minimum(sizes[donor] - 1, most - sizes[sink]) // 2
    margin = jnp.where((donor == sequence[0]) | (sink == sequence[0]) | (sizes[sink] == 0), 0, jnp.maximum(margin, 0))
    moved = jax.random.randint(jax.random.fold_in(own, 4), (count // 2,), 0, 1 << 20) % (margin + 1)
    sizes = sizes.at[donor].add(-moved).at[sink].add(moved)
    members = jnp.searchsorted(jnp.cumsum(sizes), jnp.arange(rows * top), side="right").astype(jnp.int32)
    table = members.reshape(top, rows).T
    table = table[jax.random.permutation(jax.random.fold_in(own, 1), rows)]
    rotation = jax.random.randint(jax.random.fold_in(own, 2), (rows, 1), 0, top)
    return jnp.take_along_axis(table, (jnp.arange(top)[None, :] + rotation) % top, axis=1)


def load_shares(number_of, total, most, slope, full):
    loads = [(1 << 20) // math.isqrt(grade ** slope) + 1 for grade in range(1, number_of + 1)]
    largest = most if full else min(most, max(-(-total // number_of), total * loads[0] // sum(loads)))
    least = 1 if total - largest >= number_of - 1 else 0
    counts, surplus = [largest] + [least] * (number_of - 1), total - largest - least * (number_of - 1)
    while surplus > 0:
        candidates = [i for i in range(1, number_of) if counts[i] < largest] or [i for i in range(1, number_of) if counts[i] < most]
        pool, left = sum([loads[i] for i in candidates]), surplus
        for i in candidates:
            more = min(most - counts[i], max(1, left * loads[i] // pool), surplus)
            counts[i] = counts[i] + more
            surplus = surplus - more
    return np.array(counts)


def centred(key, shape, scale, most, cuts=(), kind=jnp.bfloat16):
    entries = jax.random.normal(key, shape, jnp.float32) * scale
    if len(cuts) > 0:
        entries = level_of(key, shape, cuts, -0.22, 0.18) * entries
    return jnp.clip(entries, min=-most, max=most).astype(kind)


def bell_draw_with(own_key, shape, deviation, limit, shards, heavy, kind=jnp.bfloat16):
    drawn = deviation * jax.random.normal(own_key, shape, jnp.float32)
    if shards:
        drawn = drawn * level_of(own_key, shape, shards, -0.22, 0.18)
    return jnp.clip(strengthened(drawn, jax.random.fold_in(own_key, 3), *heavy), -limit, limit).astype(kind)


def setup_inputs(seed: int = 0) -> dict:
    seeds = jax.random.split(jax.random.key(seed), 18)
    tokens = bell_draw_with(seeds[0], (MICRO, TOKENS, D), 1.0, 6.0, ((1, 32),), (1, 2, 32, 2.75))
    cotangent = bell_draw_with(seeds[1], (MICRO, TOKENS, D), 1.0, 6.0, ((1, 32),), (1, 2, 32, 2.75))
    segments = jax.vmap(lambda own: jnp.searchsorted(jnp.cumsum(uneven_parts(own, 4, ROW_LEN, ROW_LEN // 2, 2)), jnp.arange(ROW_LEN), side="right"))(jax.random.split(seeds[2], MICRO * ROWS)).reshape((MICRO, ROWS, ROW_LEN)).astype(jnp.int32)
    value_picks = distinct(seeds[3], MICRO * TOKENS * H, EA, ATT_TOP, 0).reshape((MICRO, TOKENS, H, ATT_TOP))
    output_picks = distinct(seeds[4], MICRO * TOKENS * H, EA, ATT_TOP, 0).reshape((MICRO, TOKENS, H, ATT_TOP))
    expert_picks_keys = jax.random.split(jax.random.fold_in(seeds[5], 1), MICRO * TOKENS // ROW_LEN)
    expert_picks_turns = jax.random.permutation(jax.random.fold_in(seeds[5], 3), MICRO * TOKENS // ROW_LEN)
    expert_picks = jax.vmap(lambda own, number: deal_out(jax.random.fold_in(seeds[5], 2), own, number, ROW_LEN, EXPERTS, TOP, CAP, 1))(expert_picks_keys, expert_picks_turns).reshape((MICRO, TOKENS, TOP))
    attn_gain = jnp.clip(jnp.exp(math.log(2.0) - 1.3862944 * jax.random.uniform(seeds[6], (D,), jnp.float32) ** level_of(seeds[6], (D,), ((0, 4),), -0.2, 0.2)), 0.5, 2.0).astype(jnp.bfloat16)
    query_weight = centred(seeds[7], (D, H * DH), D ** -0.5, 0.1875, ((0, 4),))
    key_weight = centred(seeds[8], (D, H * DH), D ** -0.5, 0.1875, ((0, 4),))
    value_weight = centred(seeds[9], (D, H * EA * DH), D ** -0.5, 0.1875, ((0, 4),))
    output_expert_weight = centred(seeds[10], (D, H * EA * DH), 32 ** -0.5, 1.0, ((0, 4),))
    value_select = centred(seeds[11], (D, H * EA), (2 * D) ** -0.5, 0.125, ((0, 4),))
    output_select = centred(seeds[12], (D, H * EA), (2 * D) ** -0.5, 0.125, ((0, 4),))
    moe_gain = jnp.clip(jnp.exp(math.log(2.0) - 1.3862944 * jax.random.uniform(seeds[13], (D,), jnp.float32) ** level_of(seeds[13], (D,), ((0, 4),), -0.2, 0.2)), 0.5, 2.0).astype(jnp.bfloat16)
    router_weight = centred(seeds[14], (D, EXPERTS), (4 * D) ** -0.5, 0.09375, ((0, 4),))
    up_weight = centred(seeds[15], (EXPERTS, D, FF_E), D ** -0.5, 0.1875, ((0, 8), (1, 4)))
    down_weight = centred(seeds[16], (EXPERTS, FF_E, D), (4 * FF_E) ** -0.5, 0.25, ((0, 8), (2, 4)))
    return {"tokens": tokens, "cotangent": cotangent, "segments": segments, "value_picks": value_picks, "output_picks": output_picks, "expert_picks": expert_picks, "attn_gain": attn_gain, "query_weight": query_weight, "key_weight": key_weight, "value_weight": value_weight, "output_expert_weight": output_expert_weight, "value_select": value_select, "output_select": output_select, "moe_gain": moe_gain, "router_weight": router_weight, "up_weight": up_weight, "down_weight": down_weight}


@jax.custom_vjp
def low(v):
    return lax.optimization_barrier(v.astype(jnp.bfloat16)).astype(jnp.float32)

@jax.custom_vjp
def low_back(v):
    return v

def low_keep(v):
    return (low(v), None)

def low_pass(kept, grad):
    return (grad,)

def back_keep(v):
    return (v, None)

def back_low(kept, grad):
    return (low(grad),)
low.defvjp(low_keep, low_pass)
low_back.defvjp(back_keep, back_low)
EPSILON = 1e-05
MASKED = -1e+30

def norm_rows(layer_inputs, norm_gain):
    centered = layer_inputs - lax.optimization_barrier(jnp.mean(layer_inputs, axis=-1, keepdims=True))
    variance = lax.optimization_barrier(jnp.mean(centered * centered, axis=-1, keepdims=True))
    return centered * lax.rsqrt(variance + EPSILON) * norm_gain

def project(layer_inputs, weight_matrix):
    return jnp.einsum('uhw,wr->uhr', layer_inputs, weight_matrix, precision=lax.Precision.HIGHEST)

def pick_mask(chosen, number):
    matches = chosen[..., None] == jnp.arange(number, dtype=jnp.int32)
    return lax.optimization_barrier(jnp.sum(matches.astype(jnp.float32), axis=-2))

def slot_numbers(expert_picks):
    matches = (expert_picks[..., None] == jnp.arange(EXPERTS, dtype=jnp.int32)).astype(jnp.int32)
    per_token = lax.optimization_barrier(jnp.sum(matches, axis=-2, dtype=jnp.int32))
    earlier = (jnp.cumsum(per_token, axis=-2, dtype=jnp.int32) - per_token).astype(jnp.int32)
    return jnp.take_along_axis(earlier, expert_picks.astype(jnp.int32), axis=-1).astype(jnp.int32)

def block_forward(layer_inputs, attn_gain, query_weight, key_weight, value_weight, output_expert_weight, value_select, output_select, moe_gain, router_weight, up_weight, down_weight, segments, value_picks, output_picks, expert_picks, slots):
    group_rows, length, width = layer_inputs.shape
    highest_precision = lax.Precision.HIGHEST
    normed = low(norm_rows(layer_inputs, attn_gain))
    queries = low(low_back(project(normed, query_weight))).reshape(group_rows, length, H, DH)
    keys_all = low(low_back(project(normed, key_weight))).reshape(group_rows, length, H, DH)
    value_prob = jax.nn.sigmoid(low_back(project(normed, value_select)))
    output_prob = jax.nn.sigmoid(low_back(project(normed, output_select)))
    value_gate = (value_prob * pick_mask(value_picks, EA).reshape(group_rows, length, H * EA)).reshape(group_rows, length, H, EA, 1)
    output_gate = (output_prob * pick_mask(output_picks, EA).reshape(group_rows, length, H * EA)).reshape(group_rows, length, H, EA, 1)
    value_all = low_back(project(layer_inputs, value_weight)).reshape(group_rows, length, H, EA, DH)
    values = low(lax.optimization_barrier(jnp.sum(value_gate * value_all, axis=3)))
    raw_scores = low_back(jnp.einsum('gqhd,gkhd->ghqk', queries, keys_all, precision=highest_precision))
    positions = jnp.arange(length, dtype=jnp.int32)
    causal = positions[None, :] <= positions[:, None]
    allowed = (causal[None] & (segments[:, :, None] == segments[:, None, :]))[:, None]
    scaled = jnp.where(allowed, raw_scores * DH ** (-0.5), MASKED)
    row_max = lax.optimization_barrier(jnp.max(scaled, axis=-1, keepdims=True))
    expo = jnp.where(allowed, jnp.exp(scaled - row_max), 0.0)
    probs = expo / lax.optimization_barrier(jnp.sum(expo, axis=-1, keepdims=True))
    attended = low_back(jnp.einsum('ghqk,gkhd->gqhd', low(probs), values, precision=highest_precision))
    mixed_heads = low((output_gate * attended[:, :, :, None, :]).reshape(group_rows, length, H * EA * DH))
    residual_branch = low_back(jnp.einsum('wvn,zn->wvz', mixed_heads, output_expert_weight, precision=highest_precision))
    resid = layer_inputs + residual_branch
    resid_low = low(resid)
    normed_two = low(norm_rows(resid, moe_gain))
    router_gate = jax.nn.sigmoid(low_back(project(normed_two, router_weight)))
    pair_gate = jnp.take_along_axis(router_gate, expert_picks, axis=-1)
    row_ids = jnp.broadcast_to(jnp.arange(group_rows, dtype=jnp.int32)[:, None, None], expert_picks.shape)
    rows_in = jnp.broadcast_to(resid_low[:, :, None, :], (group_rows, length, TOP, width))
    buffer = jnp.zeros((EXPERTS, group_rows, CAP, width), resid_low.dtype).at[expert_picks, row_ids, slots].set(rows_in)
    buffer = low_back(buffer)
    pre_act = low_back(jnp.einsum('ercd,edf->ercf', buffer, up_weight, precision=highest_precision))
    hidden = low(jax.nn.silu(pre_act))
    expert_out = low(low_back(jnp.einsum('ercf,efd->ercd', hidden, down_weight, precision=highest_precision)))
    pair_out = expert_out[expert_picks, row_ids, slots]
    return resid + lax.optimization_barrier(jnp.sum(pair_gate[..., None] * pair_out, axis=2))

def reference(tokens, cotangent, segments, value_picks, output_picks, expert_picks, attn_gain, query_weight, key_weight, value_weight, output_expert_weight, value_select, output_select, moe_gain, router_weight, up_weight, down_weight):
    length = ROW_LEN
    group_rows = math.gcd(ROWS, max(1, 2048 // ROW_LEN))
    block_count = MICRO * ROWS // group_rows
    token_blocks = tokens.astype(jnp.float32).reshape(block_count, group_rows, length, D)
    cot_blocks = cotangent.astype(jnp.float32).reshape(block_count, group_rows, length, D)
    segment_blocks = segments.astype(jnp.int32).reshape(block_count, group_rows, length)
    value_blocks = value_picks.astype(jnp.int32).reshape(block_count, group_rows, length, H, ATT_TOP)
    output_blocks = output_picks.astype(jnp.int32).reshape(block_count, group_rows, length, H, ATT_TOP)
    expert_blocks = expert_picks.astype(jnp.int32).reshape(block_count, group_rows, length, TOP)
    weights = tuple((weight.astype(jnp.float32) for weight in (attn_gain, query_weight, key_weight, value_weight, output_expert_weight, value_select, output_select, moe_gain, router_weight, up_weight, down_weight)))

    def step_block(totals, pieces):
        layer_inputs, cot_piece, segment_piece, value_piece, output_piece, expert_piece = pieces
        slots = slot_numbers(expert_piece)

        def forward(block_inputs, *weight_args):
            return block_forward(block_inputs, *weight_args, segment_piece, value_piece, output_piece, expert_piece, slots)
        result, pullback = jax.vjp(forward, layer_inputs, *weights)
        gradients = pullback(cot_piece)
        new_totals = tuple((total + part for total, part in zip(totals, gradients[1:])))
        return (new_totals, (result, gradients[0]))
    zero_totals = tuple((jnp.zeros_like(weight) for weight in weights))
    totals, (results, grad_inputs) = lax.scan(step_block, zero_totals, (token_blocks, cot_blocks, segment_blocks, value_blocks, output_blocks, expert_blocks))
    return (results.reshape(MICRO, TOKENS, D), grad_inputs.reshape(MICRO, TOKENS, D), totals[0], totals[1], totals[2], totals[3], totals[4], totals[5], totals[6], totals[7], totals[8], totals[9], totals[10])
```

```python
import functools

import jax
import jax.numpy as jnp
from jax import lax
from jax.experimental import pallas as pl
from jax.experimental.pallas import tpu as pltpu
from jax.sharding import PartitionSpec as P

H = 4
DH = 128
EA = 5
HE = H * EA
EXPERTS = 128
EPSILON = 1e-05
MASKED = -1e30
SCALE = DH ** (-0.5)
LANES = 128

BF = jnp.bfloat16
F32 = jnp.float32

COL_SEL = 2 * H * DH
COL_ROUTER = COL_SEL + LANES
COL_A = COL_ROUTER + LANES
LANE_GAIN_ONE = 2 * HE
LANE_GAIN_TWO = 2 * HE + 1
COL_VG = 2 * H * DH
COL_LG = COL_VG + H * DH
COL_RG = COL_LG + LANES
COL_LATE = COL_RG + LANES
G_V = 2 * H * DH
G_O = G_V + HE * DH
G_S = G_O + HE * DH
G_R = G_S + LANES
G_ALL = G_R + LANES

VMEM = pl.BlockSpec(memory_space=pltpu.VMEM)
SMEM = pl.BlockSpec(memory_space=pltpu.SMEM)
ANY = pl.BlockSpec(memory_space=pl.ANY)


def dot(a, b):
    return jnp.dot(a, b, preferred_element_type=F32)


def dot_nt(a, b):
    return lax.dot_general(a, b, (((1,), (1,)), ((), ())), preferred_element_type=F32)


def dot_tn(a, b):
    return lax.dot_general(a, b, (((0,), (0,)), ((), ())), preferred_element_type=F32)


def sigmoid(v):
    return 1.0 / (1.0 + jnp.exp(-v))


class Grid:
    def __init__(self, nd, ne):
        self.nd, self.ne = nd, ne
        self.C = 2 if nd % 2 == 0 else 1
        self.Y = nd // self.C
        x = 1
        while (2 * x) * (2 * x) <= ne and ne % (2 * x) == 0:
            x *= 2
        self.X, self.Z = x, ne // x

    def _dp(self, v, go):
        C = self.C
        pairs = []
        for i in range(self.nd):
            y, c = go(i // C, i % C)
            pairs.append((i, y * C + c))
        return lax.ppermute(v, "dp", pairs)

    def _ex(self, v, go):
        X = self.X
        pairs = []
        for i in range(self.ne):
            z, x = go(i // X, i % X)
            pairs.append((i, z * X + x))
        return lax.ppermute(v, "expert", pairs)

    def rot_y(self, v, k):
        return self._dp(v, lambda y, c: ((y + k) % self.Y, c))

    def swap(self, v):
        return self._dp(v, lambda y, c: (y, c ^ 1))

    def rot_yc(self, v, k, r):
        return self._dp(v, lambda y, c: ((y + k) % self.Y, c ^ r))

    def rot_x(self, v, j):
        return self._ex(v, lambda z, x: (z, (x + j) % self.X))

    def rot_z(self, v, k):
        return self._ex(v, lambda z, x: ((z + k) % self.Z, x))


def gather_split(grid, w, rows_axis, at_x):
    n = w.shape[rows_axis] // grid.X
    part = lax.dynamic_slice_in_dim(w, at_x * n, n, axis=rows_axis) if grid.X > 1 else w
    pieces = [(w, (0, 0, None))]
    if grid.C > 1:
        pieces.append((grid.swap(w), (0, 1, None)))
    for k in range(1, grid.Y):
        got = [(grid.rot_y(part, k), 0)]
        for j in range(1, grid.X):
            got.append((grid.rot_x(got[0][0], j), j))
        for v, j in got:
            pieces.append((v, (k, 0, j)))
            if grid.C > 1:
                pieces.append((grid.swap(v), (k, 1, j)))
    return [p[0] for p in pieces], [p[1] for p in pieces]


def gather_dp(grid, w):
    pieces, tags = [w], [(0, 0)]
    got = [(w, 0)]
    for k in range(1, grid.Y):
        v = grid.rot_y(w, k)
        got.append((v, k))
        pieces.append(v)
        tags.append((k, 0))
    if grid.C > 1:
        for v, k in got:
            pieces.append(grid.swap(v))
            tags.append((k, 1))
    return pieces, tags


def shard_at(grid, idx, k, r):
    return lax.rem(idx[0] + (grid.Y - k), grid.Y) * grid.C + lax.rem(idx[1] + r, grid.C)


def fetch_rows(grid, idx, refs, tags, dst, sems, columns=None):
    copies = []
    width = dst.shape[0] // grid.nd
    part = width // grid.X
    for i, (ref, (k, r, j)) in enumerate(zip(refs, tags)):
        at = shard_at(grid, idx, k, r) * width
        n = width
        if j is not None:
            at = at + lax.rem(idx[3] + (grid.X - j), grid.X) * part
            n = part
        at = pl.multiple_of(at, n)
        src = ref if columns is None else ref.at[:, pl.ds(columns[0], columns[1])]
        copy = pltpu.make_async_copy(src, dst.at[pl.ds(at, n), :], sems.at[i])
        copy.start()
        copies.append(copy)
    return copies


def wait_all(copies):
    for copy in copies:
        copy.wait()


def lanes_of(shape):
    return lax.broadcasted_iota(jnp.int32, shape, 1)


def norm_stats(v):
    centered = v - jnp.mean(v, axis=-1, keepdims=True)
    inverse = lax.rsqrt(jnp.mean(centered * centered, axis=-1, keepdims=True) + EPSILON)
    return centered * inverse, inverse


def gain_row(block, lane):
    return jnp.transpose(block.astype(F32))[lane : lane + 1, :]


def col(v, i):
    return v[:, i : i + 1]


def head(v, i):
    return v[:, i * DH : (i + 1) * DH]


def attend_kernel(grid, tags, n_a, idx, x_ref, segc, segr, vp, op, *rest):
    n = len(tags)
    a_refs, v_refs = rest[:n], rest[n : 2 * n]
    (n1_ref, qk_ref, val_ref, va_ref, sig_ref, mask_ref, pr_ref, att_ref, wa, wv, sem_a, sem_v) = rest[
        2 * n :
    ]
    get_a = fetch_rows(grid, idx, a_refs, tags, wa, sem_a)
    get_v = fetch_rows(grid, idx, v_refs, tags, wv, sem_v)
    x_bf = x_ref[...]
    unit, _ = norm_stats(x_bf.astype(F32))
    tokens = x_bf.shape[0]
    lane = lanes_of((tokens, LANES))
    mask = jnp.zeros((tokens, LANES), F32)
    for h in range(H):
        for k in range(2):
            mask = mask + (lane == col(vp, 2 * h + k) + EA * h).astype(F32)
            mask = mask + (lane == col(op, 2 * h + k) + (EA * h + HE)).astype(F32)
    mask_ref[...] = mask
    wait_all(get_a)
    gain = gain_row(wa[:, COL_SEL:COL_ROUTER], LANE_GAIN_ONE)
    n1 = (unit * gain).astype(BF)
    n1_ref[...] = n1
    qks = dot(n1, wa[:, :COL_ROUTER])
    qk = qks[:, :COL_SEL].astype(BF)
    qk_ref[...] = qk
    sig = sigmoid(qks[:, COL_SEL:])
    sig_ref[...] = sig
    gate = sig * mask
    allowed = (segc[...] == segr[...]) & (
        lanes_of((tokens, tokens)) <= lax.broadcasted_iota(jnp.int32, (tokens, tokens), 0)
    )
    probs = []
    for h in range(H):
        scores = dot_nt(head(qk, h), head(qk, H + h))
        scaled = jnp.where(allowed, scores * SCALE, MASKED)
        top = jnp.max(scaled, axis=-1, keepdims=True)
        expo = jnp.where(allowed, jnp.exp(scaled - top), 0.0)
        prob = expo / jnp.sum(expo, axis=-1, keepdims=True)
        pr_ref[:, h * tokens : (h + 1) * tokens] = prob
        probs.append(prob.astype(BF))
    wait_all(get_v)
    for h in range(H):
        va = dot(x_bf, wv[:, h * EA * DH : (h + 1) * EA * DH])
        va_ref[:, h * EA * DH : (h + 1) * EA * DH] = va
        total = col(gate, h * EA) * head(va, 0)
        for e in range(1, EA):
            total = total + col(gate, h * EA + e) * head(va, e)
        value = total.astype(BF)
        val_ref[:, h * DH : (h + 1) * DH] = value
        att_ref[:, h * DH : (h + 1) * DH] = dot(probs[h], value)


def mixed_of(gate, att, first):
    return jnp.concatenate(
        [
            (col(gate, first + h * EA + e) * head(att, h)).astype(BF)
            for h in range(H)
            for e in range(EA)
        ],
        axis=1,
    )


def route_kernel(grid, tags, idx, x_ref, att_ref, sig_ref, mask_ref, ep, *rest):
    n = len(tags)
    a_refs, o_refs = rest[:n], rest[n : 2 * n]
    (res_ref, xg_ref, n2_ref, router_ref, picked_ref, gate_ref, wa, wo, sem_a, sem_o) = rest[2 * n :]
    get_o = fetch_rows(grid, idx, o_refs, tags, wo, sem_o)
    get_a = fetch_rows(grid, idx, a_refs, tags, wa, sem_a, (COL_SEL, 2 * LANES))
    gate = sig_ref[...] * mask_ref[...]
    gate_ref[...] = gate
    mixed = mixed_of(gate, att_ref[...], HE)
    tokens = gate.shape[0]
    lane = lanes_of((tokens, EXPERTS))
    picked = jnp.zeros((tokens, EXPERTS), F32)
    for k in range(ep.shape[1]):
        picked = picked + (lane == col(ep, k)).astype(F32)
    picked_ref[...] = picked
    wait_all(get_o)
    res = x_ref[...].astype(F32) + dot_nt(mixed, wo[...])
    res_ref[...] = res
    width = res.shape[1]
    wait_all(get_a)
    unit, _ = norm_stats(res)
    n2 = (unit * gain_row(wa[:, :LANES], LANE_GAIN_TWO)).astype(BF)
    n2_ref[...] = n2
    router = sigmoid(dot(n2, wa[:, LANES:]))
    router_ref[...] = router
    xg_ref[:, :width] = res.astype(BF)
    xg_ref[:, width:] = (router * picked).astype(BF)


def expert_kernel(grid, tags, idx, xg_ref, g_ref, *rest):
    n, X = len(tags), grid.X
    u_refs, d_refs = rest[:n], rest[n : 2 * n]
    rest = rest[2 * n :]
    hg_ref, pg_ref = rest[:2]
    from_refs, out_refs = rest[2 : 2 + X], rest[2 + X : 2 + 2 * X]
    up, down, gg, sem_u, sem_d = rest[2 + 2 * X :]
    local, width = up.shape[0], up.shape[1]
    tokens = g_ref.shape[0]
    piece = width // grid.nd
    copies = []
    for i, (k, r) in enumerate(tags):
        at = pl.multiple_of(shard_at(grid, idx, k, r) * piece, piece)
        copies.append(pltpu.make_async_copy(d_refs[i], down.at[:, :, pl.ds(at, piece)], sem_d.at[i]))
        copies.append(pltpu.make_async_copy(u_refs[i], up.at[:, pl.ds(at, piece), :], sem_u.at[i]))
    for copy in copies:
        copy.start()
    first = (idx[2] * X + idx[3]) * local
    gg[...] = jnp.zeros_like(gg)
    lane = lanes_of((tokens, EXPERTS))
    wait_all(copies)

    def pair(p, carry):
        w2 = jnp.concatenate([up[2 * p], up[2 * p + 1]], axis=1)
        d2 = down[pl.ds(2 * p, 2)].reshape(2 * LANES, width)
        pre = dot(xg_ref[:, :width], w2)
        gh = dot_nt(g_ref[...], d2)
        at = first + 2 * p
        gates = pltpu.roll(xg_ref[:, width:].astype(F32), EXPERTS - at, 1)
        gate = jnp.concatenate(
            [jnp.broadcast_to(col(gates, i), (tokens, LANES)) for i in range(2)], axis=1
        )
        sig = sigmoid(pre)
        hidden = (pre * sig).astype(BF).astype(F32)
        part = hidden * gh
        total = gg[...]
        for i in range(2):
            each = jnp.sum(head(part, i), axis=1, keepdims=True)
            total = total + jnp.where(lane == at + i, each, 0.0)
        gg[...] = total
        columns = pl.ds(pl.multiple_of(p * 2 * LANES, 2 * LANES), 2 * LANES)
        hg_ref[:, columns] = (gate * hidden).astype(BF)
        pg_ref[:, columns] = (gate * gh * sig * (1.0 + pre * (1.0 - sig))).astype(BF)
        return carry

    lax.fori_loop(0, local // 2, pair, 0)
    rows = tokens // X

    def send(q, carry):
        columns = pl.ds(pl.multiple_of(q * piece, piece), piece)
        w = jnp.concatenate([up[e, columns, :] for e in range(local)], axis=1)
        back = dot_nt(pg_ref[...], w).astype(BF)
        out = dot(hg_ref[...], down[:, :, columns].reshape(local * LANES, piece)).astype(BF)
        for j in range(X):
            from_refs[j][:, columns] = back[j * rows : (j + 1) * rows]
            out_refs[j][:, columns] = out[j * rows : (j + 1) * rows]
        return carry

    lax.fori_loop(0, grid.nd, send, 0)
    for j in range(X):
        from_refs[j][:, width:] = gg[j * rows : (j + 1) * rows, :].astype(BF)


def expert_grad_kernel(local, idx, x0, x1, g0, g1, pg0, pg1, hg0, hg1, gu_ref, gd_ref):
    del idx
    up = dot_tn(x0[...], pg0[...]) + dot_tn(x1[...], pg1[...])
    down = dot_tn(g0[...], hg0[...]) + dot_tn(g1[...], hg1[...])
    for e in range(local):
        gu_ref[0, e] = head(up, e).astype(BF)
        gd_ref[0, e] = jnp.transpose(head(down, e)).astype(BF)


def backward_kernel(grid, tags, n_from, idx, x_ref, g_ref, res_ref, router_ref, picked_ref, gate_ref, sig_ref,
                    mask_ref, att_ref, qk_ref, val_ref, va_ref, pr_ref, *rest):
    n = len(tags)
    f_refs = rest[:n_from]
    rest = rest[n_from:]
    a_refs, o_refs, v_refs = rest[:n], rest[n : 2 * n], rest[2 * n : 3 * n]
    late_ref, bg_ref, gt_ref, wa, wo, wv, sem_a, sem_o, sem_v = rest[3 * n :]
    get_a = fetch_rows(grid, idx, a_refs, tags, wa, sem_a)
    get_o = fetch_rows(grid, idx, o_refs, tags, wo, sem_o)
    get_v = fetch_rows(grid, idx, v_refs, tags, wv, sem_v)
    width = x_ref.shape[1]
    tokens = x_ref.shape[0]
    back = f_refs[0][...].astype(F32)
    for ref in f_refs[1:]:
        back = back + ref[...].astype(F32)
    router = router_ref[...]
    rg = (back[:, width:] * picked_ref[...] * router * (1.0 - router)).astype(BF)
    unit, inverse = norm_stats(res_ref[...])
    wait_all(get_a)
    n2g = dot_nt(rg, wa[:, COL_ROUTER:])
    selections = wa[:, COL_SEL:COL_ROUTER]
    gains = jnp.transpose(selections.astype(F32))
    gain_two = jnp.sum(n2g * unit, axis=0, keepdims=True)
    a = n2g * gains[LANE_GAIN_TWO : LANE_GAIN_TWO + 1]
    from_norm = inverse * (
        a
        - jnp.mean(a, axis=-1, keepdims=True)
        - unit * jnp.mean(a * unit, axis=-1, keepdims=True)
    )
    res_grad = g_ref[...].astype(F32) + back[:, :width] + from_norm
    bg = res_grad.astype(BF)
    gate, sig, att = gate_ref[...], sig_ref[...], att_ref[...]
    lane = lanes_of((tokens, LANES))
    logits = jnp.zeros((tokens, LANES), F32)
    wait_all(get_o)
    qgs, kgs, vgs, vags = [], [], [], []
    for h in range(H):
        mg = dot(bg, wo[:, h * EA * DH : (h + 1) * EA * DH])
        ag = jnp.zeros((tokens, DH), F32)
        for e in range(EA):
            i = HE + h * EA + e
            ag = ag + col(gate, i) * head(mg, e)
            each = jnp.sum(head(mg, e) * head(att, h), axis=1, keepdims=True)
            logits = jnp.where(lane == i, each, logits)
        ag = ag.astype(BF)
        prob = pr_ref[:, h * tokens : (h + 1) * tokens]
        vg = dot_tn(prob.astype(BF), ag)
        pgrad = dot_nt(ag, val_ref[:, h * DH : (h + 1) * DH])
        delta = jnp.sum(prob * pgrad, axis=-1, keepdims=True)
        sg = (prob * (pgrad - delta) * SCALE).astype(BF)
        qgs.append(dot(sg, qk_ref[:, (H + h) * DH : (H + h + 1) * DH]).astype(BF))
        kgs.append(dot_tn(sg, qk_ref[:, h * DH : (h + 1) * DH]).astype(BF))
        vgs.append(vg.astype(BF))
        for e in range(EA):
            i = h * EA + e
            va = va_ref[:, i * DH : (i + 1) * DH]
            each = jnp.sum(va * vg, axis=1, keepdims=True)
            logits = jnp.where(lane == i, each, logits)
            vags.append((col(gate, i) * vg).astype(BF))
    lg = (logits * mask_ref[...] * sig * (1.0 - sig)).astype(BF)
    qkg = jnp.concatenate(qgs + kgs, axis=1)
    late_ref[:, :COL_VG] = qkg
    late_ref[:, COL_VG:COL_LG] = jnp.concatenate(vgs, axis=1)
    late_ref[:, COL_LG:COL_RG] = lg
    late_ref[:, COL_RG:] = rg
    n1g = dot_nt(qkg, wa[:, :COL_SEL]) + dot_nt(lg, selections)
    unit, inverse = norm_stats(x_ref[...].astype(F32))
    gain_one = jnp.sum(n1g * unit, axis=0, keepdims=True)
    b = n1g * gains[LANE_GAIN_ONE : LANE_GAIN_ONE + 1]
    from_norm = inverse * (
        b
        - jnp.mean(b, axis=-1, keepdims=True)
        - unit * jnp.mean(b * unit, axis=-1, keepdims=True)
    )
    bg_ref[:tokens] = bg
    row = lax.broadcasted_iota(jnp.int32, (16, width), 0)
    high_one, high_two = gain_one.astype(BF).astype(F32), gain_two.astype(BF).astype(F32)
    extra = jnp.where(row == 0, high_one, 0.0)
    extra = jnp.where(row == 1, gain_one - high_one, extra)
    extra = jnp.where(row == 2, high_two, extra)
    extra = jnp.where(row == 3, gain_two - high_two, extra)
    bg_ref[tokens:] = extra.astype(BF)
    wait_all(get_v)
    gt_ref[...] = res_grad + dot_nt(jnp.concatenate(vags, axis=1), wv[...]) + from_norm


def weight_grad_kernel(nd, *refs):
    early, columns, late, bgs = refs[:nd], refs[nd : 2 * nd], refs[2 * nd : 3 * nd], refs[3 * nd : 4 * nd]
    out = refs[4 * nd]
    tokens = early[0].shape[0]
    width = bgs[0].shape[1]
    stack = functools.partial(jnp.concatenate, axis=0)
    xc = stack([r[:, :width] for r in columns])
    n1 = stack([r[:, width : 2 * width] for r in columns])
    n2 = stack([r[:, 2 * width :] for r in columns])
    bg = stack([r[:tokens] for r in bgs])
    acts = stack([r[...] for r in late])
    att = stack([r[:, : H * DH] for r in early])
    gate = stack([r[:, H * DH :] for r in early])
    out[:, :G_V] = dot_tn(n1, acts[:, :COL_VG]).astype(BF)
    values = acts[:, COL_VG:COL_LG].astype(F32)
    out[:, G_V:G_O] = dot_tn(xc, mixed_of(gate, values, 0)).astype(BF)
    out[:, G_O:G_S] = dot_tn(bg, mixed_of(gate, att, HE)).astype(BF)
    sums = bgs[0][tokens:].astype(F32)
    for r in bgs[1:]:
        sums = sums + r[tokens:].astype(F32)
    row = lax.broadcasted_iota(jnp.int32, (LANES, width), 0)
    extra = jnp.where(row == LANE_GAIN_ONE, sums[0:1] + sums[1:2], 0.0)
    extra = jnp.where(row == LANE_GAIN_TWO, sums[2:3] + sums[3:4], extra)
    out[:, G_S:G_R] = (dot_tn(n1, acts[:, COL_LG:COL_RG]) + jnp.transpose(extra)).astype(BF)
    out[:, G_R:] = dot_tn(n2, acts[:, COL_RG:]).astype(BF)


def params(mib):
    return pltpu.CompilerParams(vmem_limit_bytes=mib * 1024 * 1024)


def shape(dims, dtype):
    return jax.ShapeDtypeStruct(dims, dtype)


def per_device(
    nd,
    ne,
    tokens,
    cotangent,
    segments,
    value_picks,
    output_picks,
    expert_picks,
    attn_gain,
    query_weight,
    key_weight,
    value_weight,
    output_expert_weight,
    value_select,
    output_select,
    moe_gain,
    router_weight,
    up_weight,
    down_weight,
):
    grid = Grid(nd, ne)
    X, Y, Z, C = grid.X, grid.Y, grid.Z, grid.C
    micros, length, width = tokens.shape
    rows = micros * length
    local = up_weight.shape[0]
    piece = width // nd
    dp, ex = lax.axis_index("dp"), lax.axis_index("expert")
    at_y, at_c, at_z, at_x = dp // C, dp % C, ex // X, ex % X
    idx = jnp.stack([at_y, at_c, at_z, at_x]).astype(jnp.int32)

    block_a = jnp.concatenate(
        [
            query_weight,
            key_weight,
            value_select,
            output_select,
            attn_gain[:, None],
            moe_gain[:, None],
            jnp.zeros((piece, LANES - 2 * HE - 2), BF),
            router_weight,
        ],
        axis=1,
    )
    a_pieces, tags = gather_split(grid, block_a, 0, at_x)
    v_pieces, _ = gather_split(grid, value_weight, 0, at_x)
    o_pieces, _ = gather_split(grid, output_expert_weight, 0, at_x)
    u_pieces, dp_tags = gather_dp(grid, up_weight)
    d_pieces, _ = gather_dp(grid, down_weight)
    n_tags = len(tags)

    x_all = tokens.reshape(rows, width)
    g_all = cotangent.reshape(rows, width)
    seg = (segments[:, 0, :] + 8 * jnp.arange(micros, dtype=jnp.int32)[:, None]).reshape(rows)
    sem = pltpu.SemaphoreType.DMA((n_tags,))
    wide = H * DH
    n1, qk, vals, va, sig, mask, probs, att = pl.pallas_call(
        functools.partial(attend_kernel, grid, tags, n_tags),
        out_shape=(
            shape((rows, width), BF),
            shape((rows, 2 * wide), BF),
            shape((rows, wide), BF),
            shape((rows, HE * DH), F32),
            shape((rows, LANES), F32),
            shape((rows, LANES), F32),
            shape((rows, H * rows), F32),
            shape((rows, wide), F32),
        ),
        in_specs=[SMEM] + [VMEM] * 5 + [ANY] * (2 * n_tags),
        out_specs=(VMEM,) * 8,
        scratch_shapes=[
            pltpu.VMEM((width, COL_A), BF),
            pltpu.VMEM((width, HE * DH), BF),
            sem,
            sem,
        ],
        compiler_params=params(40),
        name="attend",
    )(
        idx,
        x_all,
        seg[:, None],
        seg[None, :],
        value_picks.reshape(rows, 2 * H),
        output_picks.reshape(rows, 2 * H),
        *a_pieces,
        *v_pieces,
    )
    res, xg, n2, router, picked, gate = pl.pallas_call(
        functools.partial(route_kernel, grid, tags),
        out_shape=(
            shape((rows, width), F32),
            shape((rows, width + EXPERTS), BF),
            shape((rows, width), BF),
            shape((rows, EXPERTS), F32),
            shape((rows, EXPERTS), F32),
            shape((rows, LANES), F32),
        ),
        in_specs=[SMEM] + [VMEM] * 5 + [ANY] * (2 * n_tags),
        out_specs=(VMEM,) * 6,
        scratch_shapes=[
            pltpu.VMEM((width, 2 * LANES), BF),
            pltpu.VMEM((width, HE * DH), BF),
            sem,
            sem,
        ],
        compiler_params=params(40),
        name="route",
    )(idx, x_all, att, sig, mask, expert_picks.reshape(rows, -1), *a_pieces, *o_pieces)

    def gather_rows(v):
        column = jnp.concatenate([v] + [grid.rot_z(v, k) for k in range(1, Z)], axis=0)
        return jnp.concatenate([column] + [grid.rot_x(column, j) for j in range(1, X)], axis=0)

    def return_rows(parts):
        total = parts[0].astype(F32)
        for j in range(1, X):
            total = total + grid.rot_x(parts[j], -j).astype(F32)
        total = total.astype(BF)
        return [total[:length]] + [
            grid.rot_z(total[k * length : (k + 1) * length], -k) for k in range(1, Z)
        ]

    group = ne * length
    g_group = [gather_rows(g_all[m * length : (m + 1) * length]) for m in range(micros)]
    xg_group = [gather_rows(xg[m * length : (m + 1) * length]) for m in range(micros)]
    hgs, pgs, froms, outs = [], [], [], []
    ff = local * LANES
    for m in range(micros):
        got = pl.pallas_call(
            functools.partial(expert_kernel, grid, dp_tags),
            out_shape=(
                shape((group, ff), BF),
                shape((group, ff), BF),
                *[shape((group // X, width + EXPERTS), BF)] * X,
                *[shape((group // X, width), BF)] * X,
            ),
            in_specs=[SMEM, VMEM, VMEM] + [ANY] * (2 * nd),
            out_specs=(VMEM,) * (2 + 2 * X),
            scratch_shapes=[
                pltpu.VMEM((local, width, LANES), BF),
                pltpu.VMEM((local, LANES, width), BF),
                pltpu.VMEM((group, EXPERTS), F32),
                pltpu.SemaphoreType.DMA((nd,)),
                pltpu.SemaphoreType.DMA((nd,)),
            ],
            compiler_params=params(56),
            name="experts",
        )(idx, xg_group[m], g_group[m], *u_pieces, *d_pieces)
        hgs.append(got[0])
        pgs.append(got[1])
        froms.append(return_rows(got[2 : 2 + X]))
        outs.append(return_rows(got[2 + X :]))
    output = jnp.stack(
        [
            sum((p.astype(F32) for p in outs[m]), res[m * length : (m + 1) * length])
            for m in range(micros)
        ]
    )

    def expert_grads(r):
        def shard(s, idx):
            return lax.rem(idx[0] + s, Y) * C + lax.rem(idx[1] + r, C)

        full = pl.BlockSpec((group, ff), lambda s, idx: (0, 0))
        part = pl.BlockSpec((group, piece), lambda s, idx: (0, shard(s, idx)))
        return pl.pallas_call(
            functools.partial(expert_grad_kernel, local),
            out_shape=(shape((Y, local, piece, LANES), BF), shape((Y, local, LANES, piece), BF)),
            grid_spec=pltpu.PrefetchScalarGridSpec(
                num_scalar_prefetch=1,
                grid=(Y,),
                in_specs=[part] * 4 + [full] * 4,
                out_specs=(
                    pl.BlockSpec((1, local, piece, LANES), lambda s, idx: (s, 0, 0, 0)),
                    pl.BlockSpec((1, local, LANES, piece), lambda s, idx: (s, 0, 0, 0)),
                ),
            ),
            compiler_params=params(56),
            name="expert_grads",
        )(idx, *xg_group, *g_group, *pgs, *hgs)

    far = expert_grads(1) if C > 1 else None
    near = expert_grads(0)

    def reduce_dp(own, other):
        total = own.astype(F32)
        if C > 1:
            total = total + grid.swap(other).astype(F32)
        sent = total[1:].astype(BF)
        result = total[0]
        for k in range(1, Y):
            result = result + grid.rot_y(sent[k - 1], k).astype(F32)
        return result

    grad_up = reduce_dp(near[0], far[0] if C > 1 else None)
    grad_down = reduce_dp(near[1], far[1] if C > 1 else None)

    back = [jnp.concatenate([froms[m][k] for m in range(micros)], axis=0) for k in range(Z)]
    late, bg, grad_tokens = pl.pallas_call(
        functools.partial(backward_kernel, grid, tags, Z),
        out_shape=(
            shape((rows, COL_LATE), BF),
            shape((rows + 16, width), BF),
            shape((rows, width), F32),
        ),
        in_specs=[SMEM] + [VMEM] * (13 + Z) + [ANY] * (3 * n_tags),
        out_specs=(VMEM,) * 3,
        scratch_shapes=[
            pltpu.VMEM((width, COL_A), BF),
            pltpu.VMEM((width, HE * DH), BF),
            pltpu.VMEM((width, HE * DH), BF),
            sem,
            sem,
            sem,
        ],
        compiler_params=params(48),
        name="backward",
    )(
        idx, x_all, g_all, res, router, picked, gate, sig, mask, att, qk, vals, va, probs,
        *back, *a_pieces, *o_pieces, *v_pieces,
    )

    def columns_to(parts):
        def cut(k, r):
            at = (((at_y + k) % Y) * C + (at_c + r) % C) * piece
            return jnp.concatenate(
                [lax.dynamic_slice_in_dim(v, at, piece, axis=1) for v in parts], axis=1
            )

        return [
            cut(0, 0) if (k, r) == (0, 0) else grid.rot_yc(cut(k, r), k, r) for k, r in dp_tags
        ]

    early, _ = gather_dp(grid, jnp.concatenate([att, gate], axis=1))
    cols = columns_to([x_all, n1, n2])
    lates, _ = gather_dp(grid, late)
    bgs = columns_to([bg])
    grads = pl.pallas_call(
        functools.partial(weight_grad_kernel, nd),
        out_shape=shape((piece, G_ALL), BF),
        in_specs=[VMEM] * (4 * nd),
        out_specs=VMEM,
        compiler_params=params(48),
        name="weight_grads",
    )(*early, *cols, *lates, *bgs)
    mine = piece // ne
    blocks = grads.reshape(Z, X, mine, G_ALL)

    def at_block(v, axis, i, n):
        return lax.dynamic_index_in_dim(v, i % n, axis=axis, keepdims=False)

    total = at_block(blocks, 1, at_x, X).astype(F32)
    for j in range(1, X):
        total = total + grid.rot_x(at_block(blocks, 1, at_x + j, X), j).astype(F32)
    sent = total.astype(BF)
    final = at_block(total, 0, at_z, Z)
    for k in range(1, Z):
        final = final + grid.rot_z(at_block(sent, 0, at_z + k, Z), k).astype(F32)
    return (
        output,
        grad_tokens.reshape(micros, length, width),
        final[:, G_S + LANE_GAIN_ONE],
        final[:, :wide],
        final[:, wide : 2 * wide],
        final[:, G_V:G_O],
        final[:, G_O:G_S],
        final[:, G_S : G_S + HE],
        final[:, G_S + HE : G_S + 2 * HE],
        final[:, G_S + LANE_GAIN_TWO],
        final[:, G_R:],
        grad_up,
        grad_down,
    )


def solution(mesh):
    rows = ("dp", "expert")
    placed = (
        P(None, rows, None),
        P(None, rows, None),
        P(None, rows, None),
        P(None, rows, None, None),
        P(None, rows, None, None),
        P(None, rows, None),
        P("dp"),
        P("dp", None),
        P("dp", None),
        P("dp", None),
        P("dp", None),
        P("dp", None),
        P("dp", None),
        P("dp"),
        P("dp", None),
        P("expert", "dp", None),
        P("expert", None, "dp"),
    )
    return jax.shard_map(
        functools.partial(per_device, mesh.shape["dp"], mesh.shape["expert"]),
        mesh=mesh,
        in_specs=placed,
        out_specs=(
            P(None, rows, None),
            P(None, rows, None),
            P(rows),
            P(rows, None),
            P(rows, None),
            P(rows, None),
            P(rows, None),
            P(rows, None),
            P(rows, None),
            P(rows),
            P(rows, None),
            P("expert", "dp", None),
            P("expert", None, "dp"),
        ),
        check_vma=False,
    )
```

```python
import functools

import jax
import jax.numpy as jnp
from jax import lax
from jax.experimental import pallas as pl
from jax.experimental.pallas import tpu as pltpu
from jax.sharding import PartitionSpec as P

H = 4
DH = 128
EA = 5
HE = H * EA
EXPERTS = 128
EPSILON = 1e-05
MASKED = -1e30
SCALE = DH ** (-0.5)
LANES = 128

BF = jnp.bfloat16
F32 = jnp.float32

COL_SEL = 2 * H * DH
COL_ROUTER = COL_SEL + LANES
COL_VALUES = COL_ROUTER + LANES
COL_OUT = COL_VALUES + HE * DH
COL_A = COL_OUT + HE * DH
STARTS = (0, 17 * LANES, 34 * LANES)
LANE_GAIN_ONE = 2 * HE
LANE_GAIN_TWO = 2 * HE + 1
LANE_MEAN = 2 * HE
LANE_INVERSE = 2 * HE + 1
COL_LG = 2 * H * DH
COL_VG = COL_LG + LANES
COL_RG = COL_VG + H * DH
COL_LATE = COL_RG + LANES

VMEM = pl.BlockSpec()
SMEM = pl.BlockSpec(memory_space=pltpu.SMEM)
ANY = pl.BlockSpec(memory_space=pltpu.HBM)


def dot(a, b):
    return jnp.dot(a, b, preferred_element_type=F32)


def dot_nt(a, b):
    return lax.dot_general(a, b, (((1,), (1,)), ((), ())), preferred_element_type=F32)


def dot_tn(a, b):
    return lax.dot_general(a, b, (((0,), (0,)), ((), ())), preferred_element_type=F32)


def sigmoid(v):
    return 1.0 / (1.0 + jnp.exp(-v))


class Grid:
    def __init__(self, nd, ne):
        self.nd, self.ne = nd, ne
        self.C = 2 if nd % 2 == 0 else 1
        self.Y = nd // self.C
        x = 1
        while (2 * x) * (2 * x) <= ne and ne % (2 * x) == 0:
            x *= 2
        self.X, self.Z = x, ne // x

    def _dp(self, v, go):
        C = self.C
        pairs = []
        for i in range(self.nd):
            y, c = go(i // C, i % C)
            pairs.append((i, y * C + c))
        return lax.ppermute(v, "dp", pairs)

    def _ex(self, v, go):
        X = self.X
        pairs = []
        for i in range(self.ne):
            z, x = go(i // X, i % X)
            pairs.append((i, z * X + x))
        return lax.ppermute(v, "expert", pairs)

    def rot_y(self, v, k):
        return self._dp(v, lambda y, c: ((y + k) % self.Y, c))

    def swap(self, v):
        return self._dp(v, lambda y, c: (y, c ^ 1))

    def rot_yc(self, v, k, r):
        return self._dp(v, lambda y, c: ((y + k) % self.Y, c ^ r))

    def rot_x(self, v, j):
        return self._ex(v, lambda z, x: (z, (x + j) % self.X))

    def rot_z(self, v, k):
        return self._ex(v, lambda z, x: ((z + k) % self.Z, x))

    def lines_z(self):
        return [[z * self.X + x for z in range(self.Z)] for x in range(self.X)]

    def gather_z(self, v):
        return lax.all_gather(v, "expert", axis=0, tiled=True, axis_index_groups=self.lines_z())

    def swap_z(self, v):
        return lax.all_to_all(v, "expert", 0, 0, tiled=True, axis_index_groups=self.lines_z())

    def send_z(self, parts):
        return [parts[0]] + [self.rot_z(parts[k], k) for k in range(1, self.Z)]

    def swap_dp(self, v):
        return lax.all_to_all(v, "dp", 0, 0, tiled=True)


def after(v, *deps):
    flat = [d for dep in deps for d in (dep if isinstance(dep, (list, tuple)) else [dep])]
    if not flat:
        return v
    return lax.optimization_barrier((v, *flat))[0]


def gather_dp(grid, w, over_y, swapped=None):
    got = [w] + list(over_y)
    if grid.C > 1:
        got = got + [grid.swap(w) if swapped is None else swapped] + [grid.swap(v) for v in over_y]
    return got


def dp_tags(grid):
    return [(k, r) for r in range(grid.C) for k in range(grid.Y)]


def shard_at(grid, idx, k, r):
    return lax.rem(idx[0] + (grid.Y - k), grid.Y) * grid.C + lax.rem(idx[1] + r, grid.C)


def fetch_rows(grid, idx, refs, tags, dst, sems, first=0):
    copies = []
    width, last = dst.shape[0] // grid.nd, first + dst.shape[1]
    for i, (ref, (k, r, split, j, column)) in enumerate(zip(refs, tags)):
        low, high = max(first, column), min(last, column + ref.shape[1])
        if low >= high:
            continue
        at = shard_at(grid, idx, k, r) * width
        n = width
        if split is not None:
            size, mine = (grid.X, idx[3]) if split == "x" else (grid.Z, idx[2])
            n = width // size
            at = at + lax.rem(mine + (size - j), size) * n
        at = pl.multiple_of(at, n)
        copy = pltpu.make_async_copy(
            ref.at[:, pl.ds(low - column, high - low)],
            dst.at[pl.ds(at, n), pl.ds(low - first, high - low)],
            sems.at[i],
        )
        copy.start()
        copies.append(copy)
    return copies


def fetch_experts(grid, idx, refs, tags, dst, axis, sems):
    copies = []
    n = dst.shape[axis] // grid.nd
    for i, (ref, (k, r, first)) in enumerate(zip(refs, tags)):
        at = pl.ds(pl.multiple_of(shard_at(grid, idx, k, r) * n, n), n)
        held = pl.ds(first, ref.shape[0])
        place = dst.at[held, at, :] if axis == 1 else dst.at[held, :, at]
        copy = pltpu.make_async_copy(ref, place, sems.at[i])
        copy.start()
        copies.append(copy)
    return copies


def wait_all(copies):
    for copy in copies:
        copy.wait()


def lanes_of(dims):
    return lax.broadcasted_iota(jnp.int32, dims, 1)


def rows_of(dims):
    return lax.broadcasted_iota(jnp.int32, dims, 0)


def norm_stats(v):
    centered = v - jnp.mean(v, axis=-1, keepdims=True)
    inverse = lax.rsqrt(jnp.mean(centered * centered, axis=-1, keepdims=True) + EPSILON)
    return centered * inverse, inverse


def window(pieces, tags, low, high):
    held = [(p, t) for p, t in zip(pieces, tags) if t[4] < high and t[4] + p.shape[1] > low]
    return [p for p, _ in held], [t for _, t in held]


def norm_back(grad, unit, inverse):
    return inverse * (
        grad
        - jnp.mean(grad, axis=-1, keepdims=True)
        - unit * jnp.mean(grad * unit, axis=-1, keepdims=True)
    )


def gain_row(block, lane):
    return jnp.transpose(block.astype(F32))[lane : lane + 1, :]


def col(v, i):
    return v[:, i : i + 1]


def head(v, i):
    return v[:, i * DH : (i + 1) * DH]


def mixed_of(gate, vectors, first):
    return jnp.concatenate(
        [
            (col(gate, first + h * EA + e) * head(vectors, h)).astype(BF)
            for h in range(H)
            for e in range(EA)
        ],
        axis=1,
    )


def pack_kernel(grid, idx, q, k, vs, os, gain_one, gain_two, router, v_ref, o_ref, w_ref, a_ref, *rest):
    parts, misc = rest[:-1], rest[-1]
    piece = q.shape[0]
    nx = piece // grid.X
    at_x = pl.ds(pl.multiple_of(idx[3] * nx, nx), nx)
    misc[...] = jnp.zeros_like(misc)
    misc[:HE, :] = vs[...].astype(F32)
    misc[HE : 2 * HE, :] = os[...].astype(F32)
    misc[LANE_GAIN_ONE : LANE_GAIN_ONE + 1, :] = gain_one[...].astype(F32).reshape(1, piece)
    misc[LANE_GAIN_TWO : LANE_GAIN_TWO + 1, :] = gain_two[...].astype(F32).reshape(1, piece)
    wide = H * DH
    a_ref[:, :wide] = q[...]
    a_ref[:, wide:COL_SEL] = k[...]
    a_ref[:, COL_SEL:COL_ROUTER] = jnp.transpose(misc[...]).astype(BF)
    a_ref[:, COL_ROUTER:] = router[...]
    w_ref[:, :COL_VALUES] = a_ref[...]
    w_ref[:, COL_VALUES:COL_OUT] = v_ref[...]
    w_ref[:, COL_OUT:] = o_ref[...]
    for part, low in zip(parts, STARTS):
        part[...] = w_ref[at_x, low : low + part.shape[1]]


def attend_kernel(grid, tags, length, idx, x_ref, seg_ref, vp, op, *rest):
    n = len(tags)
    a_refs = rest[:n]
    n1_ref, qk_ref, sig_ref, mask_ref, pr_ref, wmr_ref, wa, sem_a = rest[n:]
    get_a = fetch_rows(grid, idx, a_refs, tags, wa, sem_a)
    unit, _ = norm_stats(x_ref[...].astype(F32))
    tokens = unit.shape[0]
    lane = lanes_of((tokens, LANES))
    mask = jnp.zeros((tokens, LANES), F32)
    for h in range(H):
        for k in range(2):
            mask = mask + (lane == col(vp, 2 * h + k) + EA * h).astype(F32)
            mask = mask + (lane == col(op, 2 * h + k) + (EA * h + HE)).astype(F32)
    mask_ref[...] = mask
    square = (tokens, tokens)
    row, lane = rows_of(square), lanes_of(square)
    seg = jnp.broadcast_to(seg_ref[...].astype(F32), square)
    allowed = (seg == jnp.transpose(seg)) & (lane <= row) & (lane // length == row // length)
    wait_all(get_a)
    n1 = (unit * gain_row(wa[:, COL_SEL:COL_ROUTER], LANE_GAIN_ONE)).astype(BF)
    n1_ref[...] = n1
    qks = dot(n1, wa[:, :COL_ROUTER])
    qk = qks[:, :COL_SEL].astype(BF)
    qk_ref[...] = qk
    sig_ref[...] = sigmoid(qks[:, COL_SEL:])
    wmr_ref[...] = wa[:, COL_SEL:]
    for h in range(H):
        scores = dot_nt(head(qk, h), head(qk, H + h))
        scaled = jnp.where(allowed, scores * SCALE, MASKED)
        top = jnp.max(scaled, axis=-1, keepdims=True)
        expo = jnp.where(allowed, jnp.exp(scaled - top), 0.0)
        pr_ref[:, h * tokens : (h + 1) * tokens] = expo / jnp.sum(expo, axis=-1, keepdims=True)


def route_kernel(grid, v_tags, o_tags, idx, x_ref, n1_ref, sig_ref, mask_ref, pr_ref, wmr_ref, ep, *rest):
    nv, no = len(v_tags), len(o_tags)
    v_refs, o_refs = rest[:nv], rest[nv : nv + no]
    rest = rest[nv + no :]
    val_ref, va_ref, early_ref, res_ref, router_ref, picked_ref = rest[:6]
    xg_ref, col_ref, wv, wo, sem_v, sem_o = rest[6:]
    get_v = fetch_rows(grid, idx, v_refs, v_tags, wv, sem_v, COL_VALUES)
    get_o = fetch_rows(grid, idx, o_refs, o_tags, wo, sem_o, COL_OUT)
    gate = sig_ref[...] * mask_ref[...]
    tokens, width = x_ref.shape
    lane = lanes_of((tokens, EXPERTS))
    picked = jnp.zeros((tokens, EXPERTS), F32)
    for k in range(ep.shape[1]):
        picked = picked + (lane == col(ep, k)).astype(F32)
    picked_ref[...] = picked
    x_bf = x_ref[...]
    wait_all(get_v)
    atts = []
    for h in range(H):
        va = dot(x_bf, wv[:, h * EA * DH : (h + 1) * EA * DH])
        va_ref[:, h * EA * DH : (h + 1) * EA * DH] = va
        total = col(gate, h * EA) * head(va, 0)
        for e in range(1, EA):
            total = total + col(gate, h * EA + e) * head(va, e)
        value = total.astype(BF)
        val_ref[:, h * DH : (h + 1) * DH] = value
        atts.append(dot(pr_ref[:, h * tokens : (h + 1) * tokens].astype(BF), value))
    att = jnp.concatenate(atts, axis=1)
    early_ref[:, : H * DH] = att
    mean = jnp.mean(x_bf.astype(F32), axis=-1, keepdims=True)
    centered = x_bf.astype(F32) - mean
    inverse = lax.rsqrt(jnp.mean(centered * centered, axis=-1, keepdims=True) + EPSILON)
    lane = lanes_of((tokens, LANES))
    early_ref[:, H * DH :] = jnp.where(
        lane == LANE_MEAN, mean, jnp.where(lane == LANE_INVERSE, inverse, gate)
    )
    mixed = mixed_of(gate, att, HE)
    wait_all(get_o)
    res = x_bf.astype(F32) + dot_nt(mixed, wo[...])
    res_ref[...] = res
    unit, _ = norm_stats(res)
    n2 = (unit * gain_row(wmr_ref[:, :LANES], LANE_GAIN_TWO)).astype(BF)
    router = sigmoid(dot(n2, wmr_ref[:, LANES:]))
    router_ref[...] = router
    xg_ref[:, :width] = res.astype(BF)
    xg_ref[:, width:] = (router * picked).astype(BF)
    col_ref[:, :width] = x_bf
    col_ref[:, width : 2 * width] = n1_ref[...]
    col_ref[:, 2 * width :] = n2


def ahead_kernel(grid, tags, idx, g_ref, *rest):
    d_refs, (gh_ref, g, down, gh, sem_g, sem_d, sem_o) = rest[: len(tags)], rest[len(tags) :]
    local, width = down.shape[0], down.shape[2]
    micros = g.shape[1]
    get_g = pltpu.make_async_copy(g_ref, g, sem_g.at[0])
    get_g.start()
    get_d = fetch_experts(grid, idx, d_refs, tags, down, 2, sem_d)
    get_g.wait()
    wait_all(get_d)
    group = g.shape[0] * g.shape[2]
    copies = []
    for p in range(local // 2):
        d2 = down[2 * p : 2 * p + 2].reshape(2 * LANES, width)
        columns = pl.ds(p * 2 * LANES, 2 * LANES)
        for m in range(micros):
            gh[m * group : (m + 1) * group, columns] = dot_nt(g[:, m].reshape(group, width), d2).astype(BF)
        copies.append(pltpu.make_async_copy(gh.at[:, columns], gh_ref.at[:, columns], sem_o.at[p]))
        copies[-1].start()
    wait_all(copies)


def place_of(grid, idx, j, k):
    return lax.rem(idx[2] + (grid.Z - k), grid.Z) * grid.X + lax.rem(idx[3] + (grid.X - j), grid.X)


def expert_kernel(grid, tags, micro, micros, idx, gh_ref, *rest):
    n, X, Z, nd, nt = grid.ne, grid.X, grid.Z, grid.nd, len(tags)
    x_refs, u_refs = rest[:n], rest[n : n + nt]
    rest = rest[n + nt + (3 if micro else 0) :]
    hg_ref, pg_ref, xg_ref = rest[:3]
    from_refs = rest[3 : 3 + X]
    hg, pg, xg, gh, up, gg, back, sem_x, sem_u, sem_g, sem_o = rest[3 + X :]
    local, width = up.shape[0], up.shape[1]
    tokens = xg.shape[0]
    rows = tokens // n
    mine = pl.ds(micro * tokens, tokens)
    get_x = []
    for j in range(X):
        for k in range(Z):
            at = pl.multiple_of(place_of(grid, idx, j, k) * rows, rows)
            i = j * Z + k
            get_x.append(
                pltpu.make_async_copy(
                    x_refs[i].at[pl.ds(micro * rows, rows), :], xg.at[pl.ds(at, rows), :], sem_x.at[i]
                )
            )
            get_x[-1].start()
    get_u = fetch_experts(grid, idx, u_refs, tags, up, 1, sem_u)
    get_g = pltpu.make_async_copy(gh_ref.at[mine, :], gh, sem_g.at[0])
    get_g.start()
    first = (idx[2] * X + idx[3]) * local
    gg[...] = jnp.zeros_like(gg)
    lane = lanes_of((tokens, EXPERTS))
    wait_all(get_x)
    copies = [pltpu.make_async_copy(xg, xg_ref.at[mine, :], sem_o.at[0])]
    copies[0].start()
    wait_all(get_u)
    get_g.wait()

    def pair(p, carry):
        w2 = jnp.concatenate([up[2 * p], up[2 * p + 1]], axis=1)
        pre = dot(xg[:, :width], w2)
        columns = pl.ds(pl.multiple_of(p * 2 * LANES, 2 * LANES), 2 * LANES)
        grad = gh[:, columns].astype(F32)
        at = first + 2 * p
        gates = pltpu.roll(xg[:, width:].astype(F32), EXPERTS - at, 1)
        gate = jnp.concatenate(
            [jnp.broadcast_to(col(gates, i), (tokens, LANES)) for i in range(2)], axis=1
        )
        sig = sigmoid(pre)
        hidden = (pre * sig).astype(BF).astype(F32)
        part = hidden * grad
        total = gg[...]
        for i in range(2):
            each = jnp.sum(head(part, i), axis=1, keepdims=True)
            total = total + jnp.where(lane == at + i, each, 0.0)
        gg[...] = total
        hg[:, columns] = (gate * hidden).astype(BF)
        pg[:, columns] = (gate * grad * sig * (1.0 + pre * (1.0 - sig))).astype(BF)
        return carry

    lax.fori_loop(0, local // 2, pair, 0, unroll=2)
    for i, (src, dst) in enumerate(((hg, hg_ref), (pg, pg_ref)), 1):
        copies.append(pltpu.make_async_copy(src, dst.at[mine, :], sem_o.at[i]))
        copies[-1].start()
    piece = width // nd

    def blocks(columns):
        for j in range(X):
            for k in range(Z):
                at = pl.multiple_of(place_of(grid, idx, j, k) * rows, rows)
                from_refs[j][k, :, columns] = back[pl.ds(at, rows), : columns.size].astype(BF)

    for q in range(nd):
        columns = pl.ds(q * piece, piece)
        w = jnp.concatenate([up[e, columns, :] for e in range(local)], axis=1)
        back[:, :piece] = dot_nt(pg[...], w)
        blocks(columns)
    back[:, :EXPERTS] = gg[...]
    blocks(pl.ds(width, EXPERTS))
    wait_all(copies)


def out_kernel(grid, tags, micros, idx, hg_ref, *rest):
    nd, nt = grid.nd, len(tags)
    d_refs, (out_ref, hg, down, sem_g, sem_d) = rest[:nt], rest[nt:]
    local, width = down.shape[0], down.shape[2]
    group = hg.shape[0] // micros
    rows = group // grid.ne
    piece = width // nd
    get_d = fetch_experts(grid, idx, d_refs, tags, down, 2, sem_d)
    get_g = pltpu.make_async_copy(hg_ref, hg, sem_g.at[0])
    get_g.start()
    wait_all(get_d)
    get_g.wait()
    for q in range(nd):
        columns = pl.ds(q * piece, piece)
        back = dot(hg[...], down[:, :, columns].reshape(local * LANES, piece)).astype(BF)
        for e in range(grid.ne):
            for m in range(micros):
                at = m * group + e * rows
                out_ref[e, m * rows : (m + 1) * rows, columns] = back[at : at + rows]


def to_dp_place(grid, idx, k, r, piece):
    at = lax.rem(idx[0] + k, grid.Y) * grid.C + lax.rem(idx[1] + r, grid.C)
    return pl.ds(pl.multiple_of(at * piece, piece), piece)


def up_grad_kernel(grid, idx, x_ref, pg_ref, *rest):
    outs, acc = rest[:-1], rest[-1]
    acc[...] = dot_tn(x_ref[...], pg_ref[...])
    piece = outs[0].shape[2]
    for k, r in dp_tags(grid):
        rows = to_dp_place(grid, idx, k, r, piece)
        for e in range(outs[r].shape[1]):
            outs[r][k, e] = acc[rows, e * LANES : (e + 1) * LANES].astype(BF)


def down_grad_kernel(grid, idx, g_ref, hg_ref, *rest):
    outs, acc = rest[:-1], rest[-1]
    places, micros, rows, width = g_ref.shape
    g = jnp.concatenate([g_ref[:, m].reshape(places * rows, width) for m in range(micros)], axis=0)
    acc[...] = dot_tn(hg_ref[...], g)
    piece = outs[0].shape[3]
    for k, r in dp_tags(grid):
        columns = to_dp_place(grid, idx, k, r, piece)
        for e in range(outs[r].shape[1]):
            outs[r][k, e] = acc[e * LANES : (e + 1) * LANES, columns].astype(BF)


def fold_kernel(idx, own, *refs):
    Z = own.shape[0]
    others, out = refs[:-Z], refs[-Z:]
    del idx
    for k in range(Z):
        at = (Z - k) % Z
        total = own[at].astype(F32)
        for ref in others:
            total = total + ref[at].astype(F32)
        out[k][...] = total.astype(BF)


def fold_at_kernel(idx, own, *refs):
    Z = own.shape[0]
    others, out = refs[:-Z], refs[-Z:]
    for k in range(Z):
        at = lax.rem(idx[2] + k, Z)
        total = own[at].astype(F32)
        for ref in others:
            total = total + ref[at].astype(F32)
        out[k][...] = total.astype(BF)


def sum_kernel(*refs):
    total = refs[0][...].astype(F32)
    for ref in refs[1:-1]:
        total = total + ref[...].astype(F32)
    refs[-1][...] = total


def sum_places_kernel(parts, own, out):
    total = own[...]
    for z in range(parts.shape[0]):
        total = total + parts[z].astype(F32)
    out[...] = total


def back_norm_kernel(grid, micros, idx, wmr_ref, res_ref, g_ref, router_ref, picked_ref, *rest):
    nd, Z = grid.nd, grid.Z
    n = micros * Z
    rg_ref, bg_ref, late_ref = rest[n : n + 3]
    cols = rest[n + 3 :]
    width = res_ref.shape[1]
    parts = []
    for m in range(micros):
        total = rest[m * Z][...].astype(F32)
        for ref in rest[m * Z + 1 : (m + 1) * Z]:
            total = total + ref[...].astype(F32)
        parts.append(total)
    back = jnp.concatenate(parts, axis=0)
    router = router_ref[...]
    late = (back[:, width:] * picked_ref[...] * router * (1.0 - router)).astype(BF)
    late_ref[...] = late
    unit, inverse = norm_stats(res_ref[...])
    n2g = dot_nt(late, wmr_ref[:, LANES:])
    a = n2g * gain_row(wmr_ref[:, :LANES], LANE_GAIN_TWO)
    res_grad = g_ref[...].astype(F32) + back[:, :width] + norm_back(a, unit, inverse)
    rg_ref[...] = res_grad
    bg_ref[...] = res_grad.astype(BF)
    piece = width // nd
    for ref, (k, r) in zip(cols, dp_tags(grid)):
        at = lax.rem(idx[0] + k, grid.Y) * grid.C + lax.rem(idx[1] + r, grid.C)
        ref[...] = bg_ref[:, pl.ds(pl.multiple_of(at * piece, piece), piece)]


def back_attend_kernel(grid, tags, idx, bg_ref, rg_ref, sig_ref, mask_ref, early_ref, qk_ref, val_ref, va_ref,
                       pr_ref, *rest):
    n = len(tags)
    o_refs = rest[:n]
    late_ref, vag_ref, wo, sem_o = rest[n:]
    get_o = fetch_rows(grid, idx, o_refs, tags, wo, sem_o, COL_OUT)
    bg = bg_ref[...]
    tokens = bg.shape[0]
    sig, gate = sig_ref[...], early_ref[:, H * DH :]
    lane = lanes_of((tokens, LANES))
    logits = jnp.zeros((tokens, LANES), F32)
    wait_all(get_o)
    for h in range(H):
        att = early_ref[:, h * DH : (h + 1) * DH]
        mg = dot(bg, wo[:, h * EA * DH : (h + 1) * EA * DH])
        ag = jnp.zeros((tokens, DH), F32)
        for e in range(EA):
            i = HE + h * EA + e
            ag = ag + col(gate, i) * head(mg, e)
            each = jnp.sum(head(mg, e) * att, axis=1, keepdims=True)
            logits = jnp.where(lane == i, each, logits)
        ag = ag.astype(BF)
        prob = pr_ref[:, h * tokens : (h + 1) * tokens]
        vg = dot_tn(prob.astype(BF), ag)
        pgrad = dot_nt(ag, val_ref[:, h * DH : (h + 1) * DH])
        delta = jnp.sum(prob * pgrad, axis=-1, keepdims=True)
        sg = (prob * (pgrad - delta) * SCALE).astype(BF)
        late_ref[:, h * DH : (h + 1) * DH] = dot(
            sg, qk_ref[:, (H + h) * DH : (H + h + 1) * DH]
        ).astype(BF)
        late_ref[:, (H + h) * DH : (H + h + 1) * DH] = dot_tn(
            sg, qk_ref[:, h * DH : (h + 1) * DH]
        ).astype(BF)
        late_ref[:, COL_VG + h * DH : COL_VG + (h + 1) * DH] = vg.astype(BF)
        for e in range(EA):
            i = h * EA + e
            each = jnp.sum(va_ref[:, i * DH : (i + 1) * DH] * vg, axis=1, keepdims=True)
            logits = jnp.where(lane == i, each, logits)
            vag_ref[:, i * DH : (i + 1) * DH] = (col(gate, i) * vg).astype(BF)
    late_ref[:, COL_LG:COL_VG] = (logits * mask_ref[...] * sig * (1.0 - sig)).astype(BF)
    late_ref[:, COL_RG:] = rg_ref[...]


def back_token_kernel(grid, a_tags, idx, x_ref, rg_ref, late_ref, vag_ref, *rest):
    na = len(a_tags)
    a_refs = rest[:na]
    gt_ref, wa, wv, sem_a, sem_v = rest[na:]
    get_a = fetch_rows(grid, idx, a_refs, a_tags, wa, sem_a)
    get_v = fetch_rows(grid, idx, a_refs, a_tags, wv, sem_v, COL_VALUES)
    unit, inverse = norm_stats(x_ref[...].astype(F32))
    wait_all(get_a)
    n1g = dot_nt(late_ref[:, :COL_VG], wa[:, :COL_ROUTER])
    b = n1g * gain_row(wa[:, COL_SEL:COL_ROUTER], LANE_GAIN_ONE)
    wait_all(get_v)
    gt_ref[...] = rg_ref[...] + dot_nt(vag_ref[...], wv[...]) + norm_back(b, unit, inverse)


def stacked(refs, first=0, last=None):
    return jnp.concatenate([r[:, first:last] for r in refs], axis=0)


def in_order(grid, idx, ref, first=0, size=None):
    size = ref.shape[2] - first if size is None else size
    return jnp.concatenate(
        [ref[shard_at(grid, idx, k, r), :, pl.ds(first, size)] for k, r in dp_tags(grid)], axis=0
    )


def by_owner(grid, idx, out_refs, value, first=0):
    X, Z = grid.X, grid.Z
    mine = value.shape[0] // (X * Z)
    columns = pl.ds(first, value.shape[1])
    for z in range(Z):
        blocks = [value[(z * X + x) * mine : (z * X + x + 1) * mine] for x in range(X)]
        for j in range(X):
            chosen = blocks[0]
            for x in range(1, X):
                chosen = jnp.where(lax.rem(idx[3] + j, X) == x, blocks[x], chosen)
            out_refs[j][z, :, columns] = chosen.astype(BF)


def grad_out_kernel(grid, idx, early, *refs):
    nd = grid.nd
    bgs, out = refs[:nd], refs[nd:]
    wide = H * DH
    gate = in_order(grid, idx, early, wide)
    att = in_order(grid, idx, early, 0, wide)
    by_owner(grid, idx, out, dot_tn(stacked(bgs), mixed_of(gate, att, HE)))


def own_columns(grid, idx, cols, which):
    piece = cols.shape[2] // (3 * grid.nd)
    at = which * piece * grid.nd + shard_at(grid, idx, 0, 0) * piece
    return in_order(grid, idx, cols, pl.multiple_of(at, piece), piece)


def grad_rest_kernel(grid, idx, cols, early, a_ref, *refs):
    nd = grid.nd
    late, out = refs[:nd], refs[nd:]
    x, n1, n2 = [own_columns(grid, idx, cols, i) for i in range(3)]
    acts = stacked(late)
    both = dot_tn(n1, acts[:, :COL_VG])
    by_owner(grid, idx, out, both[:, :COL_SEL])
    misc = a_ref[:, COL_SEL:COL_ROUTER].astype(F32)
    stats = in_order(grid, idx, early, H * DH)
    unit = (x.astype(F32) - col(stats, LANE_MEAN)) * col(stats, LANE_INVERSE)
    n1_grad = dot_nt(acts[:, :COL_VG], a_ref[:, :COL_ROUTER])
    n2_grad = dot_nt(acts[:, COL_RG:], a_ref[:, COL_ROUTER:])
    one = jnp.sum(n1_grad * unit, axis=0, keepdims=True)
    gains = jnp.transpose(misc)[LANE_GAIN_TWO : LANE_GAIN_TWO + 1]
    two = jnp.sum(n2_grad * n2.astype(F32), axis=0, keepdims=True) / gains
    row = rows_of((LANES, one.shape[1]))
    extra = jnp.where(row == LANE_GAIN_ONE, one, 0.0)
    extra = jnp.where(row == LANE_GAIN_TWO, two, extra)
    by_owner(grid, idx, out, both[:, COL_SEL:] + jnp.transpose(extra), COL_SEL)
    by_owner(grid, idx, out, dot_tn(n2, acts[:, COL_RG:]), COL_ROUTER)
    mixed = mixed_of(stats, acts[:, COL_VG:COL_RG].astype(F32), 0)
    by_owner(grid, idx, out, dot_tn(x, mixed), COL_VALUES)


def finish_kernel(*refs):
    parts, (q, k, v, vs, os, router, one, two) = refs[:-8], refs[-8:]
    total = parts[0][...].astype(F32)
    for ref in parts[1:]:
        total = total + ref[...].astype(F32)
    wide = H * DH
    q[...] = total[:, :wide]
    k[...] = total[:, wide:COL_SEL]
    misc = total[:, COL_SEL:COL_ROUTER]
    turned = jnp.transpose(misc)
    vs[...] = turned[:HE]
    os[...] = turned[HE : 2 * HE]
    one[...] = turned[LANE_GAIN_ONE : LANE_GAIN_ONE + 1]
    two[...] = turned[LANE_GAIN_TWO : LANE_GAIN_TWO + 1]
    router[...] = total[:, COL_ROUTER:COL_VALUES]
    v[...] = total[:, COL_VALUES:]


def shape(dims, dtype):
    return jax.ShapeDtypeStruct(dims, dtype)


def call(name, kernel, operands, specs, outs, scratch=(), mib=58, us=5, aliases=None):
    outs = [o if isinstance(o, tuple) else (o, VMEM) for o in outs]
    operands = [
        o if s is SMEM else pltpu.with_memory_space_constraint(o, pltpu.HBM)
        for o, s in zip(operands, specs, strict=True)
    ]
    return pl.pallas_call(
        kernel,
        out_shape=tuple(pltpu.HBM(o[0].shape, o[0].dtype) for o in outs),
        in_specs=list(specs),
        out_specs=tuple(o[1] for o in outs),
        scratch_shapes=list(scratch),
        input_output_aliases=aliases or {},
        compiler_params=pltpu.CompilerParams(vmem_limit_bytes=mib * 1024 * 1024),
        cost_estimate=pl.CostEstimate(
            flops=us, bytes_accessed=us, transcendentals=0
        ),
        name=name,
    )(*operands)


def dma(n):
    return pltpu.SemaphoreType.DMA((n,))


def per_device(
    nd,
    ne,
    tokens,
    cotangent,
    segments,
    value_picks,
    output_picks,
    expert_picks,
    attn_gain,
    query_weight,
    key_weight,
    value_weight,
    output_expert_weight,
    value_select,
    output_select,
    moe_gain,
    router_weight,
    up_weight,
    down_weight,
):
    grid = Grid(nd, ne)
    X, Y, Z, C = grid.X, grid.Y, grid.Z, grid.C
    micros, length, width = tokens.shape
    rows = micros * length
    local = up_weight.shape[0]
    piece = width // nd
    wide = H * DH
    values_wide = HE * DH
    dp, ex = lax.axis_index("dp"), lax.axis_index("expert")
    idx = jnp.stack([dp // C, dp % C, ex // X, ex % X]).astype(jnp.int32)


    x_all = tokens.reshape(rows, width)
    g_all = cotangent.reshape(rows, width)

    ends = (*STARTS[1:], COL_A)
    block_w, block_a, *parts_a = call(
        "pack",
        functools.partial(pack_kernel, grid),
        (
            idx,
            query_weight,
            key_weight,
            value_select.T,
            output_select.T,
            attn_gain,
            moe_gain,
            router_weight,
            value_weight,
            output_expert_weight,
        ),
        [SMEM] + [VMEM] * 9,
        [shape((piece, COL_A), BF), shape((piece, COL_VALUES), BF)]
        + [shape((piece // X, high - low), BF) for low, high in zip(STARTS, ends)],
        [pltpu.VMEM((LANES, piece), F32)],
        us=3,
    )

    def to_y(v, *deps):
        v = after(v, *deps)
        return [grid.rot_y(v, k) for k in range(1, Y)]

    def over_x(got_y, *deps):
        return [[v] + [grid.rot_x(after(v, *deps), j) for j in range(1, X)] for v in got_y]

    def add_pieces(arrays, tags, v, tag, swapped=None):
        k, split, j, column = tag
        arrays.append(v)
        tags.append((k, 0, split, j, column))
        if C > 1:
            arrays.append(grid.swap(v) if swapped is None else swapped)
            tags.append((k, 1, split, j, column))

    def swap(v, *deps):
        return grid.swap(after(v, *deps)) if C > 1 else None

    def spread_x(got_y, *deps):
        return [[v] + [grid.rot_x(after(v, *deps), j) for j in range(1, X)] for v in got_y]

    def swap_all(values, *deps):
        return [swap(v, *deps) for v in values]

    def flat(by_k):
        return [v for by_j in by_k for v in by_j]

    g_gathered = lax.all_gather(g_all, "expert", axis=0, tiled=True)
    swap_w = swap(block_w)
    seg = segments.reshape(1, rows)
    v_picks, o_picks = value_picks.reshape(rows, 2 * H), output_picks.reshape(rows, 2 * H)
    e_picks = expert_picks.reshape(rows, -1)
    done = [swap_w, seg, v_picks, o_picks, e_picks]
    over_y, over_x_too, swap_y, swap_x = [to_y(parts_a[0])], [], [], []
    done.append(over_y[0])
    swap_d = swap_u = d_y = None
    for i in range(len(STARTS)):
        last_round = i == len(STARTS) - 1
        new = []
        if not last_round:
            over_y.append(to_y(parts_a[i + 1], *done))
            new += over_y[-1]
        else:
            d_y = to_y(down_weight, *done)
            swap_u = swap(up_weight, *done)
            new.append(swap_u)
        if i == len(STARTS) - 2:
            new.append(g_gathered)
            swap_d = swap(down_weight, *done)
            new.append(swap_d)
        over_x_too.append(spread_x(over_y[i], *done))
        swap_y.append(swap_all(over_y[i], *done))
        new += flat(over_x_too[-1]) + swap_y[-1]
        if i:
            swap_x.append([swap_all(by_j[1:], *done) for by_j in over_x_too[i - 1]])
            new += flat(swap_x[-1])
        done = new
    swap_x.append([swap_all(by_j[1:], *done) for by_j in over_x_too[-1]])
    done = flat(swap_x[-1])

    def weight_pieces(own, swapped, chunks):
        arrays, tags = [own, swapped], [(0, 0, None, 0, 0), (0, 1, None, 0, 0)]
        for column, got, others in chunks:
            for k, (by_j, swaps) in enumerate(zip(got, others), 1):
                for j, (v, o) in enumerate(zip(by_j, swaps)):
                    split = "x" if len(by_j) > 1 else None
                    arrays += [v, o]
                    tags += [(k, 0, split, j, column), (k, 1, split, j, column)]
        return arrays, tags

    chunks = [
        (low, got, [[v] + more for v, more in zip(ys, xs)])
        for low, got, ys, xs in zip(STARTS, over_x_too, swap_y, swap_x)
    ]
    first_pieces, first_tags = weight_pieces(block_w, swap_w, chunks[:1])
    a_pieces, a_tags = weight_pieces(block_w, swap_w, chunks)

    n1, qk, sig, mask, probs, wmr = call(
        "attend",
        functools.partial(attend_kernel, grid, first_tags, length),
        (
            idx,
            x_all,
            seg,
            v_picks,
            o_picks,
            *first_pieces,
        ),
        [SMEM] + [VMEM] * 4 + [ANY] * len(first_pieces),
        [
            shape((rows, width), BF),
            shape((rows, 2 * wide), BF),
            shape((rows, LANES), F32),
            shape((rows, LANES), F32),
            shape((rows, H * rows), F32),
            shape((width, 2 * LANES), BF),
        ],
        [pltpu.VMEM((width, COL_VALUES), BF), dma(len(first_pieces))],
        us=4,
    )
    v_pieces, v_tags = window(a_pieces, a_tags, COL_VALUES, COL_OUT)
    o_pieces, o_tags = window(a_pieces, a_tags, COL_OUT, COL_A)
    vals, va, early, res, router, picked, xg, cols = call(
        "route",
        functools.partial(route_kernel, grid, v_tags, o_tags),
        (idx, x_all, n1, sig, mask, probs, wmr, e_picks, *v_pieces, *o_pieces),
        [SMEM] + [VMEM] * 7 + [ANY] * (len(v_pieces) + len(o_pieces)),
        [
            shape((rows, wide), BF),
            shape((rows, values_wide), F32),
            shape((rows, wide + LANES), F32),
            shape((rows, width), F32),
            shape((rows, EXPERTS), F32),
            shape((rows, EXPERTS), F32),
            shape((rows, width + EXPERTS), BF),
            shape((rows, 3 * width), BF),
        ],
        [
            pltpu.VMEM((width, values_wide), BF),
            pltpu.VMEM((width, values_wide), BF),
            dma(len(v_pieces)),
            dma(len(o_pieces)),
        ],
        us=8,
    )

    group = ne * length
    ff = local * LANES
    swap_dy = swap_all(d_y, xg)
    u_y = to_y(up_weight, xg, *d_y)
    column, x_over, done = [xg], [], []
    for k in range(1, Z):
        held = after(column[-1], *done)
        column.append(grid.rot_z(held, 1))
        x_over.append([grid.rot_x(held, j) for j in range(1, X)])
        last_done, done = done, [column[-1], x_over[-1], *([u_y] if k == Z - 2 else [])]
    ring_done = done
    swap_uy = swap_all(u_y, *last_done)

    def expert_pieces(own, swapped, got, others):
        arrays, tags = [own, swapped], [(0, 0, 0), (0, 1, 0)]
        for k, (v, o) in enumerate(zip(got, others), 1):
            arrays += [v, o]
            tags += [(k, 0, 0), (k, 1, 0)]
        return arrays, tags

    d_pieces, d_tags = expert_pieces(down_weight, swap_d, d_y, swap_dy)
    u_pieces, u_tags = expert_pieces(up_weight, swap_u, u_y, swap_uy)
    g_rows = g_gathered.reshape(ne, micros, length, width)
    total = micros * group
    (ahead,) = call(
        "ahead",
        functools.partial(ahead_kernel, grid, d_tags),
        (idx, after(g_rows, *last_done), *d_pieces),
        [SMEM] + [ANY] * (1 + len(d_tags)),
        [(shape((total, ff), BF), ANY)],
        [
            pltpu.VMEM((ne, micros, length, width), BF),
            pltpu.VMEM((local, LANES, width), BF),
            pltpu.VMEM((total, ff), BF),
            dma(1),
            dma(len(d_tags)),
            dma(local // 2),
        ],
        us=9,
    )
    x_over.append([grid.rot_x(after(column[-1], ahead, *ring_done), j) for j in range(1, X)])
    x_pieces = column + [by_j[j] for j in range(X - 1) for by_j in x_over]
    froms = []

    def over_x(parts):
        return [grid.rot_x(parts[j], -j) for j in range(1, X)]

    def fold(parts, others, *deps):
        return call(
            "fold",
            fold_kernel,
            (idx, after(parts[0], *deps), *others),
            [SMEM] + [VMEM] * X,
            [shape(parts[0].shape[1:], BF)] * Z,
            us=2,
        )

    sent, shared = [], []
    for m in range(micros):
        hg, pg, x_group, *back = call(
            "experts",
            functools.partial(expert_kernel, grid, u_tags, m, micros),
            (idx, ahead, *x_pieces, *u_pieces, *shared),
            [SMEM, ANY] + [ANY] * (ne + len(u_tags) + len(shared)),
            [
                (shape((total, ff), BF), ANY),
                (shape((total, ff), BF), ANY),
                (shape((total, width + EXPERTS), BF), ANY),
                *[shape((Z, length, width + EXPERTS), BF)] * X,
            ],
            [
                pltpu.VMEM((group, ff), BF),
                pltpu.VMEM((group, ff), BF),
                pltpu.VMEM((group, width + EXPERTS), BF),
                pltpu.VMEM((group, ff), BF),
                pltpu.VMEM((local, width, LANES), BF),
                pltpu.VMEM((group, EXPERTS), F32),
                pltpu.VMEM((group, max(piece, EXPERTS)), F32),
                dma(ne),
                dma(len(u_tags)),
                dma(1),
                dma(3),
            ],
            us=12,
            aliases={2 + ne + len(u_tags) + i: i for i in range(len(shared))},
        )
        shared = [hg, pg, x_group]
        sent.append(back)

    def out_rows(*deps):
        return call(
            "out",
            functools.partial(out_kernel, grid, d_tags, micros),
            (idx, after(hg, *deps), *d_pieces),
            [SMEM] + [ANY] * (1 + len(d_tags)),
            [shape((ne, rows, width), BF)],
            [
                pltpu.VMEM((total, ff), BF),
                pltpu.VMEM((local, LANES, width), BF),
                dma(1),
                dma(len(d_tags)),
            ],
            us=10,
        )

    def expert_grad(name, kernel, lhs, rhs, dims, *deps):
        halves = 2
        block = pl.BlockSpec((Y, local // halves, *dims), lambda h, idx: (0, h, 0, 0))
        if lhs.ndim == 4:
            whole = pl.BlockSpec((ne, micros, length, width), lambda h, idx: (0, 0, 0, 0))
        else:
            whole = pl.BlockSpec((total, width), lambda h, idx: (0, 0))
        part = (width, ff // halves) if lhs.ndim == 2 else (ff // halves, width)
        return pl.pallas_call(
            functools.partial(kernel, grid),
            out_shape=[pltpu.HBM((Y, local, *dims), BF)] * C,
            grid_spec=pltpu.PrefetchScalarGridSpec(
                num_scalar_prefetch=1,
                grid=(halves,),
                in_specs=[whole, pl.BlockSpec((total, ff // halves), lambda h, idx: (0, h))],
                out_specs=[block] * C,
                scratch_shapes=[pltpu.VMEM(part, F32)],
            ),
            compiler_params=pltpu.CompilerParams(vmem_limit_bytes=58 * 1024 * 1024),
            cost_estimate=pl.CostEstimate(flops=4, bytes_accessed=12, transcendentals=0),
            name=name,
        )(idx, *[pltpu.with_memory_space_constraint(v, pltpu.HBM) for v in (after(lhs, *deps), rhs)])

    def added_blocks(name, arrays, dtype, split):
        steps = 2
        dims = arrays[0].shape[1:] if split else arrays[0].shape
        some = (dims[0] // steps, *dims[1:])
        one = pl.BlockSpec(some, lambda i: (i, 0, 0))
        spec = pl.BlockSpec((Y, *some), lambda i: (0, i, 0, 0)) if split else one
        results = Y if split else 1

        def kernel(*refs):
            for k, out in enumerate(refs[len(arrays) :]):
                total = 0.0
                for ref in refs[: len(arrays)]:
                    total = total + (ref[k] if split else ref[...]).astype(F32)
                out[...] = total.astype(dtype)

        return pl.pallas_call(
            kernel,
            out_shape=[pltpu.HBM(dims, dtype)] * results,
            grid=(steps,),
            in_specs=[spec] * len(arrays),
            out_specs=[one] * results,
            compiler_params=pltpu.CompilerParams(vmem_limit_bytes=58 * 1024 * 1024),
            cost_estimate=pl.CostEstimate(flops=1, bytes_accessed=3, transcendentals=0),
            name=name,
        )(*[pltpu.with_memory_space_constraint(v, pltpu.HBM) for v in arrays])

    down_args = ("down_grad", down_grad_kernel, g_rows, hg, (LANES, piece))
    up_args = ("up_grad", up_grad_kernel, x_group, pg, (piece, LANES))

    def reduce_y(total, *deps):
        got = [grid.rot_y(after(total[k], *deps), k) for k in range(1, Y)]
        return lambda *more: added_blocks("last_sum", [after(total[0], *more), *got], F32, False)[0], got

    from_x = [over_x(v) for v in sent]
    sums = fold(sent[0], from_x[0], hg)
    froms.append(grid.send_z(sums))
    outs_sent = out_rows(sums[0])
    before, down_came, up_came = outs_sent[0], [], []
    for m in range(1, micros):
        sums = fold(sent[m], from_x[m], before, froms[-1])
        froms.append(grid.send_z(sums))
        before = sums[0]
    down_near, *down_far = expert_grad(*down_args, before)
    up_near, *up_far = expert_grad(*up_args, down_near)
    before = up_near

    early_all = lax.all_gather(after(early, u_pieces), "dp", axis=0)
    cols_all = lax.all_gather(after(cols, u_pieces), "dp", axis=0)
    res_grad, bg, rg, *bg_cols = call(
        "back_norm",
        functools.partial(back_norm_kernel, grid, micros),
        (
            idx,
            wmr,
            res,
            g_all,
            after(router, before, early_all, cols_all),
            picked,
            *[p for f in froms for p in f],
        ),
        [SMEM] + [VMEM] * (5 + micros * Z),
        [
            shape((rows, width), F32),
            shape((rows, width), BF),
            shape((rows, EXPERTS), BF),
            *[shape((rows, piece), BF)] * nd,
        ],
        us=3,
    )
    bgs = [v if t == (0, 0) else grid.rot_yc(v, *t) for v, t in zip(bg_cols, dp_tags(grid))]
    late, vag = call(
        "back_attend",
        functools.partial(back_attend_kernel, grid, o_tags),
        (idx, bg, rg, sig, mask, early, qk, vals, va, probs, *o_pieces),
        [SMEM] + [VMEM] * 9 + [ANY] * len(o_pieces),
        [shape((rows, COL_LATE), BF), shape((rows, values_wide), BF)],
        [pltpu.VMEM((width, values_wide), BF), dma(len(o_pieces))],
        us=8,
    )
    outs = lax.all_to_all(after(outs_sent[0], bg), "expert", 0, 0, tiled=True)
    down_came, up_came = swap_all(down_far, bg), swap_all(up_far, bg)
    late_swap = swap(late, bgs[1:], *down_came, *up_came)
    late_y = to_y(late, bgs[1:])

    mine = piece // ne

    def weight_grad(name, kernel, operands, columns):
        parts = call(
            name,
            functools.partial(kernel, grid),
            (idx, *operands),
            [SMEM] + [VMEM] * len(operands),
            [shape((Z, mine, columns), BF)] * X,
            us=3,
        )
        return parts, [grid.rot_x(parts[j], j) for j in range(1, X)]

    def fold_at(parts, others, *deps):
        sums = call(
            "fold_at",
            fold_at_kernel,
            (idx, after(parts[0], *deps), *others),
            [SMEM] + [VMEM] * X,
            [shape(parts[0].shape[1:], BF)] * Z,
            us=1,
        )
        return sums[0], grid.send_z(sums)

    def added(parts, *deps):
        return call(
            "sum",
            sum_kernel,
            (after(parts[0], *deps), *parts[1:]),
            [VMEM] * len(parts),
            [shape(parts[0].shape, F32)],
            us=1,
        )[0]

    down_sum = added_blocks("core_sum", [after(down_near, late), *down_came], BF, True)
    up_sum = added_blocks("core_sum", [after(up_near, down_sum), *up_came], BF, True)
    o_parts, o_others = weight_grad(
        "grad_out", grad_out_kernel, [after(early_all, up_sum), *bgs], values_wide
    )
    down_last, down_got = reduce_y(down_sum, late_y)
    up_last, up_got = reduce_y(up_sum, late_y)
    late_all = [late, *late_y, late_swap, *swap_all(late_y, o_parts[0])]
    r_parts, r_others = weight_grad(
        "grad_rest",
        grad_rest_kernel,
        [after(cols_all, o_parts[0]), early_all, block_a, *late_all],
        COL_OUT,
    )
    o_fold, o_sums = fold_at(o_parts, o_others, r_parts[0])
    r_fold, r_sums = fold_at(r_parts, r_others, o_sums, outs)
    grad_down = down_last(r_fold)
    grad_up = up_last(grad_down)
    (grad_tokens,) = call(
        "back_token",
        functools.partial(back_token_kernel, grid, a_tags),
        (idx, x_all, res_grad, after(late, r_fold), vag, *a_pieces),
        [SMEM] + [VMEM] * 4 + [ANY] * len(a_pieces),
        [shape((rows, width), F32)],
        [
            pltpu.VMEM((width, COL_VALUES), BF),
            pltpu.VMEM((width, values_wide), BF),
            dma(len(a_pieces)),
            dma(len(a_pieces)),
        ],
        us=8,
    )
    (output,) = call(
        "add_out",
        sum_places_kernel,
        (outs, after(res, grad_tokens)),
        [VMEM] * 2,
        [shape((rows, width), F32)],
        us=2,
    )
    grad_output = added(o_sums, output)
    q, k, grad_value, vs, os, r, one, two = call(
        "finish",
        finish_kernel,
        (after(r_sums[0], grad_tokens, output, grad_output, grad_up), *r_sums[1:]),
        [VMEM] * Z,
        [
            shape((mine, wide), F32),
            shape((mine, wide), F32),
            shape((mine, values_wide), F32),
            shape((HE, mine), F32),
            shape((HE, mine), F32),
            shape((mine, EXPERTS), F32),
            shape((1, mine), F32),
            shape((1, mine), F32),
        ],
        us=1,
    )
    return (
        output.reshape(micros, length, width),
        grad_tokens.reshape(micros, length, width),
        one.reshape(mine),
        q,
        k,
        grad_value,
        grad_output,
        vs.T,
        os.T,
        two.reshape(mine),
        r,
        grad_up,
        grad_down,
    )


def solution(mesh):
    rows = ("dp", "expert")
    placed = (
        P(None, rows, None),
        P(None, rows, None),
        P(None, rows, None),
        P(None, rows, None, None),
        P(None, rows, None, None),
        P(None, rows, None),
        P("dp"),
        P("dp", None),
        P("dp", None),
        P("dp", None),
        P("dp", None),
        P("dp", None),
        P("dp", None),
        P("dp"),
        P("dp", None),
        P("expert", "dp", None),
        P("expert", None, "dp"),
    )
    return jax.shard_map(
        functools.partial(per_device, mesh.shape["dp"], mesh.shape["expert"]),
        mesh=mesh,
        in_specs=placed,
        out_specs=(
            P(None, rows, None),
            P(None, rows, None),
            P(rows),
            P(rows, None),
            P(rows, None),
            P(rows, None),
            P(rows, None),
            P(rows, None),
            P(rows, None),
            P(rows),
            P(rows, None),
            P("expert", "dp", None),
            P("expert", None, "dp"),
        ),
        check_vma=False,
    )
```

```python
import functools

import jax
import jax.numpy as jnp
from jax import lax
from jax.experimental import pallas as pl
from jax.experimental.pallas import tpu as pltpu
from jax.sharding import PartitionSpec as P

H = 4
DH = 128
EA = 5
HE = H * EA
EXPERTS = 128
EPSILON = 1e-05
MASKED = -1e30
SCALE = DH ** (-0.5)
LANES = 128

BF = jnp.bfloat16
F32 = jnp.float32

COL_SEL = 2 * H * DH
COL_ROUTER = COL_SEL + LANES
COL_VALUES = COL_ROUTER + LANES
COL_OUT = COL_VALUES + HE * DH
COL_A = COL_OUT + HE * DH
STARTS = (0, 17 * LANES, 34 * LANES)
LANE_GAIN_ONE = 2 * HE
LANE_GAIN_TWO = 2 * HE + 1
LANE_MEAN = 2 * HE
LANE_INVERSE = 2 * HE + 1
COL_LG = 2 * H * DH
COL_VG = COL_LG + LANES
COL_RG = COL_VG + H * DH
COL_LATE = COL_RG + LANES

VMEM = pl.BlockSpec()
SMEM = pl.BlockSpec(memory_space=pltpu.SMEM)
ANY = pl.BlockSpec(memory_space=pltpu.HBM)


def dot(a, b):
    return jnp.dot(a, b, preferred_element_type=F32)


def dot_nt(a, b):
    return lax.dot_general(a, b, (((1,), (1,)), ((), ())), preferred_element_type=F32)


def dot_tn(a, b):
    return lax.dot_general(a, b, (((0,), (0,)), ((), ())), preferred_element_type=F32)


def sigmoid(v):
    return 1.0 / (1.0 + jnp.exp(-v))


class Grid:
    def __init__(self, nd, ne):
        self.nd, self.ne = nd, ne
        self.C = 2 if nd % 2 == 0 else 1
        self.Y = nd // self.C
        x = 1
        while (2 * x) * (2 * x) <= ne and ne % (2 * x) == 0:
            x *= 2
        self.X, self.Z = x, ne // x

    def _dp(self, v, go):
        C = self.C
        pairs = []
        for i in range(self.nd):
            y, c = go(i // C, i % C)
            pairs.append((i, y * C + c))
        return lax.ppermute(v, "dp", pairs)

    def _ex(self, v, go):
        X = self.X
        pairs = []
        for i in range(self.ne):
            z, x = go(i // X, i % X)
            pairs.append((i, z * X + x))
        return lax.ppermute(v, "expert", pairs)

    def rot_y(self, v, k):
        return self._dp(v, lambda y, c: ((y + k) % self.Y, c))

    def swap(self, v):
        return self._dp(v, lambda y, c: (y, c ^ 1))

    def rot_yc(self, v, k, r):
        return self._dp(v, lambda y, c: ((y + k) % self.Y, c ^ r))

    def rot_x(self, v, j):
        return self._ex(v, lambda z, x: (z, (x + j) % self.X))

    def rot_z(self, v, k):
        return self._ex(v, lambda z, x: ((z + k) % self.Z, x))

    def lines_z(self):
        return [[z * self.X + x for z in range(self.Z)] for x in range(self.X)]

    def gather_z(self, v):
        return lax.all_gather(v, "expert", axis=0, tiled=True, axis_index_groups=self.lines_z())

    def swap_z(self, v):
        return lax.all_to_all(v, "expert", 0, 0, tiled=True, axis_index_groups=self.lines_z())

    def send_z(self, parts):
        return [parts[0]] + [self.rot_z(parts[k], k) for k in range(1, self.Z)]

    def swap_dp(self, v):
        return lax.all_to_all(v, "dp", 0, 0, tiled=True)


def after(v, *deps):
    flat = [d for dep in deps for d in (dep if isinstance(dep, (list, tuple)) else [dep])]
    if not flat:
        return v
    return lax.optimization_barrier((v, *flat))[0]


def gather_dp(grid, w, over_y, swapped=None):
    got = [w] + list(over_y)
    if grid.C > 1:
        got = got + [grid.swap(w) if swapped is None else swapped] + [grid.swap(v) for v in over_y]
    return got


def dp_tags(grid):
    return [(k, r) for r in range(grid.C) for k in range(grid.Y)]


def shard_at(grid, idx, k, r):
    return lax.rem(idx[0] + (grid.Y - k), grid.Y) * grid.C + lax.rem(idx[1] + r, grid.C)


def fetch_rows(grid, idx, refs, tags, dst, sems, first=0):
    copies = []
    width, last = dst.shape[0] // grid.nd, first + dst.shape[1]
    for i, (ref, (k, r, split, j, column)) in enumerate(zip(refs, tags)):
        low, high = max(first, column), min(last, column + ref.shape[1])
        if low >= high:
            continue
        at = shard_at(grid, idx, k, r) * width
        n = width
        if split is not None:
            size, mine = (grid.X, idx[3]) if split == "x" else (grid.Z, idx[2])
            n = width // size
            at = at + lax.rem(mine + (size - j), size) * n
        at = pl.multiple_of(at, n)
        copy = pltpu.make_async_copy(
            ref.at[:, pl.ds(low - column, high - low)],
            dst.at[pl.ds(at, n), pl.ds(low - first, high - low)],
            sems.at[i],
        )
        copy.start()
        copies.append(copy)
    return copies


def fetch_experts(grid, idx, refs, tags, dst, axis, sems):
    copies = []
    n = dst.shape[axis] // grid.nd
    for i, (ref, (k, r, first)) in enumerate(zip(refs, tags)):
        at = pl.ds(pl.multiple_of(shard_at(grid, idx, k, r) * n, n), n)
        held = pl.ds(first, ref.shape[0])
        place = dst.at[held, at, :] if axis == 1 else dst.at[held, :, at]
        copy = pltpu.make_async_copy(ref, place, sems.at[i])
        copy.start()
        copies.append(copy)
    return copies


def wait_all(copies):
    for copy in copies:
        copy.wait()


def lanes_of(dims):
    return lax.broadcasted_iota(jnp.int32, dims, 1)


def rows_of(dims):
    return lax.broadcasted_iota(jnp.int32, dims, 0)


def norm_stats(v):
    centered = v - jnp.mean(v, axis=-1, keepdims=True)
    inverse = lax.rsqrt(jnp.mean(centered * centered, axis=-1, keepdims=True) + EPSILON)
    return centered * inverse, inverse


def window(pieces, tags, low, high):
    held = [(p, t) for p, t in zip(pieces, tags) if t[4] < high and t[4] + p.shape[1] > low]
    return [p for p, _ in held], [t for _, t in held]


def norm_back(grad, unit, inverse):
    return inverse * (
        grad
        - jnp.mean(grad, axis=-1, keepdims=True)
        - unit * jnp.mean(grad * unit, axis=-1, keepdims=True)
    )


def gain_row(block, lane):
    return jnp.transpose(block.astype(F32))[lane : lane + 1, :]


def col(v, i):
    return v[:, i : i + 1]


def head(v, i):
    return v[:, i * DH : (i + 1) * DH]


def mixed_of(gate, vectors, first):
    return jnp.concatenate(
        [
            (col(gate, first + h * EA + e) * head(vectors, h)).astype(BF)
            for h in range(H)
            for e in range(EA)
        ],
        axis=1,
    )


def pack_kernel(grid, idx, q, k, vs, os, gain_one, gain_two, router, v_ref, o_ref, w_ref, a_ref, *rest):
    parts, misc = rest[:-1], rest[-1]
    piece = q.shape[0]
    nx = piece // grid.X
    at_x = pl.ds(pl.multiple_of(idx[3] * nx, nx), nx)
    misc[...] = jnp.zeros_like(misc)
    misc[:HE, :] = vs[...].astype(F32)
    misc[HE : 2 * HE, :] = os[...].astype(F32)
    misc[LANE_GAIN_ONE : LANE_GAIN_ONE + 1, :] = gain_one[...].astype(F32).reshape(1, piece)
    misc[LANE_GAIN_TWO : LANE_GAIN_TWO + 1, :] = gain_two[...].astype(F32).reshape(1, piece)
    wide = H * DH
    a_ref[:, :wide] = q[...]
    a_ref[:, wide:COL_SEL] = k[...]
    a_ref[:, COL_SEL:COL_ROUTER] = jnp.transpose(misc[...]).astype(BF)
    a_ref[:, COL_ROUTER:] = router[...]
    w_ref[:, :COL_VALUES] = a_ref[...]
    w_ref[:, COL_VALUES:COL_OUT] = v_ref[...]
    w_ref[:, COL_OUT:] = o_ref[...]
    for part, low in zip(parts, STARTS):
        part[...] = w_ref[at_x, low : low + part.shape[1]]


def attend_kernel(grid, tags, length, idx, x_ref, seg_ref, vp, op, *rest):
    n = len(tags)
    a_refs = rest[:n]
    n1_ref, qk_ref, sig_ref, mask_ref, pr_ref, wmr_ref, wa, sem_a = rest[n:]
    get_a = fetch_rows(grid, idx, a_refs, tags, wa, sem_a)
    unit, _ = norm_stats(x_ref[...].astype(F32))
    tokens = unit.shape[0]
    lane = lanes_of((tokens, LANES))
    mask = jnp.zeros((tokens, LANES), F32)
    for h in range(H):
        for k in range(2):
            mask = mask + (lane == col(vp, 2 * h + k) + EA * h).astype(F32)
            mask = mask + (lane == col(op, 2 * h + k) + (EA * h + HE)).astype(F32)
    mask_ref[...] = mask
    square = (tokens, tokens)
    row, lane = rows_of(square), lanes_of(square)
    seg = jnp.broadcast_to(seg_ref[...].astype(F32), square)
    allowed = (seg == jnp.transpose(seg)) & (lane <= row) & (lane // length == row // length)
    wait_all(get_a)
    n1 = (unit * gain_row(wa[:, COL_SEL:COL_ROUTER], LANE_GAIN_ONE)).astype(BF)
    n1_ref[...] = n1
    qks = dot(n1, wa[:, :COL_ROUTER])
    qk = qks[:, :COL_SEL].astype(BF)
    qk_ref[...] = qk
    sig_ref[...] = sigmoid(qks[:, COL_SEL:])
    wmr_ref[...] = wa[:, COL_SEL:]
    for h in range(H):
        scores = dot_nt(head(qk, h), head(qk, H + h))
        scaled = jnp.where(allowed, scores * SCALE, MASKED)
        top = jnp.max(scaled, axis=-1, keepdims=True)
        expo = jnp.where(allowed, jnp.exp(scaled - top), 0.0)
        pr_ref[:, h * tokens : (h + 1) * tokens] = expo / jnp.sum(expo, axis=-1, keepdims=True)


def route_kernel(grid, v_tags, o_tags, idx, x_ref, n1_ref, sig_ref, mask_ref, pr_ref, wmr_ref, ep, *rest):
    nv, no = len(v_tags), len(o_tags)
    v_refs, o_refs = rest[:nv], rest[nv : nv + no]
    rest = rest[nv + no :]
    val_ref, va_ref, early_ref, res_ref, router_ref, picked_ref = rest[:6]
    xg_ref, col_ref, wv, wo, sem_v, sem_o = rest[6:]
    get_v = fetch_rows(grid, idx, v_refs, v_tags, wv, sem_v, COL_VALUES)
    get_o = fetch_rows(grid, idx, o_refs, o_tags, wo, sem_o, COL_OUT)
    gate = sig_ref[...] * mask_ref[...]
    tokens, width = x_ref.shape
    lane = lanes_of((tokens, EXPERTS))
    picked = jnp.zeros((tokens, EXPERTS), F32)
    for k in range(ep.shape[1]):
        picked = picked + (lane == col(ep, k)).astype(F32)
    picked_ref[...] = picked
    x_bf = x_ref[...]
    wait_all(get_v)
    atts = []
    for h in range(H):
        va = dot(x_bf, wv[:, h * EA * DH : (h + 1) * EA * DH])
        va_ref[:, h * EA * DH : (h + 1) * EA * DH] = va
        total = col(gate, h * EA) * head(va, 0)
        for e in range(1, EA):
            total = total + col(gate, h * EA + e) * head(va, e)
        value = total.astype(BF)
        val_ref[:, h * DH : (h + 1) * DH] = value
        atts.append(dot(pr_ref[:, h * tokens : (h + 1) * tokens].astype(BF), value))
    att = jnp.concatenate(atts, axis=1)
    early_ref[:, : H * DH] = att
    mean = jnp.mean(x_bf.astype(F32), axis=-1, keepdims=True)
    centered = x_bf.astype(F32) - mean
    inverse = lax.rsqrt(jnp.mean(centered * centered, axis=-1, keepdims=True) + EPSILON)
    lane = lanes_of((tokens, LANES))
    early_ref[:, H * DH :] = jnp.where(
        lane == LANE_MEAN, mean, jnp.where(lane == LANE_INVERSE, inverse, gate)
    )
    mixed = mixed_of(gate, att, HE)
    wait_all(get_o)
    res = x_bf.astype(F32) + dot_nt(mixed, wo[...])
    res_ref[...] = res
    unit, _ = norm_stats(res)
    n2 = (unit * gain_row(wmr_ref[:, :LANES], LANE_GAIN_TWO)).astype(BF)
    router = sigmoid(dot(n2, wmr_ref[:, LANES:]))
    router_ref[...] = router
    xg_ref[:, :width] = res.astype(BF)
    xg_ref[:, width:] = (router * picked).astype(BF)
    col_ref[:, :width] = x_bf
    col_ref[:, width : 2 * width] = n1_ref[...]
    col_ref[:, 2 * width :] = n2


def ahead_kernel(grid, tags, idx, g_ref, *rest):
    d_refs, (gh_ref, g, down, gh, sem_g, sem_d, sem_o) = rest[: len(tags)], rest[len(tags) :]
    local, width = down.shape[0], down.shape[2]
    micros = g.shape[1]
    get_g = pltpu.make_async_copy(g_ref, g, sem_g.at[0])
    get_g.start()
    get_d = fetch_experts(grid, idx, d_refs, tags, down, 2, sem_d)
    get_g.wait()
    wait_all(get_d)
    group = g.shape[0] * g.shape[2]
    copies = []
    for p in range(local // 2):
        d2 = down[2 * p : 2 * p + 2].reshape(2 * LANES, width)
        columns = pl.ds(p * 2 * LANES, 2 * LANES)
        for m in range(micros):
            gh[m * group : (m + 1) * group, columns] = dot_nt(g[:, m].reshape(group, width), d2).astype(BF)
        copies.append(pltpu.make_async_copy(gh.at[:, columns], gh_ref.at[:, columns], sem_o.at[p]))
        copies[-1].start()
    wait_all(copies)


def place_of(grid, idx, j, k):
    return lax.rem(idx[2] + (grid.Z - k), grid.Z) * grid.X + lax.rem(idx[3] + (grid.X - j), grid.X)


def expert_kernel(grid, tags, micro, micros, idx, gh_ref, *rest):
    n, X, Z, nd, nt = grid.ne, grid.X, grid.Z, grid.nd, len(tags)
    x_refs, u_refs = rest[:n], rest[n : n + nt]
    rest = rest[n + nt + (3 if micro else 0) :]
    hg_ref, pg_ref, xg_ref = rest[:3]
    from_refs = rest[3 : 3 + X]
    hg, pg, xg, gh, up, gg, back, sem_x, sem_u, sem_g, sem_o = rest[3 + X :]
    local, width = up.shape[0], up.shape[1]
    tokens = xg.shape[0]
    rows = tokens // n
    mine = pl.ds(micro * tokens, tokens)
    get_x = []
    for j in range(X):
        for k in range(Z):
            at = pl.multiple_of(place_of(grid, idx, j, k) * rows, rows)
            i = j * Z + k
            get_x.append(
                pltpu.make_async_copy(
                    x_refs[i].at[pl.ds(micro * rows, rows), :], xg.at[pl.ds(at, rows), :], sem_x.at[i]
                )
            )
            get_x[-1].start()
    get_u = fetch_experts(grid, idx, u_refs, tags, up, 1, sem_u)
    get_g = pltpu.make_async_copy(gh_ref.at[mine, :], gh, sem_g.at[0])
    get_g.start()
    first = (idx[2] * X + idx[3]) * local
    gg[...] = jnp.zeros_like(gg)
    lane = lanes_of((tokens, EXPERTS))
    wait_all(get_x)
    copies = [pltpu.make_async_copy(xg, xg_ref.at[mine, :], sem_o.at[0])]
    copies[0].start()
    wait_all(get_u)
    get_g.wait()

    def pair(p, carry):
        w2 = jnp.concatenate([up[2 * p], up[2 * p + 1]], axis=1)
        pre = dot(xg[:, :width], w2)
        columns = pl.ds(pl.multiple_of(p * 2 * LANES, 2 * LANES), 2 * LANES)
        grad = gh[:, columns].astype(F32)
        at = first + 2 * p
        gates = pltpu.roll(xg[:, width:].astype(F32), EXPERTS - at, 1)
        gate = jnp.concatenate(
            [jnp.broadcast_to(col(gates, i), (tokens, LANES)) for i in range(2)], axis=1
        )
        sig = sigmoid(pre)
        hidden = (pre * sig).astype(BF).astype(F32)
        part = hidden * grad
        total = gg[...]
        for i in range(2):
            each = jnp.sum(head(part, i), axis=1, keepdims=True)
            total = total + jnp.where(lane == at + i, each, 0.0)
        gg[...] = total
        hg[:, columns] = (gate * hidden).astype(BF)
        pg[:, columns] = (gate * grad * sig * (1.0 + pre * (1.0 - sig))).astype(BF)
        return carry

    lax.fori_loop(0, local // 2, pair, 0, unroll=2)
    for i, (src, dst) in enumerate(((hg, hg_ref), (pg, pg_ref)), 1):
        copies.append(pltpu.make_async_copy(src, dst.at[mine, :], sem_o.at[i]))
        copies[-1].start()
    piece = width // nd

    def blocks(columns):
        for j in range(X):
            for k in range(Z):
                at = pl.multiple_of(place_of(grid, idx, j, k) * rows, rows)
                from_refs[j][k, :, columns] = back[pl.ds(at, rows), : columns.size].astype(BF)

    for q in range(nd):
        columns = pl.ds(q * piece, piece)
        w = jnp.concatenate([up[e, columns, :] for e in range(local)], axis=1)
        back[:, :piece] = dot_nt(pg[...], w)
        blocks(columns)
    back[:, :EXPERTS] = gg[...]
    blocks(pl.ds(width, EXPERTS))
    wait_all(copies)


def out_kernel(grid, tags, micros, idx, hg_ref, *rest):
    nd, nt = grid.nd, len(tags)
    d_refs, (out_ref, hg, down, sem_g, sem_d) = rest[:nt], rest[nt:]
    local, width = down.shape[0], down.shape[2]
    group = hg.shape[0] // micros
    rows = group // grid.ne
    piece = width // nd
    get_d = fetch_experts(grid, idx, d_refs, tags, down, 2, sem_d)
    get_g = pltpu.make_async_copy(hg_ref, hg, sem_g.at[0])
    get_g.start()
    wait_all(get_d)
    get_g.wait()
    for q in range(nd):
        columns = pl.ds(q * piece, piece)
        back = dot(hg[...], down[:, :, columns].reshape(local * LANES, piece)).astype(BF)
        for e in range(grid.ne):
            for m in range(micros):
                at = m * group + e * rows
                out_ref[e, m * rows : (m + 1) * rows, columns] = back[at : at + rows]


def to_dp_place(grid, idx, k, r, piece):
    at = lax.rem(idx[0] + k, grid.Y) * grid.C + lax.rem(idx[1] + r, grid.C)
    return pl.ds(pl.multiple_of(at * piece, piece), piece)


def up_grad_kernel(grid, idx, x_ref, pg_ref, *rest):
    outs, acc = rest[:-1], rest[-1]
    acc[...] = dot_tn(x_ref[...], pg_ref[...])
    piece = outs[0].shape[2]
    for k, r in dp_tags(grid):
        rows = to_dp_place(grid, idx, k, r, piece)
        for e in range(outs[r].shape[1]):
            outs[r][k, e] = acc[rows, e * LANES : (e + 1) * LANES].astype(BF)


def down_grad_kernel(grid, idx, g_ref, hg_ref, *rest):
    outs, acc = rest[:-1], rest[-1]
    places, micros, rows, width = g_ref.shape
    g = jnp.concatenate([g_ref[:, m].reshape(places * rows, width) for m in range(micros)], axis=0)
    acc[...] = dot_tn(hg_ref[...], g)
    piece = outs[0].shape[3]
    for k, r in dp_tags(grid):
        columns = to_dp_place(grid, idx, k, r, piece)
        for e in range(outs[r].shape[1]):
            outs[r][k, e] = acc[e * LANES : (e + 1) * LANES, columns].astype(BF)


def fold_kernel(idx, own, *refs):
    Z = own.shape[0]
    others, out = refs[:-Z], refs[-Z:]
    del idx
    for k in range(Z):
        at = (Z - k) % Z
        total = own[at].astype(F32)
        for ref in others:
            total = total + ref[at].astype(F32)
        out[k][...] = total.astype(BF)


def fold_at_kernel(idx, own, *refs):
    Z = own.shape[0]
    others, out = refs[:-Z], refs[-Z:]
    for k in range(Z):
        at = lax.rem(idx[2] + k, Z)
        total = own[at].astype(F32)
        for ref in others:
            total = total + ref[at].astype(F32)
        out[k][...] = total.astype(BF)


def sum_kernel(*refs):
    total = refs[0][...].astype(F32)
    for ref in refs[1:-1]:
        total = total + ref[...].astype(F32)
    refs[-1][...] = total


def sum_places_kernel(parts, own, out):
    total = own[...]
    for z in range(parts.shape[0]):
        total = total + parts[z].astype(F32)
    out[...] = total


def back_norm_kernel(grid, micros, idx, wmr_ref, res_ref, g_ref, router_ref, picked_ref, *rest):
    nd, Z = grid.nd, grid.Z
    n = micros * Z
    rg_ref, bg_ref, late_ref = rest[n : n + 3]
    cols = rest[n + 3 :]
    width = res_ref.shape[1]
    parts = []
    for m in range(micros):
        total = rest[m * Z][...].astype(F32)
        for ref in rest[m * Z + 1 : (m + 1) * Z]:
            total = total + ref[...].astype(F32)
        parts.append(total)
    back = jnp.concatenate(parts, axis=0)
    router = router_ref[...]
    late = (back[:, width:] * picked_ref[...] * router * (1.0 - router)).astype(BF)
    late_ref[...] = late
    unit, inverse = norm_stats(res_ref[...])
    n2g = dot_nt(late, wmr_ref[:, LANES:])
    a = n2g * gain_row(wmr_ref[:, :LANES], LANE_GAIN_TWO)
    res_grad = g_ref[...].astype(F32) + back[:, :width] + norm_back(a, unit, inverse)
    rg_ref[...] = res_grad
    bg_ref[...] = res_grad.astype(BF)
    piece = width // nd
    for ref, (k, r) in zip(cols, dp_tags(grid)):
        at = lax.rem(idx[0] + k, grid.Y) * grid.C + lax.rem(idx[1] + r, grid.C)
        ref[...] = bg_ref[:, pl.ds(pl.multiple_of(at * piece, piece), piece)]


def back_attend_kernel(grid, tags, idx, bg_ref, rg_ref, sig_ref, mask_ref, early_ref, qk_ref, val_ref, va_ref,
                       pr_ref, *rest):
    n = len(tags)
    o_refs = rest[:n]
    late_ref, vag_ref, wo, sem_o = rest[n:]
    get_o = fetch_rows(grid, idx, o_refs, tags, wo, sem_o, COL_OUT)
    bg = bg_ref[...]
    tokens = bg.shape[0]
    sig, gate = sig_ref[...], early_ref[:, H * DH :]
    lane = lanes_of((tokens, LANES))
    logits = jnp.zeros((tokens, LANES), F32)
    wait_all(get_o)
    for h in range(H):
        att = early_ref[:, h * DH : (h + 1) * DH]
        mg = dot(bg, wo[:, h * EA * DH : (h + 1) * EA * DH])
        ag = jnp.zeros((tokens, DH), F32)
        for e in range(EA):
            i = HE + h * EA + e
            ag = ag + col(gate, i) * head(mg, e)
            each = jnp.sum(head(mg, e) * att, axis=1, keepdims=True)
            logits = jnp.where(lane == i, each, logits)
        ag = ag.astype(BF)
        prob = pr_ref[:, h * tokens : (h + 1) * tokens]
        vg = dot_tn(prob.astype(BF), ag)
        pgrad = dot_nt(ag, val_ref[:, h * DH : (h + 1) * DH])
        delta = jnp.sum(prob * pgrad, axis=-1, keepdims=True)
        sg = (prob * (pgrad - delta) * SCALE).astype(BF)
        late_ref[:, h * DH : (h + 1) * DH] = dot(
            sg, qk_ref[:, (H + h) * DH : (H + h + 1) * DH]
        ).astype(BF)
        late_ref[:, (H + h) * DH : (H + h + 1) * DH] = dot_tn(
            sg, qk_ref[:, h * DH : (h + 1) * DH]
        ).astype(BF)
        late_ref[:, COL_VG + h * DH : COL_VG + (h + 1) * DH] = vg.astype(BF)
        for e in range(EA):
            i = h * EA + e
            each = jnp.sum(va_ref[:, i * DH : (i + 1) * DH] * vg, axis=1, keepdims=True)
            logits = jnp.where(lane == i, each, logits)
            vag_ref[:, i * DH : (i + 1) * DH] = (col(gate, i) * vg).astype(BF)
    late_ref[:, COL_LG:COL_VG] = (logits * mask_ref[...] * sig * (1.0 - sig)).astype(BF)
    late_ref[:, COL_RG:] = rg_ref[...]


def back_token_kernel(grid, a_tags, idx, x_ref, rg_ref, late_ref, vag_ref, *rest):
    na = len(a_tags)
    a_refs = rest[:na]
    gt_ref, wa, wv, sem_a, sem_v = rest[na:]
    get_a = fetch_rows(grid, idx, a_refs, a_tags, wa, sem_a)
    get_v = fetch_rows(grid, idx, a_refs, a_tags, wv, sem_v, COL_VALUES)
    unit, inverse = norm_stats(x_ref[...].astype(F32))
    wait_all(get_a)
    n1g = dot_nt(late_ref[:, :COL_VG], wa[:, :COL_ROUTER])
    b = n1g * gain_row(wa[:, COL_SEL:COL_ROUTER], LANE_GAIN_ONE)
    wait_all(get_v)
    gt_ref[...] = rg_ref[...] + dot_nt(vag_ref[...], wv[...]) + norm_back(b, unit, inverse)


def stacked(refs, first=0, last=None):
    return jnp.concatenate([r[:, first:last] for r in refs], axis=0)


def in_order(grid, idx, ref, first=0, size=None):
    size = ref.shape[2] - first if size is None else size
    return jnp.concatenate(
        [ref[shard_at(grid, idx, k, r), :, pl.ds(first, size)] for k, r in dp_tags(grid)], axis=0
    )


def by_owner(grid, idx, out_refs, value, first=0):
    X, Z = grid.X, grid.Z
    mine = value.shape[0] // (X * Z)
    columns = pl.ds(first, value.shape[1])
    for z in range(Z):
        blocks = [value[(z * X + x) * mine : (z * X + x + 1) * mine] for x in range(X)]
        for j in range(X):
            chosen = blocks[0]
            for x in range(1, X):
                chosen = jnp.where(lax.rem(idx[3] + j, X) == x, blocks[x], chosen)
            out_refs[j][z, :, columns] = chosen.astype(BF)


def grad_out_kernel(grid, idx, early, *refs):
    nd = grid.nd
    bgs, out = refs[:nd], refs[nd:]
    wide = H * DH
    gate = in_order(grid, idx, early, wide)
    att = in_order(grid, idx, early, 0, wide)
    by_owner(grid, idx, out, dot_tn(stacked(bgs), mixed_of(gate, att, HE)))


def own_columns(grid, idx, cols, which):
    piece = cols.shape[2] // (3 * grid.nd)
    at = which * piece * grid.nd + shard_at(grid, idx, 0, 0) * piece
    return in_order(grid, idx, cols, pl.multiple_of(at, piece), piece)


def grad_rest_kernel(grid, idx, cols, early, a_ref, *refs):
    nd = grid.nd
    late, out = refs[:nd], refs[nd:]
    x, n1, n2 = [own_columns(grid, idx, cols, i) for i in range(3)]
    acts = stacked(late)
    both = dot_tn(n1, acts[:, :COL_VG])
    by_owner(grid, idx, out, both[:, :COL_SEL])
    misc = a_ref[:, COL_SEL:COL_ROUTER].astype(F32)
    stats = in_order(grid, idx, early, H * DH)
    unit = (x.astype(F32) - col(stats, LANE_MEAN)) * col(stats, LANE_INVERSE)
    n1_grad = dot_nt(acts[:, :COL_VG], a_ref[:, :COL_ROUTER])
    n2_grad = dot_nt(acts[:, COL_RG:], a_ref[:, COL_ROUTER:])
    one = jnp.sum(n1_grad * unit, axis=0, keepdims=True)
    gains = jnp.transpose(misc)[LANE_GAIN_TWO : LANE_GAIN_TWO + 1]
    two = jnp.sum(n2_grad * n2.astype(F32), axis=0, keepdims=True) / gains
    row = rows_of((LANES, one.shape[1]))
    extra = jnp.where(row == LANE_GAIN_ONE, one, 0.0)
    extra = jnp.where(row == LANE_GAIN_TWO, two, extra)
    by_owner(grid, idx, out, both[:, COL_SEL:] + jnp.transpose(extra), COL_SEL)
    by_owner(grid, idx, out, dot_tn(n2, acts[:, COL_RG:]), COL_ROUTER)
    mixed = mixed_of(stats, acts[:, COL_VG:COL_RG].astype(F32), 0)
    by_owner(grid, idx, out, dot_tn(x, mixed), COL_VALUES)


def finish_kernel(*refs):
    parts, (q, k, v, vs, os, router, one, two) = refs[:-8], refs[-8:]
    total = parts[0][...].astype(F32)
    for ref in parts[1:]:
        total = total + ref[...].astype(F32)
    wide = H * DH
    q[...] = total[:, :wide]
    k[...] = total[:, wide:COL_SEL]
    misc = total[:, COL_SEL:COL_ROUTER]
    turned = jnp.transpose(misc)
    vs[...] = turned[:HE]
    os[...] = turned[HE : 2 * HE]
    one[...] = turned[LANE_GAIN_ONE : LANE_GAIN_ONE + 1]
    two[...] = turned[LANE_GAIN_TWO : LANE_GAIN_TWO + 1]
    router[...] = total[:, COL_ROUTER:COL_VALUES]
    v[...] = total[:, COL_VALUES:]


def shape(dims, dtype):
    return jax.ShapeDtypeStruct(dims, dtype)


def call(name, kernel, operands, specs, outs, scratch=(), mib=58, us=5, aliases=None):
    outs = [o if isinstance(o, tuple) else (o, VMEM) for o in outs]
    operands = [
        o if s is SMEM else pltpu.with_memory_space_constraint(o, pltpu.HBM)
        for o, s in zip(operands, specs, strict=True)
    ]
    return pl.pallas_call(
        kernel,
        out_shape=tuple(pltpu.HBM(o[0].shape, o[0].dtype) for o in outs),
        in_specs=list(specs),
        out_specs=tuple(o[1] for o in outs),
        scratch_shapes=list(scratch),
        input_output_aliases=aliases or {},
        compiler_params=pltpu.CompilerParams(vmem_limit_bytes=mib * 1024 * 1024),
        cost_estimate=pl.CostEstimate(
            flops=us, bytes_accessed=us, transcendentals=0
        ),
        name=name,
    )(*operands)


def dma(n):
    return pltpu.SemaphoreType.DMA((n,))


def per_device(
    nd,
    ne,
    tokens,
    cotangent,
    segments,
    value_picks,
    output_picks,
    expert_picks,
    attn_gain,
    query_weight,
    key_weight,
    value_weight,
    output_expert_weight,
    value_select,
    output_select,
    moe_gain,
    router_weight,
    up_weight,
    down_weight,
):
    grid = Grid(nd, ne)
    X, Y, Z, C = grid.X, grid.Y, grid.Z, grid.C
    micros, length, width = tokens.shape
    rows = micros * length
    local = up_weight.shape[0]
    piece = width // nd
    wide = H * DH
    values_wide = HE * DH
    dp, ex = lax.axis_index("dp"), lax.axis_index("expert")
    idx = jnp.stack([dp // C, dp % C, ex // X, ex % X]).astype(jnp.int32)


    x_all = tokens.reshape(rows, width)
    g_all = cotangent.reshape(rows, width)

    ends = (*STARTS[1:], COL_A)
    block_w, block_a, *parts_a = call(
        "pack",
        functools.partial(pack_kernel, grid),
        (
            idx,
            query_weight,
            key_weight,
            value_select.T,
            output_select.T,
            attn_gain,
            moe_gain,
            router_weight,
            value_weight,
            output_expert_weight,
        ),
        [SMEM] + [VMEM] * 9,
        [shape((piece, COL_A), BF), shape((piece, COL_VALUES), BF)]
        + [shape((piece // X, high - low), BF) for low, high in zip(STARTS, ends)],
        [pltpu.VMEM((LANES, piece), F32)],
        us=3,
    )

    def to_y(v, *deps):
        v = after(v, *deps)
        return [grid.rot_y(v, k) for k in range(1, Y)]

    def over_x(got_y, *deps):
        return [[v] + [grid.rot_x(after(v, *deps), j) for j in range(1, X)] for v in got_y]

    def add_pieces(arrays, tags, v, tag, swapped=None):
        k, split, j, column = tag
        arrays.append(v)
        tags.append((k, 0, split, j, column))
        if C > 1:
            arrays.append(grid.swap(v) if swapped is None else swapped)
            tags.append((k, 1, split, j, column))

    def swap(v, *deps):
        return grid.swap(after(v, *deps)) if C > 1 else None

    def spread_x(got_y, *deps):
        return [[v] + [grid.rot_x(after(v, *deps), j) for j in range(1, X)] for v in got_y]

    def swap_all(values, *deps):
        return [swap(v, *deps) for v in values]

    def flat(by_k):
        return [v for by_j in by_k for v in by_j]

    g_gathered = lax.all_gather(g_all, "expert", axis=0, tiled=True)
    swap_w = swap(block_w)
    seg = segments.reshape(1, rows)
    v_picks, o_picks = value_picks.reshape(rows, 2 * H), output_picks.reshape(rows, 2 * H)
    e_picks = expert_picks.reshape(rows, -1)
    done = [swap_w, seg, v_picks, o_picks, e_picks]
    over_y, over_x_too, swap_y, swap_x = [to_y(parts_a[0])], [], [], []
    done.append(over_y[0])
    swap_d = swap_u = d_y = None
    for i in range(len(STARTS)):
        last_round = i == len(STARTS) - 1
        new = []
        if not last_round:
            over_y.append(to_y(parts_a[i + 1], *done))
            new += over_y[-1]
        else:
            d_y = to_y(down_weight, *done)
            swap_u = swap(up_weight, *done)
            new += [swap_u, g_gathered]
        if i == len(STARTS) - 2:
            swap_d = swap(down_weight, *done)
            new.append(swap_d)
        over_x_too.append(spread_x(over_y[i], *done))
        swap_y.append(swap_all(over_y[i], *done))
        new += flat(over_x_too[-1]) + swap_y[-1]
        if i:
            swap_x.append([swap_all(by_j[1:], *done) for by_j in over_x_too[i - 1]])
            new += flat(swap_x[-1])
        done = new
    def weight_pieces(own, swapped, chunks):
        arrays, tags = [own, swapped], [(0, 0, None, 0, 0), (0, 1, None, 0, 0)]
        for column, got, others in chunks:
            for k, (by_j, swaps) in enumerate(zip(got, others), 1):
                for j, (v, o) in enumerate(zip(by_j, swaps)):
                    split = "x" if len(by_j) > 1 else None
                    arrays += [v, o]
                    tags += [(k, 0, split, j, column), (k, 1, split, j, column)]
        return arrays, tags

    def all_chunks():
        return [
            (low, got, [[v] + more for v, more in zip(ys, xs)])
            for low, got, ys, xs in zip(STARTS, over_x_too, swap_y, swap_x)
        ]

    first_pieces, first_tags = weight_pieces(block_w, swap_w, all_chunks()[:1])

    n1, qk, sig, mask, probs, wmr = call(
        "attend",
        functools.partial(attend_kernel, grid, first_tags, length),
        (
            idx,
            x_all,
            seg,
            v_picks,
            o_picks,
            *first_pieces,
        ),
        [SMEM] + [VMEM] * 4 + [ANY] * len(first_pieces),
        [
            shape((rows, width), BF),
            shape((rows, 2 * wide), BF),
            shape((rows, LANES), F32),
            shape((rows, LANES), F32),
            shape((rows, H * rows), F32),
            shape((width, 2 * LANES), BF),
        ],
        [pltpu.VMEM((width, COL_VALUES), BF), dma(len(first_pieces))],
        us=4,
    )
    swap_x.append([swap_all(by_j[1:], n1, *done) for by_j in over_x_too[-1]])
    a_pieces, a_tags = weight_pieces(block_w, swap_w, all_chunks())
    v_pieces, v_tags = window(a_pieces, a_tags, COL_VALUES, COL_OUT)
    o_pieces, o_tags = window(a_pieces, a_tags, COL_OUT, COL_A)
    vals, va, early, res, router, picked, xg, cols = call(
        "route",
        functools.partial(route_kernel, grid, v_tags, o_tags),
        (idx, x_all, n1, sig, mask, probs, wmr, e_picks, *v_pieces, *o_pieces),
        [SMEM] + [VMEM] * 7 + [ANY] * (len(v_pieces) + len(o_pieces)),
        [
            shape((rows, wide), BF),
            shape((rows, values_wide), F32),
            shape((rows, wide + LANES), F32),
            shape((rows, width), F32),
            shape((rows, EXPERTS), F32),
            shape((rows, EXPERTS), F32),
            shape((rows, width + EXPERTS), BF),
            shape((rows, 3 * width), BF),
        ],
        [
            pltpu.VMEM((width, values_wide), BF),
            pltpu.VMEM((width, values_wide), BF),
            dma(len(v_pieces)),
            dma(len(o_pieces)),
        ],
        us=8,
    )

    group = ne * length
    ff = local * LANES
    swap_dy = swap_all(d_y, xg)
    u_y = to_y(up_weight, xg, *d_y)
    column, x_over, done = [xg], [], []
    for k in range(1, Z):
        held = after(column[-1], *done)
        column.append(grid.rot_z(held, 1))
        x_over.append([grid.rot_x(held, j) for j in range(1, X)])
        last_done, done = done, [column[-1], x_over[-1], *([u_y] if k == Z - 2 else [])]
    ring_done = done
    swap_uy = swap_all(u_y, *last_done)

    def expert_pieces(own, swapped, got, others):
        arrays, tags = [own, swapped], [(0, 0, 0), (0, 1, 0)]
        for k, (v, o) in enumerate(zip(got, others), 1):
            arrays += [v, o]
            tags += [(k, 0, 0), (k, 1, 0)]
        return arrays, tags

    d_pieces, d_tags = expert_pieces(down_weight, swap_d, d_y, swap_dy)
    u_pieces, u_tags = expert_pieces(up_weight, swap_u, u_y, swap_uy)
    g_rows = g_gathered.reshape(ne, micros, length, width)
    total = micros * group
    (ahead,) = call(
        "ahead",
        functools.partial(ahead_kernel, grid, d_tags),
        (idx, after(g_rows, *last_done), *d_pieces),
        [SMEM] + [ANY] * (1 + len(d_tags)),
        [(shape((total, ff), BF), ANY)],
        [
            pltpu.VMEM((ne, micros, length, width), BF),
            pltpu.VMEM((local, LANES, width), BF),
            pltpu.VMEM((total, ff), BF),
            dma(1),
            dma(len(d_tags)),
            dma(local // 2),
        ],
        us=9,
    )
    x_over.append([grid.rot_x(after(column[-1], ahead, *ring_done), j) for j in range(1, X)])
    x_pieces = column + [by_j[j] for j in range(X - 1) for by_j in x_over]
    froms = []

    def over_x(parts):
        return [grid.rot_x(parts[j], -j) for j in range(1, X)]

    def fold(parts, others, *deps):
        return call(
            "fold",
            fold_kernel,
            (idx, after(parts[0], *deps), *others),
            [SMEM] + [VMEM] * X,
            [shape(parts[0].shape[1:], BF)] * Z,
            us=2,
        )

    sent, shared = [], []
    for m in range(micros):
        hg, pg, x_group, *back = call(
            "experts",
            functools.partial(expert_kernel, grid, u_tags, m, micros),
            (idx, ahead, *x_pieces, *u_pieces, *shared),
            [SMEM, ANY] + [ANY] * (ne + len(u_tags) + len(shared)),
            [
                (shape((total, ff), BF), ANY),
                (shape((total, ff), BF), ANY),
                (shape((total, width + EXPERTS), BF), ANY),
                *[shape((Z, length, width + EXPERTS), BF)] * X,
            ],
            [
                pltpu.VMEM((group, ff), BF),
                pltpu.VMEM((group, ff), BF),
                pltpu.VMEM((group, width + EXPERTS), BF),
                pltpu.VMEM((group, ff), BF),
                pltpu.VMEM((local, width, LANES), BF),
                pltpu.VMEM((group, EXPERTS), F32),
                pltpu.VMEM((group, max(piece, EXPERTS)), F32),
                dma(ne),
                dma(len(u_tags)),
                dma(1),
                dma(3),
            ],
            us=12,
            aliases={2 + ne + len(u_tags) + i: i for i in range(len(shared))},
        )
        shared = [hg, pg, x_group]
        sent.append(back)

    def out_rows(*deps):
        return call(
            "out",
            functools.partial(out_kernel, grid, d_tags, micros),
            (idx, after(hg, *deps), *d_pieces),
            [SMEM] + [ANY] * (1 + len(d_tags)),
            [shape((ne, rows, width), BF)],
            [
                pltpu.VMEM((total, ff), BF),
                pltpu.VMEM((local, LANES, width), BF),
                dma(1),
                dma(len(d_tags)),
            ],
            us=10,
        )

    def expert_grad(name, kernel, lhs, rhs, dims, *deps):
        halves = 2
        block = pl.BlockSpec((Y, local // halves, *dims), lambda h, idx: (0, h, 0, 0))
        if lhs.ndim == 4:
            whole = pl.BlockSpec((ne, micros, length, width), lambda h, idx: (0, 0, 0, 0))
        else:
            whole = pl.BlockSpec((total, width), lambda h, idx: (0, 0))
        part = (width, ff // halves) if lhs.ndim == 2 else (ff // halves, width)
        return pl.pallas_call(
            functools.partial(kernel, grid),
            out_shape=[pltpu.HBM((Y, local, *dims), BF)] * C,
            grid_spec=pltpu.PrefetchScalarGridSpec(
                num_scalar_prefetch=1,
                grid=(halves,),
                in_specs=[whole, pl.BlockSpec((total, ff // halves), lambda h, idx: (0, h))],
                out_specs=[block] * C,
                scratch_shapes=[pltpu.VMEM(part, F32)],
            ),
            compiler_params=pltpu.CompilerParams(vmem_limit_bytes=58 * 1024 * 1024),
            cost_estimate=pl.CostEstimate(flops=4, bytes_accessed=12, transcendentals=0),
            name=name,
        )(idx, *[pltpu.with_memory_space_constraint(v, pltpu.HBM) for v in (after(lhs, *deps), rhs)])

    def added_blocks(name, arrays, dtype, split):
        steps = 2
        dims = arrays[0].shape[1:] if split else arrays[0].shape
        some = (dims[0] // steps, *dims[1:])
        one = pl.BlockSpec(some, lambda i: (i, 0, 0))
        spec = pl.BlockSpec((Y, *some), lambda i: (0, i, 0, 0)) if split else one
        results = Y if split else 1

        def kernel(*refs):
            for k, out in enumerate(refs[len(arrays) :]):
                total = 0.0
                for ref in refs[: len(arrays)]:
                    total = total + (ref[k] if split else ref[...]).astype(F32)
                out[...] = total.astype(dtype)

        return pl.pallas_call(
            kernel,
            out_shape=[pltpu.HBM(dims, dtype)] * results,
            grid=(steps,),
            in_specs=[spec] * len(arrays),
            out_specs=[one] * results,
            compiler_params=pltpu.CompilerParams(vmem_limit_bytes=58 * 1024 * 1024),
            cost_estimate=pl.CostEstimate(flops=1, bytes_accessed=3, transcendentals=0),
            name=name,
        )(*[pltpu.with_memory_space_constraint(v, pltpu.HBM) for v in arrays])

    down_args = ("down_grad", down_grad_kernel, g_rows, hg, (LANES, piece))
    up_args = ("up_grad", up_grad_kernel, x_group, pg, (piece, LANES))

    def reduce_y(total, *deps):
        got = [grid.rot_y(after(total[k], *deps), k) for k in range(1, Y)]
        return lambda *more: added_blocks("last_sum", [after(total[0], *more), *got], F32, False)[0], got

    from_x = [over_x(v) for v in sent]
    sums = fold(sent[0], from_x[0], hg)
    froms.append(grid.send_z(sums))
    outs_sent = out_rows(sums[0])
    before, down_came, up_came = outs_sent[0], [], []
    for m in range(1, micros):
        sums = fold(sent[m], from_x[m], before, froms[-1])
        froms.append(grid.send_z(sums))
        before = sums[0]
    down_near, *down_far = expert_grad(*down_args, before)
    up_near, *up_far = expert_grad(*up_args, down_near)
    before = up_near

    early_all = lax.all_gather(after(early, u_pieces), "dp", axis=0)
    cols_all = lax.all_gather(after(cols, u_pieces), "dp", axis=0)
    res_grad, bg, rg, *bg_cols = call(
        "back_norm",
        functools.partial(back_norm_kernel, grid, micros),
        (
            idx,
            wmr,
            res,
            g_all,
            after(router, before, early_all, cols_all),
            picked,
            *[p for f in froms for p in f],
        ),
        [SMEM] + [VMEM] * (5 + micros * Z),
        [
            shape((rows, width), F32),
            shape((rows, width), BF),
            shape((rows, EXPERTS), BF),
            *[shape((rows, piece), BF)] * nd,
        ],
        us=3,
    )
    bgs = [v if t == (0, 0) else grid.rot_yc(v, *t) for v, t in zip(bg_cols, dp_tags(grid))]
    late, vag = call(
        "back_attend",
        functools.partial(back_attend_kernel, grid, o_tags),
        (idx, bg, rg, sig, mask, early, qk, vals, va, probs, *o_pieces),
        [SMEM] + [VMEM] * 9 + [ANY] * len(o_pieces),
        [shape((rows, COL_LATE), BF), shape((rows, values_wide), BF)],
        [pltpu.VMEM((width, values_wide), BF), dma(len(o_pieces))],
        us=8,
    )
    outs = lax.all_to_all(after(outs_sent[0], bg), "expert", 0, 0, tiled=True)
    down_came, up_came = swap_all(down_far, bg), swap_all(up_far, bg)
    late_swap = swap(late, bgs[1:], *down_came, *up_came)
    late_y = to_y(late, bgs[1:])

    mine = piece // ne

    def weight_grad(name, kernel, operands, columns):
        parts = call(
            name,
            functools.partial(kernel, grid),
            (idx, *operands),
            [SMEM] + [VMEM] * len(operands),
            [shape((Z, mine, columns), BF)] * X,
            us=3,
        )
        return parts, [grid.rot_x(parts[j], j) for j in range(1, X)]

    def fold_at(parts, others, *deps):
        sums = call(
            "fold_at",
            fold_at_kernel,
            (idx, after(parts[0], *deps), *others),
            [SMEM] + [VMEM] * X,
            [shape(parts[0].shape[1:], BF)] * Z,
            us=1,
        )
        return sums[0], grid.send_z(sums)

    def added(parts, *deps):
        return call(
            "sum",
            sum_kernel,
            (after(parts[0], *deps), *parts[1:]),
            [VMEM] * len(parts),
            [shape(parts[0].shape, F32)],
            us=1,
        )[0]

    down_sum = added_blocks("core_sum", [after(down_near, late), *down_came], BF, True)
    up_sum = added_blocks("core_sum", [after(up_near, down_sum), *up_came], BF, True)
    o_parts, o_others = weight_grad(
        "grad_out", grad_out_kernel, [after(early_all, up_sum), *bgs], values_wide
    )
    down_last, down_got = reduce_y(down_sum, late_y)
    up_last, up_got = reduce_y(up_sum, late_y)
    late_all = [late, *late_y, late_swap, *swap_all(late_y, o_parts[0])]
    r_parts, r_others = weight_grad(
        "grad_rest",
        grad_rest_kernel,
        [after(cols_all, o_parts[0]), early_all, block_a, *late_all],
        COL_OUT,
    )
    o_fold, o_sums = fold_at(o_parts, o_others, r_parts[0])
    r_fold, r_sums = fold_at(r_parts, r_others, o_sums, outs)
    grad_down = down_last(r_fold)
    grad_up = up_last(grad_down)
    (grad_tokens,) = call(
        "back_token",
        functools.partial(back_token_kernel, grid, a_tags),
        (idx, x_all, res_grad, after(late, r_fold), vag, *a_pieces),
        [SMEM] + [VMEM] * 4 + [ANY] * len(a_pieces),
        [shape((rows, width), F32)],
        [
            pltpu.VMEM((width, COL_VALUES), BF),
            pltpu.VMEM((width, values_wide), BF),
            dma(len(a_pieces)),
            dma(len(a_pieces)),
        ],
        us=8,
    )
    (output,) = call(
        "add_out",
        sum_places_kernel,
        (outs, after(res, grad_tokens)),
        [VMEM] * 2,
        [shape((rows, width), F32)],
        us=2,
    )
    grad_output = added(o_sums, output)
    q, k, grad_value, vs, os, r, one, two = call(
        "finish",
        finish_kernel,
        (after(r_sums[0], grad_tokens, output, grad_output, grad_up), *r_sums[1:]),
        [VMEM] * Z,
        [
            shape((mine, wide), F32),
            shape((mine, wide), F32),
            shape((mine, values_wide), F32),
            shape((HE, mine), F32),
            shape((HE, mine), F32),
            shape((mine, EXPERTS), F32),
            shape((1, mine), F32),
            shape((1, mine), F32),
        ],
        us=1,
    )
    return (
        output.reshape(micros, length, width),
        grad_tokens.reshape(micros, length, width),
        one.reshape(mine),
        q,
        k,
        grad_value,
        grad_output,
        vs.T,
        os.T,
        two.reshape(mine),
        r,
        grad_up,
        grad_down,
    )


def solution(mesh):
    rows = ("dp", "expert")
    placed = (
        P(None, rows, None),
        P(None, rows, None),
        P(None, rows, None),
        P(None, rows, None, None),
        P(None, rows, None, None),
        P(None, rows, None),
        P("dp"),
        P("dp", None),
        P("dp", None),
        P("dp", None),
        P("dp", None),
        P("dp", None),
        P("dp", None),
        P("dp"),
        P("dp", None),
        P("expert", "dp", None),
        P("expert", None, "dp"),
    )
    return jax.shard_map(
        functools.partial(per_device, mesh.shape["dp"], mesh.shape["expert"]),
        mesh=mesh,
        in_specs=placed,
        out_specs=(
            P(None, rows, None),
            P(None, rows, None),
            P(rows),
            P(rows, None),
            P(rows, None),
            P(rows, None),
            P(rows, None),
            P(rows, None),
            P(rows, None),
            P(rows),
            P(rows, None),
            P("expert", "dp", None),
            P("expert", None, "dp"),
        ),
        check_vma=False,
    )
```

```python
import functools

import jax
import jax.numpy as jnp
from jax import lax
from jax.experimental import pallas as pl
from jax.experimental.pallas import tpu as pltpu
from jax.sharding import PartitionSpec as P

H = 4
DH = 128
EA = 5
HE = H * EA
EXPERTS = 128
EPSILON = 1e-05
MASKED = -1e30
SCALE = DH ** (-0.5)
LANES = 128

BF = jnp.bfloat16
F32 = jnp.float32

COL_SEL = 2 * H * DH
COL_ROUTER = COL_SEL + LANES
COL_VALUES = COL_ROUTER + LANES
COL_OUT = COL_VALUES + HE * DH
COL_A = COL_OUT + HE * DH
STARTS = (0, 17 * LANES, 34 * LANES)
LANE_GAIN_ONE = 2 * HE
LANE_GAIN_TWO = 2 * HE + 1
LANE_MEAN = 2 * HE
LANE_INVERSE = 2 * HE + 1
COL_LG = 2 * H * DH
COL_VG = COL_LG + LANES
COL_RG = COL_VG + H * DH
COL_LATE = COL_RG + LANES

VMEM = pl.BlockSpec()
SMEM = pl.BlockSpec(memory_space=pltpu.SMEM)
ANY = pl.BlockSpec(memory_space=pltpu.HBM)


def dot(a, b):
    return jnp.dot(a, b, preferred_element_type=F32)


def dot_nt(a, b):
    return lax.dot_general(a, b, (((1,), (1,)), ((), ())), preferred_element_type=F32)


def dot_tn(a, b):
    return lax.dot_general(a, b, (((0,), (0,)), ((), ())), preferred_element_type=F32)


def sigmoid(v):
    return 1.0 / (1.0 + jnp.exp(-v))


class Grid:
    def __init__(self, nd, ne):
        self.nd, self.ne = nd, ne
        self.C = 2 if nd % 2 == 0 else 1
        self.Y = nd // self.C
        x = 1
        while (2 * x) * (2 * x) <= ne and ne % (2 * x) == 0:
            x *= 2
        self.X, self.Z = x, ne // x

    def _dp(self, v, go):
        C = self.C
        pairs = []
        for i in range(self.nd):
            y, c = go(i // C, i % C)
            pairs.append((i, y * C + c))
        return lax.ppermute(v, "dp", pairs)

    def _ex(self, v, go):
        X = self.X
        pairs = []
        for i in range(self.ne):
            z, x = go(i // X, i % X)
            pairs.append((i, z * X + x))
        return lax.ppermute(v, "expert", pairs)

    def rot_y(self, v, k):
        return self._dp(v, lambda y, c: ((y + k) % self.Y, c))

    def swap(self, v):
        return self._dp(v, lambda y, c: (y, c ^ 1))

    def rot_yc(self, v, k, r):
        return self._dp(v, lambda y, c: ((y + k) % self.Y, c ^ r))

    def rot_x(self, v, j):
        return self._ex(v, lambda z, x: (z, (x + j) % self.X))

    def rot_z(self, v, k):
        return self._ex(v, lambda z, x: ((z + k) % self.Z, x))

    def lines_z(self):
        return [[z * self.X + x for z in range(self.Z)] for x in range(self.X)]

    def gather_z(self, v):
        return lax.all_gather(v, "expert", axis=0, tiled=True, axis_index_groups=self.lines_z())

    def swap_z(self, v):
        return lax.all_to_all(v, "expert", 0, 0, tiled=True, axis_index_groups=self.lines_z())

    def send_z(self, parts):
        return [parts[0]] + [self.rot_z(parts[k], k) for k in range(1, self.Z)]

    def swap_dp(self, v):
        return lax.all_to_all(v, "dp", 0, 0, tiled=True)


def after(v, *deps):
    flat = [d for dep in deps for d in (dep if isinstance(dep, (list, tuple)) else [dep])]
    if not flat:
        return v
    return lax.optimization_barrier((v, *flat))[0]


def gather_dp(grid, w, over_y, swapped=None):
    got = [w] + list(over_y)
    if grid.C > 1:
        got = got + [grid.swap(w) if swapped is None else swapped] + [grid.swap(v) for v in over_y]
    return got


def dp_tags(grid):
    return [(k, r) for r in range(grid.C) for k in range(grid.Y)]


def shard_at(grid, idx, k, r):
    return lax.rem(idx[0] + (grid.Y - k), grid.Y) * grid.C + lax.rem(idx[1] + r, grid.C)


def fetch_rows(grid, idx, refs, tags, dst, sems, first=0):
    copies = []
    width, last = dst.shape[0] // grid.nd, first + dst.shape[1]
    for i, (ref, (k, r, split, j, column)) in enumerate(zip(refs, tags)):
        low, high = max(first, column), min(last, column + ref.shape[1])
        if low >= high:
            continue
        at = shard_at(grid, idx, k, r) * width
        n = width
        if split is not None:
            size, mine = (grid.X, idx[3]) if split == "x" else (grid.Z, idx[2])
            n = width // size
            at = at + lax.rem(mine + (size - j), size) * n
        at = pl.multiple_of(at, n)
        copy = pltpu.make_async_copy(
            ref.at[:, pl.ds(low - column, high - low)],
            dst.at[pl.ds(at, n), pl.ds(low - first, high - low)],
            sems.at[i],
        )
        copy.start()
        copies.append(copy)
    return copies


def fetch_experts(grid, idx, refs, tags, dst, axis, sems):
    copies = []
    n = dst.shape[axis] // grid.nd
    for i, (ref, (k, r, first)) in enumerate(zip(refs, tags)):
        at = pl.ds(pl.multiple_of(shard_at(grid, idx, k, r) * n, n), n)
        held = pl.ds(first, ref.shape[0])
        place = dst.at[held, at, :] if axis == 1 else dst.at[held, :, at]
        copy = pltpu.make_async_copy(ref, place, sems.at[i])
        copy.start()
        copies.append(copy)
    return copies


def wait_all(copies):
    for copy in copies:
        copy.wait()


def lanes_of(dims):
    return lax.broadcasted_iota(jnp.int32, dims, 1)


def rows_of(dims):
    return lax.broadcasted_iota(jnp.int32, dims, 0)


def norm_stats(v):
    centered = v - jnp.mean(v, axis=-1, keepdims=True)
    inverse = lax.rsqrt(jnp.mean(centered * centered, axis=-1, keepdims=True) + EPSILON)
    return centered * inverse, inverse


def window(pieces, tags, low, high):
    held = [(p, t) for p, t in zip(pieces, tags) if t[4] < high and t[4] + p.shape[1] > low]
    return [p for p, _ in held], [t for _, t in held]


def norm_back(grad, unit, inverse):
    return inverse * (
        grad
        - jnp.mean(grad, axis=-1, keepdims=True)
        - unit * jnp.mean(grad * unit, axis=-1, keepdims=True)
    )


def gain_row(block, lane):
    return jnp.transpose(block.astype(F32))[lane : lane + 1, :]


def col(v, i):
    return v[:, i : i + 1]


def head(v, i):
    return v[:, i * DH : (i + 1) * DH]


def mixed_of(gate, vectors, first):
    return jnp.concatenate(
        [
            (col(gate, first + h * EA + e) * head(vectors, h)).astype(BF)
            for h in range(H)
            for e in range(EA)
        ],
        axis=1,
    )


def pack_kernel(grid, idx, q, k, vs, os, gain_one, gain_two, router, v_ref, o_ref, w_ref, a_ref, *rest):
    parts, misc = rest[:-1], rest[-1]
    piece = q.shape[0]
    nx = piece // grid.X
    at_x = pl.ds(pl.multiple_of(idx[3] * nx, nx), nx)
    misc[...] = jnp.zeros_like(misc)
    misc[:HE, :] = vs[...].astype(F32)
    misc[HE : 2 * HE, :] = os[...].astype(F32)
    misc[LANE_GAIN_ONE : LANE_GAIN_ONE + 1, :] = gain_one[...].astype(F32).reshape(1, piece)
    misc[LANE_GAIN_TWO : LANE_GAIN_TWO + 1, :] = gain_two[...].astype(F32).reshape(1, piece)
    wide = H * DH
    a_ref[:, :wide] = q[...]
    a_ref[:, wide:COL_SEL] = k[...]
    a_ref[:, COL_SEL:COL_ROUTER] = jnp.transpose(misc[...]).astype(BF)
    a_ref[:, COL_ROUTER:] = router[...]
    w_ref[:, :COL_VALUES] = a_ref[...]
    w_ref[:, COL_VALUES:COL_OUT] = v_ref[...]
    w_ref[:, COL_OUT:] = o_ref[...]
    for part, low in zip(parts, STARTS):
        part[...] = w_ref[at_x, low : low + part.shape[1]]


def attend_kernel(grid, tags, length, idx, x_ref, seg_ref, vp, op, *rest):
    n = len(tags)
    a_refs = rest[:n]
    n1_ref, qk_ref, sig_ref, mask_ref, pr_ref, wmr_ref, wa, sem_a = rest[n:]
    get_a = fetch_rows(grid, idx, a_refs, tags, wa, sem_a)
    unit, _ = norm_stats(x_ref[...].astype(F32))
    tokens = unit.shape[0]
    lane = lanes_of((tokens, LANES))
    mask = jnp.zeros((tokens, LANES), F32)
    for h in range(H):
        for k in range(2):
            mask = mask + (lane == col(vp, 2 * h + k) + EA * h).astype(F32)
            mask = mask + (lane == col(op, 2 * h + k) + (EA * h + HE)).astype(F32)
    mask_ref[...] = mask
    square = (tokens, tokens)
    row, lane = rows_of(square), lanes_of(square)
    seg = jnp.broadcast_to(seg_ref[...].astype(F32), square)
    allowed = (seg == jnp.transpose(seg)) & (lane <= row) & (lane // length == row // length)
    wait_all(get_a)
    n1 = (unit * gain_row(wa[:, COL_SEL:COL_ROUTER], LANE_GAIN_ONE)).astype(BF)
    n1_ref[...] = n1
    qks = dot(n1, wa[:, :COL_ROUTER])
    qk = qks[:, :COL_SEL].astype(BF)
    qk_ref[...] = qk
    sig_ref[...] = sigmoid(qks[:, COL_SEL:])
    wmr_ref[...] = wa[:, COL_SEL:]
    for h in range(H):
        scores = dot_nt(head(qk, h), head(qk, H + h))
        scaled = jnp.where(allowed, scores * SCALE, MASKED)
        top = jnp.max(scaled, axis=-1, keepdims=True)
        expo = jnp.where(allowed, jnp.exp(scaled - top), 0.0)
        pr_ref[:, h * tokens : (h + 1) * tokens] = expo / jnp.sum(expo, axis=-1, keepdims=True)


def route_kernel(grid, v_tags, o_tags, idx, x_ref, n1_ref, sig_ref, mask_ref, pr_ref, wmr_ref, ep, *rest):
    nv, no = len(v_tags), len(o_tags)
    v_refs, o_refs = rest[:nv], rest[nv : nv + no]
    rest = rest[nv + no :]
    val_ref, va_ref, early_ref, res_ref, router_ref, picked_ref = rest[:6]
    xg_ref, col_ref, wv, wo, sem_v, sem_o = rest[6:]
    get_v = fetch_rows(grid, idx, v_refs, v_tags, wv, sem_v, COL_VALUES)
    get_o = fetch_rows(grid, idx, o_refs, o_tags, wo, sem_o, COL_OUT)
    gate = sig_ref[...] * mask_ref[...]
    tokens, width = x_ref.shape
    lane = lanes_of((tokens, EXPERTS))
    picked = jnp.zeros((tokens, EXPERTS), F32)
    for k in range(ep.shape[1]):
        picked = picked + (lane == col(ep, k)).astype(F32)
    picked_ref[...] = picked
    x_bf = x_ref[...]
    wait_all(get_v)
    atts = []
    for h in range(H):
        va = dot(x_bf, wv[:, h * EA * DH : (h + 1) * EA * DH])
        va_ref[:, h * EA * DH : (h + 1) * EA * DH] = va
        total = col(gate, h * EA) * head(va, 0)
        for e in range(1, EA):
            total = total + col(gate, h * EA + e) * head(va, e)
        value = total.astype(BF)
        val_ref[:, h * DH : (h + 1) * DH] = value
        atts.append(dot(pr_ref[:, h * tokens : (h + 1) * tokens].astype(BF), value))
    att = jnp.concatenate(atts, axis=1)
    early_ref[:, : H * DH] = att
    mean = jnp.mean(x_bf.astype(F32), axis=-1, keepdims=True)
    centered = x_bf.astype(F32) - mean
    inverse = lax.rsqrt(jnp.mean(centered * centered, axis=-1, keepdims=True) + EPSILON)
    lane = lanes_of((tokens, LANES))
    early_ref[:, H * DH :] = jnp.where(
        lane == LANE_MEAN, mean, jnp.where(lane == LANE_INVERSE, inverse, gate)
    )
    mixed = mixed_of(gate, att, HE)
    wait_all(get_o)
    res = x_bf.astype(F32) + dot_nt(mixed, wo[...])
    res_ref[...] = res
    unit, _ = norm_stats(res)
    n2 = (unit * gain_row(wmr_ref[:, :LANES], LANE_GAIN_TWO)).astype(BF)
    router = sigmoid(dot(n2, wmr_ref[:, LANES:]))
    router_ref[...] = router
    xg_ref[:, :width] = res.astype(BF)
    xg_ref[:, width:] = (router * picked).astype(BF)
    col_ref[:, :width] = x_bf
    col_ref[:, width : 2 * width] = n1_ref[...]
    col_ref[:, 2 * width :] = n2


def ahead_kernel(grid, tags, idx, g_ref, *rest):
    d_refs, (gh_ref, g, down, gh, sem_g, sem_d, sem_o) = rest[: len(tags)], rest[len(tags) :]
    local, width = down.shape[0], down.shape[2]
    micros = g.shape[1]
    get_g = pltpu.make_async_copy(g_ref, g, sem_g.at[0])
    get_g.start()
    get_d = fetch_experts(grid, idx, d_refs, tags, down, 2, sem_d)
    get_g.wait()
    wait_all(get_d)
    group = g.shape[0] * g.shape[2]
    copies = []
    for p in range(local // 2):
        d2 = down[2 * p : 2 * p + 2].reshape(2 * LANES, width)
        columns = pl.ds(p * 2 * LANES, 2 * LANES)
        for m in range(micros):
            gh[m * group : (m + 1) * group, columns] = dot_nt(g[:, m].reshape(group, width), d2).astype(BF)
        copies.append(pltpu.make_async_copy(gh.at[:, columns], gh_ref.at[:, columns], sem_o.at[p]))
        copies[-1].start()
    wait_all(copies)


def place_of(grid, idx, j, k):
    return lax.rem(idx[2] + (grid.Z - k), grid.Z) * grid.X + lax.rem(idx[3] + (grid.X - j), grid.X)


def expert_kernel(grid, tags, micro, micros, idx, gh_ref, *rest):
    n, X, Z, nd, nt = grid.ne, grid.X, grid.Z, grid.nd, len(tags)
    x_refs, u_refs = rest[:n], rest[n : n + nt]
    rest = rest[n + nt + (3 if micro else 0) :]
    hg_ref, pg_ref, xg_ref = rest[:3]
    from_refs = rest[3 : 3 + X]
    hg, pg, xg, gh, up, gg, back, sem_x, sem_u, sem_g, sem_o = rest[3 + X :]
    local, width = up.shape[0], up.shape[1]
    tokens = xg.shape[0]
    rows = tokens // n
    mine = pl.ds(micro * tokens, tokens)
    get_x = []
    for j in range(X):
        for k in range(Z):
            at = pl.multiple_of(place_of(grid, idx, j, k) * rows, rows)
            i = j * Z + k
            get_x.append(
                pltpu.make_async_copy(
                    x_refs[i].at[pl.ds(micro * rows, rows), :], xg.at[pl.ds(at, rows), :], sem_x.at[i]
                )
            )
            get_x[-1].start()
    get_u = fetch_experts(grid, idx, u_refs, tags, up, 1, sem_u)
    get_g = pltpu.make_async_copy(gh_ref.at[mine, :], gh, sem_g.at[0])
    get_g.start()
    first = (idx[2] * X + idx[3]) * local
    gg[...] = jnp.zeros_like(gg)
    lane = lanes_of((tokens, EXPERTS))
    wait_all(get_x)
    copies = [pltpu.make_async_copy(xg, xg_ref.at[mine, :], sem_o.at[0])]
    copies[0].start()
    wait_all(get_u)
    get_g.wait()

    def pair(p, carry):
        w2 = jnp.concatenate([up[2 * p], up[2 * p + 1]], axis=1)
        pre = dot(xg[:, :width], w2)
        columns = pl.ds(pl.multiple_of(p * 2 * LANES, 2 * LANES), 2 * LANES)
        grad = gh[:, columns].astype(F32)
        at = first + 2 * p
        gates = pltpu.roll(xg[:, width:].astype(F32), EXPERTS - at, 1)
        gate = jnp.concatenate(
            [jnp.broadcast_to(col(gates, i), (tokens, LANES)) for i in range(2)], axis=1
        )
        sig = sigmoid(pre)
        hidden = (pre * sig).astype(BF).astype(F32)
        part = hidden * grad
        total = gg[...]
        for i in range(2):
            each = jnp.sum(head(part, i), axis=1, keepdims=True)
            total = total + jnp.where(lane == at + i, each, 0.0)
        gg[...] = total
        hg[:, columns] = (gate * hidden).astype(BF)
        pg[:, columns] = (gate * grad * sig * (1.0 + pre * (1.0 - sig))).astype(BF)
        return carry

    lax.fori_loop(0, local // 2, pair, 0, unroll=2)
    for i, (src, dst) in enumerate(((hg, hg_ref), (pg, pg_ref)), 1):
        copies.append(pltpu.make_async_copy(src, dst.at[mine, :], sem_o.at[i]))
        copies[-1].start()
    piece = width // nd

    def blocks(columns):
        for j in range(X):
            for k in range(Z):
                at = pl.multiple_of(place_of(grid, idx, j, k) * rows, rows)
                from_refs[j][k, :, columns] = back[pl.ds(at, rows), : columns.size].astype(BF)

    for q in range(nd):
        columns = pl.ds(q * piece, piece)
        w = jnp.concatenate([up[e, columns, :] for e in range(local)], axis=1)
        back[:, :piece] = dot_nt(pg[...], w)
        blocks(columns)
    back[:, :EXPERTS] = gg[...]
    blocks(pl.ds(width, EXPERTS))
    wait_all(copies)


def out_kernel(grid, tags, micros, idx, hg_ref, *rest):
    nd, nt = grid.nd, len(tags)
    d_refs, (out_ref, hg, down, sem_g, sem_d) = rest[:nt], rest[nt:]
    local, width = down.shape[0], down.shape[2]
    group = hg.shape[0] // micros
    rows = group // grid.ne
    piece = width // nd
    get_d = fetch_experts(grid, idx, d_refs, tags, down, 2, sem_d)
    get_g = pltpu.make_async_copy(hg_ref, hg, sem_g.at[0])
    get_g.start()
    wait_all(get_d)
    get_g.wait()
    for q in range(nd):
        columns = pl.ds(q * piece, piece)
        back = dot(hg[...], down[:, :, columns].reshape(local * LANES, piece)).astype(BF)
        for e in range(grid.ne):
            for m in range(micros):
                at = m * group + e * rows
                out_ref[e, m * rows : (m + 1) * rows, columns] = back[at : at + rows]


def to_dp_place(grid, idx, k, r, piece):
    at = lax.rem(idx[0] + k, grid.Y) * grid.C + lax.rem(idx[1] + r, grid.C)
    return pl.ds(pl.multiple_of(at * piece, piece), piece)


def up_grad_kernel(grid, idx, x_ref, pg_ref, *rest):
    outs, acc = rest[:-1], rest[-1]
    acc[...] = dot_tn(x_ref[...], pg_ref[...])
    piece = outs[0].shape[2]
    for k, r in dp_tags(grid):
        rows = to_dp_place(grid, idx, k, r, piece)
        for e in range(outs[r].shape[1]):
            outs[r][k, e] = acc[rows, e * LANES : (e + 1) * LANES].astype(BF)


def down_grad_kernel(grid, idx, g_ref, hg_ref, *rest):
    outs, acc = rest[:-1], rest[-1]
    places, micros, rows, width = g_ref.shape
    g = jnp.concatenate([g_ref[:, m].reshape(places * rows, width) for m in range(micros)], axis=0)
    acc[...] = dot_tn(hg_ref[...], g)
    piece = outs[0].shape[3]
    for k, r in dp_tags(grid):
        columns = to_dp_place(grid, idx, k, r, piece)
        for e in range(outs[r].shape[1]):
            outs[r][k, e] = acc[e * LANES : (e + 1) * LANES, columns].astype(BF)


def fold_kernel(idx, own, *refs):
    Z = own.shape[0]
    others, out = refs[:-Z], refs[-Z:]
    del idx
    for k in range(Z):
        at = (Z - k) % Z
        total = own[at].astype(F32)
        for ref in others:
            total = total + ref[at].astype(F32)
        out[k][...] = total.astype(BF)


def fold_at_kernel(idx, own, *refs):
    Z = own.shape[0]
    others, out = refs[:-Z], refs[-Z:]
    for k in range(Z):
        at = lax.rem(idx[2] + k, Z)
        total = own[at].astype(F32)
        for ref in others:
            total = total + ref[at].astype(F32)
        out[k][...] = total.astype(BF)


def sum_kernel(*refs):
    total = refs[0][...].astype(F32)
    for ref in refs[1:-1]:
        total = total + ref[...].astype(F32)
    refs[-1][...] = total


def sum_places_kernel(parts, own, out):
    total = own[...]
    for z in range(parts.shape[0]):
        total = total + parts[z].astype(F32)
    out[...] = total


def back_norm_kernel(grid, micros, idx, wmr_ref, res_ref, g_ref, router_ref, picked_ref, *rest):
    nd, Z = grid.nd, grid.Z
    n = micros * Z
    rg_ref, bg_ref, late_ref = rest[n : n + 3]
    cols = rest[n + 3 :]
    width = res_ref.shape[1]
    parts = []
    for m in range(micros):
        total = rest[m * Z][...].astype(F32)
        for ref in rest[m * Z + 1 : (m + 1) * Z]:
            total = total + ref[...].astype(F32)
        parts.append(total)
    back = jnp.concatenate(parts, axis=0)
    router = router_ref[...]
    late = (back[:, width:] * picked_ref[...] * router * (1.0 - router)).astype(BF)
    late_ref[...] = late
    unit, inverse = norm_stats(res_ref[...])
    n2g = dot_nt(late, wmr_ref[:, LANES:])
    a = n2g * gain_row(wmr_ref[:, :LANES], LANE_GAIN_TWO)
    res_grad = g_ref[...].astype(F32) + back[:, :width] + norm_back(a, unit, inverse)
    rg_ref[...] = res_grad
    bg_ref[...] = res_grad.astype(BF)
    piece = width // nd
    for ref, (k, r) in zip(cols, dp_tags(grid)):
        at = lax.rem(idx[0] + k, grid.Y) * grid.C + lax.rem(idx[1] + r, grid.C)
        ref[...] = bg_ref[:, pl.ds(pl.multiple_of(at * piece, piece), piece)]


def back_attend_kernel(grid, tags, idx, bg_ref, rg_ref, sig_ref, mask_ref, early_ref, qk_ref, val_ref, va_ref,
                       pr_ref, *rest):
    n = len(tags)
    o_refs = rest[:n]
    late_ref, vag_ref, wo, sem_o = rest[n:]
    get_o = fetch_rows(grid, idx, o_refs, tags, wo, sem_o, COL_OUT)
    bg = bg_ref[...]
    tokens = bg.shape[0]
    sig, gate = sig_ref[...], early_ref[:, H * DH :]
    lane = lanes_of((tokens, LANES))
    logits = jnp.zeros((tokens, LANES), F32)
    wait_all(get_o)
    for h in range(H):
        att = early_ref[:, h * DH : (h + 1) * DH]
        mg = dot(bg, wo[:, h * EA * DH : (h + 1) * EA * DH])
        ag = jnp.zeros((tokens, DH), F32)
        for e in range(EA):
            i = HE + h * EA + e
            ag = ag + col(gate, i) * head(mg, e)
            each = jnp.sum(head(mg, e) * att, axis=1, keepdims=True)
            logits = jnp.where(lane == i, each, logits)
        ag = ag.astype(BF)
        prob = pr_ref[:, h * tokens : (h + 1) * tokens]
        vg = dot_tn(prob.astype(BF), ag)
        pgrad = dot_nt(ag, val_ref[:, h * DH : (h + 1) * DH])
        delta = jnp.sum(prob * pgrad, axis=-1, keepdims=True)
        sg = (prob * (pgrad - delta) * SCALE).astype(BF)
        late_ref[:, h * DH : (h + 1) * DH] = dot(
            sg, qk_ref[:, (H + h) * DH : (H + h + 1) * DH]
        ).astype(BF)
        late_ref[:, (H + h) * DH : (H + h + 1) * DH] = dot_tn(
            sg, qk_ref[:, h * DH : (h + 1) * DH]
        ).astype(BF)
        late_ref[:, COL_VG + h * DH : COL_VG + (h + 1) * DH] = vg.astype(BF)
        for e in range(EA):
            i = h * EA + e
            each = jnp.sum(va_ref[:, i * DH : (i + 1) * DH] * vg, axis=1, keepdims=True)
            logits = jnp.where(lane == i, each, logits)
            vag_ref[:, i * DH : (i + 1) * DH] = (col(gate, i) * vg).astype(BF)
    late_ref[:, COL_LG:COL_VG] = (logits * mask_ref[...] * sig * (1.0 - sig)).astype(BF)
    late_ref[:, COL_RG:] = rg_ref[...]


def back_token_kernel(grid, a_tags, idx, x_ref, rg_ref, late_ref, vag_ref, *rest):
    na = len(a_tags)
    a_refs = rest[:na]
    gt_ref, wa, wv, sem_a, sem_v = rest[na:]
    get_a = fetch_rows(grid, idx, a_refs, a_tags, wa, sem_a)
    get_v = fetch_rows(grid, idx, a_refs, a_tags, wv, sem_v, COL_VALUES)
    unit, inverse = norm_stats(x_ref[...].astype(F32))
    wait_all(get_a)
    n1g = dot_nt(late_ref[:, :COL_VG], wa[:, :COL_ROUTER])
    b = n1g * gain_row(wa[:, COL_SEL:COL_ROUTER], LANE_GAIN_ONE)
    wait_all(get_v)
    gt_ref[...] = rg_ref[...] + dot_nt(vag_ref[...], wv[...]) + norm_back(b, unit, inverse)


def stacked(refs, first=0, last=None):
    return jnp.concatenate([r[:, first:last] for r in refs], axis=0)


def in_order(grid, idx, ref, first=0, size=None):
    size = ref.shape[2] - first if size is None else size
    return jnp.concatenate(
        [ref[shard_at(grid, idx, k, r), :, pl.ds(first, size)] for k, r in dp_tags(grid)], axis=0
    )


def by_owner(grid, idx, out_refs, value, first=0):
    X, Z = grid.X, grid.Z
    mine = value.shape[0] // (X * Z)
    columns = pl.ds(first, value.shape[1])
    for z in range(Z):
        blocks = [value[(z * X + x) * mine : (z * X + x + 1) * mine] for x in range(X)]
        for j in range(X):
            chosen = blocks[0]
            for x in range(1, X):
                chosen = jnp.where(lax.rem(idx[3] + j, X) == x, blocks[x], chosen)
            out_refs[j][z, :, columns] = chosen.astype(BF)


def grad_out_kernel(grid, idx, early, *refs):
    nd = grid.nd
    bgs, out = refs[:nd], refs[nd:]
    wide = H * DH
    gate = in_order(grid, idx, early, wide)
    att = in_order(grid, idx, early, 0, wide)
    by_owner(grid, idx, out, dot_tn(stacked(bgs), mixed_of(gate, att, HE)))


def own_columns(grid, idx, cols, which):
    piece = cols.shape[2] // (3 * grid.nd)
    at = which * piece * grid.nd + shard_at(grid, idx, 0, 0) * piece
    return in_order(grid, idx, cols, pl.multiple_of(at, piece), piece)


def grad_rest_kernel(grid, idx, cols, early, a_ref, *refs):
    nd = grid.nd
    late, out = refs[:nd], refs[nd:]
    x, n1, n2 = [own_columns(grid, idx, cols, i) for i in range(3)]
    acts = stacked(late)
    both = dot_tn(n1, acts[:, :COL_VG])
    by_owner(grid, idx, out, both[:, :COL_SEL])
    misc = a_ref[:, COL_SEL:COL_ROUTER].astype(F32)
    stats = in_order(grid, idx, early, H * DH)
    unit = (x.astype(F32) - col(stats, LANE_MEAN)) * col(stats, LANE_INVERSE)
    n1_grad = dot_nt(acts[:, :COL_VG], a_ref[:, :COL_ROUTER])
    n2_grad = dot_nt(acts[:, COL_RG:], a_ref[:, COL_ROUTER:])
    one = jnp.sum(n1_grad * unit, axis=0, keepdims=True)
    gains = jnp.transpose(misc)[LANE_GAIN_TWO : LANE_GAIN_TWO + 1]
    two = jnp.sum(n2_grad * n2.astype(F32), axis=0, keepdims=True) / gains
    row = rows_of((LANES, one.shape[1]))
    extra = jnp.where(row == LANE_GAIN_ONE, one, 0.0)
    extra = jnp.where(row == LANE_GAIN_TWO, two, extra)
    by_owner(grid, idx, out, both[:, COL_SEL:] + jnp.transpose(extra), COL_SEL)
    by_owner(grid, idx, out, dot_tn(n2, acts[:, COL_RG:]), COL_ROUTER)
    mixed = mixed_of(stats, acts[:, COL_VG:COL_RG].astype(F32), 0)
    by_owner(grid, idx, out, dot_tn(x, mixed), COL_VALUES)


def finish_kernel(*refs):
    parts, (q, k, v, vs, os, router, one, two) = refs[:-8], refs[-8:]
    total = parts[0][...].astype(F32)
    for ref in parts[1:]:
        total = total + ref[...].astype(F32)
    wide = H * DH
    q[...] = total[:, :wide]
    k[...] = total[:, wide:COL_SEL]
    misc = total[:, COL_SEL:COL_ROUTER]
    turned = jnp.transpose(misc)
    vs[...] = turned[:HE]
    os[...] = turned[HE : 2 * HE]
    one[...] = turned[LANE_GAIN_ONE : LANE_GAIN_ONE + 1]
    two[...] = turned[LANE_GAIN_TWO : LANE_GAIN_TWO + 1]
    router[...] = total[:, COL_ROUTER:COL_VALUES]
    v[...] = total[:, COL_VALUES:]


def shape(dims, dtype):
    return jax.ShapeDtypeStruct(dims, dtype)


def call(name, kernel, operands, specs, outs, scratch=(), mib=58, us=5, aliases=None):
    outs = [o if isinstance(o, tuple) else (o, VMEM) for o in outs]
    operands = [
        o if s is SMEM else pltpu.with_memory_space_constraint(o, pltpu.HBM)
        for o, s in zip(operands, specs, strict=True)
    ]
    return pl.pallas_call(
        kernel,
        out_shape=tuple(pltpu.HBM(o[0].shape, o[0].dtype) for o in outs),
        in_specs=list(specs),
        out_specs=tuple(o[1] for o in outs),
        scratch_shapes=list(scratch),
        input_output_aliases=aliases or {},
        compiler_params=pltpu.CompilerParams(vmem_limit_bytes=mib * 1024 * 1024),
        cost_estimate=pl.CostEstimate(
            flops=us, bytes_accessed=us, transcendentals=0
        ),
        name=name,
    )(*operands)


def dma(n):
    return pltpu.SemaphoreType.DMA((n,))


def per_device(
    nd,
    ne,
    tokens,
    cotangent,
    segments,
    value_picks,
    output_picks,
    expert_picks,
    attn_gain,
    query_weight,
    key_weight,
    value_weight,
    output_expert_weight,
    value_select,
    output_select,
    moe_gain,
    router_weight,
    up_weight,
    down_weight,
):
    grid = Grid(nd, ne)
    X, Y, Z, C = grid.X, grid.Y, grid.Z, grid.C
    micros, length, width = tokens.shape
    rows = micros * length
    local = up_weight.shape[0]
    piece = width // nd
    wide = H * DH
    values_wide = HE * DH
    dp, ex = lax.axis_index("dp"), lax.axis_index("expert")
    idx = jnp.stack([dp // C, dp % C, ex // X, ex % X]).astype(jnp.int32)


    x_all = tokens.reshape(rows, width)
    g_all = cotangent.reshape(rows, width)

    ends = (*STARTS[1:], COL_A)
    block_w, block_a, *parts_a = call(
        "pack",
        functools.partial(pack_kernel, grid),
        (
            idx,
            query_weight,
            key_weight,
            value_select.T,
            output_select.T,
            attn_gain,
            moe_gain,
            router_weight,
            value_weight,
            output_expert_weight,
        ),
        [SMEM] + [VMEM] * 9,
        [shape((piece, COL_A), BF), shape((piece, COL_VALUES), BF)]
        + [shape((piece // X, high - low), BF) for low, high in zip(STARTS, ends)],
        [pltpu.VMEM((LANES, piece), F32)],
        us=3,
    )

    def to_y(v, *deps):
        v = after(v, *deps)
        return [grid.rot_y(v, k) for k in range(1, Y)]

    def over_x(got_y, *deps):
        return [[v] + [grid.rot_x(after(v, *deps), j) for j in range(1, X)] for v in got_y]

    def add_pieces(arrays, tags, v, tag, swapped=None):
        k, split, j, column = tag
        arrays.append(v)
        tags.append((k, 0, split, j, column))
        if C > 1:
            arrays.append(grid.swap(v) if swapped is None else swapped)
            tags.append((k, 1, split, j, column))

    def swap(v, *deps):
        return grid.swap(after(v, *deps)) if C > 1 else None

    def spread_x(got_y, *deps):
        return [[v] + [grid.rot_x(after(v, *deps), j) for j in range(1, X)] for v in got_y]

    def swap_all(values, *deps):
        return [swap(v, *deps) for v in values]

    def flat(by_k):
        return [v for by_j in by_k for v in by_j]

    g_gathered = lax.all_gather(g_all, "expert", axis=0, tiled=True)
    swap_w = swap(block_w)
    seg = segments.reshape(1, rows)
    v_picks, o_picks = value_picks.reshape(rows, 2 * H), output_picks.reshape(rows, 2 * H)
    e_picks = expert_picks.reshape(rows, -1)
    done = [swap_w, seg, v_picks, o_picks, e_picks]
    over_y, over_x_too, swap_y, swap_x = [to_y(parts_a[0])], [], [], []
    done.append(over_y[0])
    swap_d = swap_u = d_y = None
    for i in range(len(STARTS)):
        last_round = i == len(STARTS) - 1
        new = []
        if not last_round:
            over_y.append(to_y(parts_a[i + 1], *done))
            new += over_y[-1]
        else:
            d_y = to_y(down_weight, *done)
            swap_u = swap(up_weight, *done)
            new += [swap_u, g_gathered]
        if i == len(STARTS) - 2:
            swap_d = swap(down_weight, *done)
            new.append(swap_d)
        over_x_too.append(spread_x(over_y[i], *done))
        swap_y.append(swap_all(over_y[i], *done))
        new += flat(over_x_too[-1]) + swap_y[-1]
        if i:
            swap_x.append([swap_all(by_j[1:], *done) for by_j in over_x_too[i - 1]])
            new += flat(swap_x[-1])
        done = new
    def weight_pieces(own, swapped, chunks):
        arrays, tags = [own, swapped], [(0, 0, None, 0, 0), (0, 1, None, 0, 0)]
        for column, got, others in chunks:
            for k, (by_j, swaps) in enumerate(zip(got, others), 1):
                for j, (v, o) in enumerate(zip(by_j, swaps)):
                    split = "x" if len(by_j) > 1 else None
                    arrays += [v, o]
                    tags += [(k, 0, split, j, column), (k, 1, split, j, column)]
        return arrays, tags

    def all_chunks():
        return [
            (low, got, [[v] + more for v, more in zip(ys, xs)])
            for low, got, ys, xs in zip(STARTS, over_x_too, swap_y, swap_x)
        ]

    first_pieces, first_tags = weight_pieces(block_w, swap_w, all_chunks()[:1])

    n1, qk, sig, mask, probs, wmr = call(
        "attend",
        functools.partial(attend_kernel, grid, first_tags, length),
        (
            idx,
            x_all,
            seg,
            v_picks,
            o_picks,
            *first_pieces,
        ),
        [SMEM] + [VMEM] * 4 + [ANY] * len(first_pieces),
        [
            shape((rows, width), BF),
            shape((rows, 2 * wide), BF),
            shape((rows, LANES), F32),
            shape((rows, LANES), F32),
            shape((rows, H * rows), F32),
            shape((width, 2 * LANES), BF),
        ],
        [pltpu.VMEM((width, COL_VALUES), BF), dma(len(first_pieces))],
        us=4,
    )
    swap_x.append([swap_all(by_j[1:], n1, *done) for by_j in over_x_too[-1]])
    a_pieces, a_tags = weight_pieces(block_w, swap_w, all_chunks())
    v_pieces, v_tags = window(a_pieces, a_tags, COL_VALUES, COL_OUT)
    o_pieces, o_tags = window(a_pieces, a_tags, COL_OUT, COL_A)
    vals, va, early, res, router, picked, xg, cols = call(
        "route",
        functools.partial(route_kernel, grid, v_tags, o_tags),
        (idx, x_all, n1, sig, mask, probs, wmr, e_picks, *v_pieces, *o_pieces),
        [SMEM] + [VMEM] * 7 + [ANY] * (len(v_pieces) + len(o_pieces)),
        [
            shape((rows, wide), BF),
            shape((rows, values_wide), F32),
            shape((rows, wide + LANES), F32),
            shape((rows, width), F32),
            shape((rows, EXPERTS), F32),
            shape((rows, EXPERTS), F32),
            shape((rows, width + EXPERTS), BF),
            shape((rows, 3 * width), BF),
        ],
        [
            pltpu.VMEM((width, values_wide), BF),
            pltpu.VMEM((width, values_wide), BF),
            dma(len(v_pieces)),
            dma(len(o_pieces)),
        ],
        us=8,
    )

    group = ne * length
    ff = local * LANES
    swap_dy = swap_all(d_y, xg)
    u_y = to_y(up_weight, xg, *d_y)
    column, x_over, done = [xg], [], []
    for k in range(1, Z):
        held = after(column[-1], *done)
        column.append(grid.rot_z(held, 1))
        x_over.append([grid.rot_x(held, j) for j in range(1, X)])
        last_done, done = done, [column[-1], x_over[-1]]
    ring_done = done

    def expert_pieces(own, swapped, got, others):
        arrays, tags = [own, swapped], [(0, 0, 0), (0, 1, 0)]
        for k, (v, o) in enumerate(zip(got, others), 1):
            arrays += [v, o]
            tags += [(k, 0, 0), (k, 1, 0)]
        return arrays, tags

    d_pieces, d_tags = expert_pieces(down_weight, swap_d, d_y, swap_dy)
    g_rows = g_gathered.reshape(ne, micros, length, width)
    total = micros * group
    (ahead,) = call(
        "ahead",
        functools.partial(ahead_kernel, grid, d_tags),
        (idx, after(g_rows, *last_done), *d_pieces),
        [SMEM] + [ANY] * (1 + len(d_tags)),
        [(shape((total, ff), BF), ANY)],
        [
            pltpu.VMEM((ne, micros, length, width), BF),
            pltpu.VMEM((local, LANES, width), BF),
            pltpu.VMEM((total, ff), BF),
            dma(1),
            dma(len(d_tags)),
            dma(local // 2),
        ],
        us=9,
    )
    x_over.append([grid.rot_x(after(column[-1], ahead, *ring_done), j) for j in range(1, X)])
    x_pieces = column + [by_j[j] for j in range(X - 1) for by_j in x_over]
    swap_uy = swap_all(u_y, *flat(x_over))
    u_pieces, u_tags = expert_pieces(up_weight, swap_u, u_y, swap_uy)
    froms = []

    def over_x(parts):
        return [grid.rot_x(parts[j], -j) for j in range(1, X)]

    def fold(parts, others, *deps):
        return call(
            "fold",
            fold_kernel,
            (idx, after(parts[0], *deps), *others),
            [SMEM] + [VMEM] * X,
            [shape(parts[0].shape[1:], BF)] * Z,
            us=2,
        )

    sent, shared = [], []
    for m in range(micros):
        hg, pg, x_group, *back = call(
            "experts",
            functools.partial(expert_kernel, grid, u_tags, m, micros),
            (idx, ahead, *x_pieces, *u_pieces, *shared),
            [SMEM, ANY] + [ANY] * (ne + len(u_tags) + len(shared)),
            [
                (shape((total, ff), BF), ANY),
                (shape((total, ff), BF), ANY),
                (shape((total, width + EXPERTS), BF), ANY),
                *[shape((Z, length, width + EXPERTS), BF)] * X,
            ],
            [
                pltpu.VMEM((group, ff), BF),
                pltpu.VMEM((group, ff), BF),
                pltpu.VMEM((group, width + EXPERTS), BF),
                pltpu.VMEM((group, ff), BF),
                pltpu.VMEM((local, width, LANES), BF),
                pltpu.VMEM((group, EXPERTS), F32),
                pltpu.VMEM((group, max(piece, EXPERTS)), F32),
                dma(ne),
                dma(len(u_tags)),
                dma(1),
                dma(3),
            ],
            us=12,
            aliases={2 + ne + len(u_tags) + i: i for i in range(len(shared))},
        )
        shared = [hg, pg, x_group]
        sent.append(back)

    def out_rows(*deps):
        return call(
            "out",
            functools.partial(out_kernel, grid, d_tags, micros),
            (idx, after(hg, *deps), *d_pieces),
            [SMEM] + [ANY] * (1 + len(d_tags)),
            [shape((ne, rows, width), BF)],
            [
                pltpu.VMEM((total, ff), BF),
                pltpu.VMEM((local, LANES, width), BF),
                dma(1),
                dma(len(d_tags)),
            ],
            us=10,
        )

    def expert_grad(name, kernel, lhs, rhs, dims, *deps):
        halves = 2
        block = pl.BlockSpec((Y, local // halves, *dims), lambda h, idx: (0, h, 0, 0))
        if lhs.ndim == 4:
            whole = pl.BlockSpec((ne, micros, length, width), lambda h, idx: (0, 0, 0, 0))
        else:
            whole = pl.BlockSpec((total, width), lambda h, idx: (0, 0))
        part = (width, ff // halves) if lhs.ndim == 2 else (ff // halves, width)
        return pl.pallas_call(
            functools.partial(kernel, grid),
            out_shape=[pltpu.HBM((Y, local, *dims), BF)] * C,
            grid_spec=pltpu.PrefetchScalarGridSpec(
                num_scalar_prefetch=1,
                grid=(halves,),
                in_specs=[whole, pl.BlockSpec((total, ff // halves), lambda h, idx: (0, h))],
                out_specs=[block] * C,
                scratch_shapes=[pltpu.VMEM(part, F32)],
            ),
            compiler_params=pltpu.CompilerParams(vmem_limit_bytes=58 * 1024 * 1024),
            cost_estimate=pl.CostEstimate(flops=4, bytes_accessed=12, transcendentals=0),
            name=name,
        )(idx, *[pltpu.with_memory_space_constraint(v, pltpu.HBM) for v in (after(lhs, *deps), rhs)])

    def added_blocks(name, arrays, dtype, split):
        steps = 2
        dims = arrays[0].shape[1:] if split else arrays[0].shape
        some = (dims[0] // steps, *dims[1:])
        one = pl.BlockSpec(some, lambda i: (i, 0, 0))
        spec = pl.BlockSpec((Y, *some), lambda i: (0, i, 0, 0)) if split else one
        results = Y if split else 1

        def kernel(*refs):
            for k, out in enumerate(refs[len(arrays) :]):
                total = 0.0
                for ref in refs[: len(arrays)]:
                    total = total + (ref[k] if split else ref[...]).astype(F32)
                out[...] = total.astype(dtype)

        return pl.pallas_call(
            kernel,
            out_shape=[pltpu.HBM(dims, dtype)] * results,
            grid=(steps,),
            in_specs=[spec] * len(arrays),
            out_specs=[one] * results,
            compiler_params=pltpu.CompilerParams(vmem_limit_bytes=58 * 1024 * 1024),
            cost_estimate=pl.CostEstimate(flops=1, bytes_accessed=3, transcendentals=0),
            name=name,
        )(*[pltpu.with_memory_space_constraint(v, pltpu.HBM) for v in arrays])

    down_args = ("down_grad", down_grad_kernel, g_rows, hg, (LANES, piece))
    up_args = ("up_grad", up_grad_kernel, x_group, pg, (piece, LANES))

    def reduce_y(total, *deps):
        got = [grid.rot_y(after(total[k], *deps), k) for k in range(1, Y)]
        return lambda *more: added_blocks("last_sum", [after(total[0], *more), *got], F32, False)[0], got

    from_x = [over_x(v) for v in sent]
    sums = fold(sent[0], from_x[0], hg)
    froms.append(grid.send_z(sums))
    outs_sent = out_rows(sums[0])
    before, down_came, up_came = outs_sent[0], [], []
    for m in range(1, micros):
        sums = fold(sent[m], from_x[m], before, froms[-1])
        froms.append(grid.send_z(sums))
        before = sums[0]
    down_near, *down_far = expert_grad(*down_args, before)
    up_near, *up_far = expert_grad(*up_args, down_near)
    before = up_near

    early_all = lax.all_gather(after(early, u_pieces), "dp", axis=0)
    cols_all = lax.all_gather(after(cols, u_pieces), "dp", axis=0)
    res_grad, bg, rg, *bg_cols = call(
        "back_norm",
        functools.partial(back_norm_kernel, grid, micros),
        (
            idx,
            wmr,
            res,
            g_all,
            after(router, before, early_all, cols_all),
            picked,
            *[p for f in froms for p in f],
        ),
        [SMEM] + [VMEM] * (5 + micros * Z),
        [
            shape((rows, width), F32),
            shape((rows, width), BF),
            shape((rows, EXPERTS), BF),
            *[shape((rows, piece), BF)] * nd,
        ],
        us=3,
    )
    bgs = [v if t == (0, 0) else grid.rot_yc(v, *t) for v, t in zip(bg_cols, dp_tags(grid))]
    late, vag = call(
        "back_attend",
        functools.partial(back_attend_kernel, grid, o_tags),
        (idx, bg, rg, sig, mask, early, qk, vals, va, probs, *o_pieces),
        [SMEM] + [VMEM] * 9 + [ANY] * len(o_pieces),
        [shape((rows, COL_LATE), BF), shape((rows, values_wide), BF)],
        [pltpu.VMEM((width, values_wide), BF), dma(len(o_pieces))],
        us=8,
    )
    outs = lax.all_to_all(after(outs_sent[0], bg), "expert", 0, 0, tiled=True)
    down_came, up_came = swap_all(down_far, bg), swap_all(up_far, bg)
    late_swap = swap(late, bgs[1:], *down_came, *up_came)
    late_y = to_y(late, bgs[1:])

    mine = piece // ne

    def weight_grad(name, kernel, operands, columns):
        parts = call(
            name,
            functools.partial(kernel, grid),
            (idx, *operands),
            [SMEM] + [VMEM] * len(operands),
            [shape((Z, mine, columns), BF)] * X,
            us=3,
        )
        return parts, [grid.rot_x(parts[j], j) for j in range(1, X)]

    def fold_at(parts, others, *deps):
        sums = call(
            "fold_at",
            fold_at_kernel,
            (idx, after(parts[0], *deps), *others),
            [SMEM] + [VMEM] * X,
            [shape(parts[0].shape[1:], BF)] * Z,
            us=1,
        )
        return sums[0], grid.send_z(sums)

    def added(parts, *deps):
        return call(
            "sum",
            sum_kernel,
            (after(parts[0], *deps), *parts[1:]),
            [VMEM] * len(parts),
            [shape(parts[0].shape, F32)],
            us=1,
        )[0]

    down_sum = added_blocks("core_sum", [after(down_near, late), *down_came], BF, True)
    up_sum = added_blocks("core_sum", [after(up_near, down_sum), *up_came], BF, True)
    o_parts, o_others = weight_grad(
        "grad_out", grad_out_kernel, [after(early_all, up_sum), *bgs], values_wide
    )
    down_last, down_got = reduce_y(down_sum, late_y)
    up_last, up_got = reduce_y(up_sum, late_y)
    late_all = [late, *late_y, late_swap, *swap_all(late_y, o_parts[0])]
    r_parts, r_others = weight_grad(
        "grad_rest",
        grad_rest_kernel,
        [after(cols_all, o_parts[0]), early_all, block_a, *late_all],
        COL_OUT,
    )
    o_fold, o_sums = fold_at(o_parts, o_others, r_parts[0])
    r_fold, r_sums = fold_at(r_parts, r_others, o_sums, outs)
    grad_down = down_last(r_fold)
    grad_up = up_last(grad_down)
    (grad_tokens,) = call(
        "back_token",
        functools.partial(back_token_kernel, grid, a_tags),
        (idx, x_all, res_grad, after(late, r_fold), vag, *a_pieces),
        [SMEM] + [VMEM] * 4 + [ANY] * len(a_pieces),
        [shape((rows, width), F32)],
        [
            pltpu.VMEM((width, COL_VALUES), BF),
            pltpu.VMEM((width, values_wide), BF),
            dma(len(a_pieces)),
            dma(len(a_pieces)),
        ],
        us=8,
    )
    (output,) = call(
        "add_out",
        sum_places_kernel,
        (outs, after(res, grad_tokens)),
        [VMEM] * 2,
        [shape((rows, width), F32)],
        us=2,
    )
    grad_output = added(o_sums, output)
    q, k, grad_value, vs, os, r, one, two = call(
        "finish",
        finish_kernel,
        (after(r_sums[0], grad_tokens, output, grad_output, grad_up), *r_sums[1:]),
        [VMEM] * Z,
        [
            shape((mine, wide), F32),
            shape((mine, wide), F32),
            shape((mine, values_wide), F32),
            shape((HE, mine), F32),
            shape((HE, mine), F32),
            shape((mine, EXPERTS), F32),
            shape((1, mine), F32),
            shape((1, mine), F32),
        ],
        us=1,
    )
    return (
        output.reshape(micros, length, width),
        grad_tokens.reshape(micros, length, width),
        one.reshape(mine),
        q,
        k,
        grad_value,
        grad_output,
        vs.T,
        os.T,
        two.reshape(mine),
        r,
        grad_up,
        grad_down,
    )


def solution(mesh):
    rows = ("dp", "expert")
    placed = (
        P(None, rows, None),
        P(None, rows, None),
        P(None, rows, None),
        P(None, rows, None, None),
        P(None, rows, None, None),
        P(None, rows, None),
        P("dp"),
        P("dp", None),
        P("dp", None),
        P("dp", None),
        P("dp", None),
        P("dp", None),
        P("dp", None),
        P("dp"),
        P("dp", None),
        P("expert", "dp", None),
        P("expert", None, "dp"),
    )
    return jax.shard_map(
        functools.partial(per_device, mesh.shape["dp"], mesh.shape["expert"]),
        mesh=mesh,
        in_specs=placed,
        out_specs=(
            P(None, rows, None),
            P(None, rows, None),
            P(rows),
            P(rows, None),
            P(rows, None),
            P(rows, None),
            P(rows, None),
            P(rows, None),
            P(rows, None),
            P(rows),
            P(rows, None),
            P("expert", "dp", None),
            P("expert", None, "dp"),
        ),
        check_vma=False,
    )
```

```python
import functools

import jax
import jax.numpy as jnp
from jax import lax
from jax.experimental import pallas as pl
from jax.experimental.pallas import tpu as pltpu
from jax.sharding import PartitionSpec as P

H = 4
DH = 128
EA = 5
HE = H * EA
EXPERTS = 128
EPSILON = 1e-05
MASKED = -1e30
SCALE = DH ** (-0.5)
LANES = 128

BF = jnp.bfloat16
F32 = jnp.float32

COL_SEL = 2 * H * DH
COL_ROUTER = COL_SEL + LANES
COL_VALUES = COL_ROUTER + LANES
COL_OUT = COL_VALUES + HE * DH
COL_A = COL_OUT + HE * DH
STARTS = (0, 17 * LANES, 34 * LANES)
LANE_GAIN_ONE = 2 * HE
LANE_GAIN_TWO = 2 * HE + 1
LANE_MEAN = 2 * HE
LANE_INVERSE = 2 * HE + 1
COL_LG = 2 * H * DH
COL_VG = COL_LG + LANES
COL_RG = COL_VG + H * DH
COL_LATE = COL_RG + LANES

VMEM = pl.BlockSpec()
SMEM = pl.BlockSpec(memory_space=pltpu.SMEM)
ANY = pl.BlockSpec(memory_space=pltpu.HBM)


def dot(a, b):
    return jnp.dot(a, b, preferred_element_type=F32)


def dot_nt(a, b):
    return lax.dot_general(a, b, (((1,), (1,)), ((), ())), preferred_element_type=F32)


def dot_tn(a, b):
    return lax.dot_general(a, b, (((0,), (0,)), ((), ())), preferred_element_type=F32)


def sigmoid(v):
    return 1.0 / (1.0 + jnp.exp(-v))


class Grid:
    def __init__(self, nd, ne):
        self.nd, self.ne = nd, ne
        self.C = 2 if nd % 2 == 0 else 1
        self.Y = nd // self.C
        x = 1
        while (2 * x) * (2 * x) <= ne and ne % (2 * x) == 0:
            x *= 2
        self.X, self.Z = x, ne // x

    def _dp(self, v, go):
        C = self.C
        pairs = []
        for i in range(self.nd):
            y, c = go(i // C, i % C)
            pairs.append((i, y * C + c))
        return lax.ppermute(v, "dp", pairs)

    def _ex(self, v, go):
        X = self.X
        pairs = []
        for i in range(self.ne):
            z, x = go(i // X, i % X)
            pairs.append((i, z * X + x))
        return lax.ppermute(v, "expert", pairs)

    def rot_y(self, v, k):
        return self._dp(v, lambda y, c: ((y + k) % self.Y, c))

    def swap(self, v):
        return self._dp(v, lambda y, c: (y, c ^ 1))

    def rot_yc(self, v, k, r):
        return self._dp(v, lambda y, c: ((y + k) % self.Y, c ^ r))

    def rot_x(self, v, j):
        return self._ex(v, lambda z, x: (z, (x + j) % self.X))

    def rot_z(self, v, k):
        return self._ex(v, lambda z, x: ((z + k) % self.Z, x))

    def lines_z(self):
        return [[z * self.X + x for z in range(self.Z)] for x in range(self.X)]

    def gather_z(self, v):
        return lax.all_gather(v, "expert", axis=0, tiled=True, axis_index_groups=self.lines_z())

    def swap_z(self, v):
        return lax.all_to_all(v, "expert", 0, 0, tiled=True, axis_index_groups=self.lines_z())

    def send_z(self, parts):
        return [parts[0]] + [self.rot_z(parts[k], k) for k in range(1, self.Z)]

    def swap_dp(self, v):
        return lax.all_to_all(v, "dp", 0, 0, tiled=True)


def after(v, *deps):
    flat = [d for dep in deps for d in (dep if isinstance(dep, (list, tuple)) else [dep])]
    if not flat:
        return v
    return lax.optimization_barrier((v, *flat))[0]


def gather_dp(grid, w, over_y, swapped=None):
    got = [w] + list(over_y)
    if grid.C > 1:
        got = got + [grid.swap(w) if swapped is None else swapped] + [grid.swap(v) for v in over_y]
    return got


def dp_tags(grid):
    return [(k, r) for r in range(grid.C) for k in range(grid.Y)]


def shard_at(grid, idx, k, r):
    return lax.rem(idx[0] + (grid.Y - k), grid.Y) * grid.C + lax.rem(idx[1] + r, grid.C)


def fetch_rows(grid, idx, refs, tags, dst, sems, first=0):
    copies = []
    width, last = dst.shape[0] // grid.nd, first + dst.shape[1]
    for i, (ref, (k, r, split, j, column)) in enumerate(zip(refs, tags)):
        low, high = max(first, column), min(last, column + ref.shape[1])
        if low >= high:
            continue
        at = shard_at(grid, idx, k, r) * width
        n = width
        if split is not None:
            size, mine = (grid.X, idx[3]) if split == "x" else (grid.Z, idx[2])
            n = width // size
            at = at + lax.rem(mine + (size - j), size) * n
        at = pl.multiple_of(at, n)
        copy = pltpu.make_async_copy(
            ref.at[:, pl.ds(low - column, high - low)],
            dst.at[pl.ds(at, n), pl.ds(low - first, high - low)],
            sems.at[i],
        )
        copy.start()
        copies.append(copy)
    return copies


def fetch_experts(grid, idx, refs, tags, dst, axis, sems):
    copies = []
    n = dst.shape[axis] // grid.nd
    for i, (ref, (k, r, first)) in enumerate(zip(refs, tags)):
        at = pl.ds(pl.multiple_of(shard_at(grid, idx, k, r) * n, n), n)
        held = pl.ds(first, ref.shape[0])
        place = dst.at[held, at, :] if axis == 1 else dst.at[held, :, at]
        copy = pltpu.make_async_copy(ref, place, sems.at[i])
        copy.start()
        copies.append(copy)
    return copies


def wait_all(copies):
    for copy in copies:
        copy.wait()


def lanes_of(dims):
    return lax.broadcasted_iota(jnp.int32, dims, 1)


def rows_of(dims):
    return lax.broadcasted_iota(jnp.int32, dims, 0)


def norm_stats(v):
    centered = v - jnp.mean(v, axis=-1, keepdims=True)
    inverse = lax.rsqrt(jnp.mean(centered * centered, axis=-1, keepdims=True) + EPSILON)
    return centered * inverse, inverse


def window(pieces, tags, low, high):
    held = [(p, t) for p, t in zip(pieces, tags) if t[4] < high and t[4] + p.shape[1] > low]
    return [p for p, _ in held], [t for _, t in held]


def norm_back(grad, unit, inverse):
    return inverse * (
        grad
        - jnp.mean(grad, axis=-1, keepdims=True)
        - unit * jnp.mean(grad * unit, axis=-1, keepdims=True)
    )


def gain_row(block, lane):
    return jnp.transpose(block.astype(F32))[lane : lane + 1, :]


def col(v, i):
    return v[:, i : i + 1]


def head(v, i):
    return v[:, i * DH : (i + 1) * DH]


def mixed_of(gate, vectors, first):
    return jnp.concatenate(
        [
            (col(gate, first + h * EA + e) * head(vectors, h)).astype(BF)
            for h in range(H)
            for e in range(EA)
        ],
        axis=1,
    )


def pack_kernel(grid, idx, q, k, vs, os, gain_one, gain_two, router, v_ref, o_ref, w_ref, a_ref, *rest):
    parts, misc = rest[:-1], rest[-1]
    piece = q.shape[0]
    nx = piece // grid.X
    at_x = pl.ds(pl.multiple_of(idx[3] * nx, nx), nx)
    misc[...] = jnp.zeros_like(misc)
    misc[:HE, :] = vs[...].astype(F32)
    misc[HE : 2 * HE, :] = os[...].astype(F32)
    misc[LANE_GAIN_ONE : LANE_GAIN_ONE + 1, :] = gain_one[...].astype(F32).reshape(1, piece)
    misc[LANE_GAIN_TWO : LANE_GAIN_TWO + 1, :] = gain_two[...].astype(F32).reshape(1, piece)
    wide = H * DH
    a_ref[:, :wide] = q[...]
    a_ref[:, wide:COL_SEL] = k[...]
    a_ref[:, COL_SEL:COL_ROUTER] = jnp.transpose(misc[...]).astype(BF)
    a_ref[:, COL_ROUTER:] = router[...]
    w_ref[:, :COL_VALUES] = a_ref[...]
    w_ref[:, COL_VALUES:COL_OUT] = v_ref[...]
    w_ref[:, COL_OUT:] = o_ref[...]
    for part, low in zip(parts, STARTS):
        part[...] = w_ref[at_x, low : low + part.shape[1]]


def attend_kernel(grid, tags, length, idx, x_ref, seg_ref, vp, op, *rest):
    n = len(tags)
    a_refs = rest[:n]
    n1_ref, qk_ref, sig_ref, mask_ref, pr_ref, wmr_ref, wa, sem_a = rest[n:]
    get_a = fetch_rows(grid, idx, a_refs, tags, wa, sem_a)
    unit, _ = norm_stats(x_ref[...].astype(F32))
    tokens = unit.shape[0]
    lane = lanes_of((tokens, LANES))
    mask = jnp.zeros((tokens, LANES), F32)
    for h in range(H):
        for k in range(2):
            mask = mask + (lane == col(vp, 2 * h + k) + EA * h).astype(F32)
            mask = mask + (lane == col(op, 2 * h + k) + (EA * h + HE)).astype(F32)
    mask_ref[...] = mask
    square = (tokens, tokens)
    row, lane = rows_of(square), lanes_of(square)
    seg = jnp.broadcast_to(seg_ref[...].astype(F32), square)
    allowed = (seg == jnp.transpose(seg)) & (lane <= row) & (lane // length == row // length)
    wait_all(get_a)
    n1 = (unit * gain_row(wa[:, COL_SEL:COL_ROUTER], LANE_GAIN_ONE)).astype(BF)
    n1_ref[...] = n1
    qks = dot(n1, wa[:, :COL_ROUTER])
    qk = qks[:, :COL_SEL].astype(BF)
    qk_ref[...] = qk
    sig_ref[...] = sigmoid(qks[:, COL_SEL:])
    wmr_ref[...] = wa[:, COL_SEL:]
    for h in range(H):
        scores = dot_nt(head(qk, h), head(qk, H + h))
        scaled = jnp.where(allowed, scores * SCALE, MASKED)
        top = jnp.max(scaled, axis=-1, keepdims=True)
        expo = jnp.where(allowed, jnp.exp(scaled - top), 0.0)
        pr_ref[:, h * tokens : (h + 1) * tokens] = expo / jnp.sum(expo, axis=-1, keepdims=True)


def route_kernel(grid, v_tags, o_tags, idx, x_ref, n1_ref, sig_ref, mask_ref, pr_ref, wmr_ref, ep, *rest):
    nv, no = len(v_tags), len(o_tags)
    v_refs, o_refs = rest[:nv], rest[nv : nv + no]
    rest = rest[nv + no :]
    val_ref, va_ref, early_ref, res_ref, router_ref, picked_ref = rest[:6]
    xg_ref, col_ref, wv, wo, sem_v, sem_o = rest[6:]
    get_v = fetch_rows(grid, idx, v_refs, v_tags, wv, sem_v, COL_VALUES)
    get_o = fetch_rows(grid, idx, o_refs, o_tags, wo, sem_o, COL_OUT)
    gate = sig_ref[...] * mask_ref[...]
    tokens, width = x_ref.shape
    lane = lanes_of((tokens, EXPERTS))
    picked = jnp.zeros((tokens, EXPERTS), F32)
    for k in range(ep.shape[1]):
        picked = picked + (lane == col(ep, k)).astype(F32)
    picked_ref[...] = picked
    x_bf = x_ref[...]
    wait_all(get_v)
    atts = []
    for h in range(H):
        va = dot(x_bf, wv[:, h * EA * DH : (h + 1) * EA * DH])
        va_ref[:, h * EA * DH : (h + 1) * EA * DH] = va
        total = col(gate, h * EA) * head(va, 0)
        for e in range(1, EA):
            total = total + col(gate, h * EA + e) * head(va, e)
        value = total.astype(BF)
        val_ref[:, h * DH : (h + 1) * DH] = value
        atts.append(dot(pr_ref[:, h * tokens : (h + 1) * tokens].astype(BF), value))
    att = jnp.concatenate(atts, axis=1)
    early_ref[:, : H * DH] = att
    mean = jnp.mean(x_bf.astype(F32), axis=-1, keepdims=True)
    centered = x_bf.astype(F32) - mean
    inverse = lax.rsqrt(jnp.mean(centered * centered, axis=-1, keepdims=True) + EPSILON)
    lane = lanes_of((tokens, LANES))
    early_ref[:, H * DH :] = jnp.where(
        lane == LANE_MEAN, mean, jnp.where(lane == LANE_INVERSE, inverse, gate)
    )
    mixed = mixed_of(gate, att, HE)
    wait_all(get_o)
    res = x_bf.astype(F32) + dot_nt(mixed, wo[...])
    res_ref[...] = res
    unit, _ = norm_stats(res)
    n2 = (unit * gain_row(wmr_ref[:, :LANES], LANE_GAIN_TWO)).astype(BF)
    router = sigmoid(dot(n2, wmr_ref[:, LANES:]))
    router_ref[...] = router
    xg_ref[:, :width] = res.astype(BF)
    xg_ref[:, width:] = (router * picked).astype(BF)
    col_ref[:, :width] = x_bf
    col_ref[:, width : 2 * width] = n1_ref[...]
    col_ref[:, 2 * width :] = n2


def ahead_kernel(grid, tags, idx, g_ref, *rest):
    d_refs, (gh_ref, g, down, gh, sem_g, sem_d, sem_o) = rest[: len(tags)], rest[len(tags) :]
    local, width = down.shape[0], down.shape[2]
    micros = g.shape[1]
    get_g = pltpu.make_async_copy(g_ref, g, sem_g.at[0])
    get_g.start()
    get_d = fetch_experts(grid, idx, d_refs, tags, down, 2, sem_d)
    get_g.wait()
    wait_all(get_d)
    group = g.shape[0] * g.shape[2]
    copies = []
    for p in range(local // 2):
        d2 = down[2 * p : 2 * p + 2].reshape(2 * LANES, width)
        columns = pl.ds(p * 2 * LANES, 2 * LANES)
        for m in range(micros):
            gh[m * group : (m + 1) * group, columns] = dot_nt(g[:, m].reshape(group, width), d2).astype(BF)
        copies.append(pltpu.make_async_copy(gh.at[:, columns], gh_ref.at[:, columns], sem_o.at[p]))
        copies[-1].start()
    wait_all(copies)


def place_of(grid, idx, j, k):
    return lax.rem(idx[2] + (grid.Z - k), grid.Z) * grid.X + lax.rem(idx[3] + (grid.X - j), grid.X)


def expert_kernel(grid, tags, micro, micros, idx, gh_ref, *rest):
    n, X, Z, nd, nt = grid.ne, grid.X, grid.Z, grid.nd, len(tags)
    x_refs, u_refs = rest[:n], rest[n : n + nt]
    rest = rest[n + nt + (3 if micro else 0) :]
    hg_ref, pg_ref, xg_ref = rest[:3]
    from_refs = rest[3 : 3 + X]
    hg, pg, xg, gh, up, gg, back, sem_x, sem_u, sem_g, sem_o = rest[3 + X :]
    local, width = up.shape[0], up.shape[1]
    tokens = xg.shape[0]
    rows = tokens // n
    mine = pl.ds(micro * tokens, tokens)
    get_x = []
    for j in range(X):
        for k in range(Z):
            at = pl.multiple_of(place_of(grid, idx, j, k) * rows, rows)
            i = j * Z + k
            get_x.append(
                pltpu.make_async_copy(
                    x_refs[i].at[pl.ds(micro * rows, rows), :], xg.at[pl.ds(at, rows), :], sem_x.at[i]
                )
            )
            get_x[-1].start()
    get_u = fetch_experts(grid, idx, u_refs, tags, up, 1, sem_u)
    get_g = pltpu.make_async_copy(gh_ref.at[mine, :], gh, sem_g.at[0])
    get_g.start()
    first = (idx[2] * X + idx[3]) * local
    gg[...] = jnp.zeros_like(gg)
    lane = lanes_of((tokens, EXPERTS))
    wait_all(get_x)
    copies = [pltpu.make_async_copy(xg, xg_ref.at[mine, :], sem_o.at[0])]
    copies[0].start()
    wait_all(get_u)
    get_g.wait()

    def pair(p, carry):
        w2 = jnp.concatenate([up[2 * p], up[2 * p + 1]], axis=1)
        pre = dot(xg[:, :width], w2)
        columns = pl.ds(pl.multiple_of(p * 2 * LANES, 2 * LANES), 2 * LANES)
        grad = gh[:, columns].astype(F32)
        at = first + 2 * p
        gates = pltpu.roll(xg[:, width:].astype(F32), EXPERTS - at, 1)
        gate = jnp.concatenate(
            [jnp.broadcast_to(col(gates, i), (tokens, LANES)) for i in range(2)], axis=1
        )
        sig = sigmoid(pre)
        hidden = (pre * sig).astype(BF).astype(F32)
        part = hidden * grad
        total = gg[...]
        for i in range(2):
            each = jnp.sum(head(part, i), axis=1, keepdims=True)
            total = total + jnp.where(lane == at + i, each, 0.0)
        gg[...] = total
        hg[:, columns] = (gate * hidden).astype(BF)
        pg[:, columns] = (gate * grad * sig * (1.0 + pre * (1.0 - sig))).astype(BF)
        return carry

    lax.fori_loop(0, local // 2, pair, 0)
    for i, (src, dst) in enumerate(((hg, hg_ref), (pg, pg_ref)), 1):
        copies.append(pltpu.make_async_copy(src, dst.at[mine, :], sem_o.at[i]))
        copies[-1].start()
    piece = width // nd

    def blocks(columns):
        for j in range(X):
            for k in range(Z):
                at = pl.multiple_of(place_of(grid, idx, j, k) * rows, rows)
                from_refs[j][k, :, columns] = back[pl.ds(at, rows), : columns.size].astype(BF)

    for q in range(nd):
        columns = pl.ds(q * piece, piece)
        w = jnp.concatenate([up[e, columns, :] for e in range(local)], axis=1)
        back[:, :piece] = dot_nt(pg[...], w)
        blocks(columns)
    back[:, :EXPERTS] = gg[...]
    blocks(pl.ds(width, EXPERTS))
    wait_all(copies)


def out_kernel(grid, tags, micros, idx, hg_ref, *rest):
    nd, nt = grid.nd, len(tags)
    d_refs, (out_ref, hg, down, sem_g, sem_d) = rest[:nt], rest[nt:]
    local, width = down.shape[0], down.shape[2]
    group = hg.shape[0] // micros
    rows = group // grid.ne
    piece = width // nd
    get_d = fetch_experts(grid, idx, d_refs, tags, down, 2, sem_d)
    get_g = pltpu.make_async_copy(hg_ref, hg, sem_g.at[0])
    get_g.start()
    wait_all(get_d)
    get_g.wait()
    for q in range(nd):
        columns = pl.ds(q * piece, piece)
        back = dot(hg[...], down[:, :, columns].reshape(local * LANES, piece)).astype(BF)
        for e in range(grid.ne):
            for m in range(micros):
                at = m * group + e * rows
                out_ref[e, m * rows : (m + 1) * rows, columns] = back[at : at + rows]


def to_dp_place(grid, idx, k, r, piece):
    at = lax.rem(idx[0] + k, grid.Y) * grid.C + lax.rem(idx[1] + r, grid.C)
    return pl.ds(pl.multiple_of(at * piece, piece), piece)


def up_grad_kernel(grid, idx, x_ref, pg_ref, *rest):
    outs, acc = rest[:-1], rest[-1]
    acc[...] = dot_tn(x_ref[...], pg_ref[...])
    piece = outs[0].shape[2]
    for k, r in dp_tags(grid):
        rows = to_dp_place(grid, idx, k, r, piece)
        for e in range(outs[r].shape[1]):
            outs[r][k, e] = acc[rows, e * LANES : (e + 1) * LANES].astype(BF)


def down_grad_kernel(grid, idx, g_ref, hg_ref, *rest):
    outs, acc = rest[:-1], rest[-1]
    places, micros, rows, width = g_ref.shape
    g = jnp.concatenate([g_ref[:, m].reshape(places * rows, width) for m in range(micros)], axis=0)
    acc[...] = dot_tn(hg_ref[...], g)
    piece = outs[0].shape[3]
    for k, r in dp_tags(grid):
        columns = to_dp_place(grid, idx, k, r, piece)
        for e in range(outs[r].shape[1]):
            outs[r][k, e] = acc[e * LANES : (e + 1) * LANES, columns].astype(BF)


def fold_kernel(idx, own, *refs):
    Z = own.shape[0]
    others, out = refs[:-Z], refs[-Z:]
    del idx
    for k in range(Z):
        at = (Z - k) % Z
        total = own[at].astype(F32)
        for ref in others:
            total = total + ref[at].astype(F32)
        out[k][...] = total.astype(BF)


def fold_at_kernel(idx, own, *refs):
    Z = own.shape[0]
    others, out = refs[:-Z], refs[-Z:]
    for k in range(Z):
        at = lax.rem(idx[2] + k, Z)
        total = own[at].astype(F32)
        for ref in others:
            total = total + ref[at].astype(F32)
        out[k][...] = total.astype(BF)


def sum_kernel(*refs):
    total = refs[0][...].astype(F32)
    for ref in refs[1:-1]:
        total = total + ref[...].astype(F32)
    refs[-1][...] = total


def sum_places_kernel(parts, own, out):
    total = own[...]
    for z in range(parts.shape[0]):
        total = total + parts[z].astype(F32)
    out[...] = total


def back_norm_kernel(grid, micros, idx, wmr_ref, res_ref, g_ref, router_ref, picked_ref, *rest):
    nd, Z = grid.nd, grid.Z
    n = micros * Z
    rg_ref, bg_ref, late_ref = rest[n : n + 3]
    cols = rest[n + 3 :]
    width = res_ref.shape[1]
    parts = []
    for m in range(micros):
        total = rest[m * Z][...].astype(F32)
        for ref in rest[m * Z + 1 : (m + 1) * Z]:
            total = total + ref[...].astype(F32)
        parts.append(total)
    back = jnp.concatenate(parts, axis=0)
    router = router_ref[...]
    late = (back[:, width:] * picked_ref[...] * router * (1.0 - router)).astype(BF)
    late_ref[...] = late
    unit, inverse = norm_stats(res_ref[...])
    n2g = dot_nt(late, wmr_ref[:, LANES:])
    a = n2g * gain_row(wmr_ref[:, :LANES], LANE_GAIN_TWO)
    res_grad = g_ref[...].astype(F32) + back[:, :width] + norm_back(a, unit, inverse)
    rg_ref[...] = res_grad
    bg_ref[...] = res_grad.astype(BF)
    piece = width // nd
    for ref, (k, r) in zip(cols, dp_tags(grid)):
        at = lax.rem(idx[0] + k, grid.Y) * grid.C + lax.rem(idx[1] + r, grid.C)
        ref[...] = bg_ref[:, pl.ds(pl.multiple_of(at * piece, piece), piece)]


def back_attend_kernel(grid, tags, idx, bg_ref, rg_ref, sig_ref, mask_ref, early_ref, qk_ref, val_ref, va_ref,
                       pr_ref, *rest):
    n = len(tags)
    o_refs = rest[:n]
    late_ref, vag_ref, wo, sem_o = rest[n:]
    get_o = fetch_rows(grid, idx, o_refs, tags, wo, sem_o, COL_OUT)
    bg = bg_ref[...]
    tokens = bg.shape[0]
    sig, gate = sig_ref[...], early_ref[:, H * DH :]
    lane = lanes_of((tokens, LANES))
    logits = jnp.zeros((tokens, LANES), F32)
    wait_all(get_o)
    for h in range(H):
        att = early_ref[:, h * DH : (h + 1) * DH]
        mg = dot(bg, wo[:, h * EA * DH : (h + 1) * EA * DH])
        ag = jnp.zeros((tokens, DH), F32)
        for e in range(EA):
            i = HE + h * EA + e
            ag = ag + col(gate, i) * head(mg, e)
            each = jnp.sum(head(mg, e) * att, axis=1, keepdims=True)
            logits = jnp.where(lane == i, each, logits)
        ag = ag.astype(BF)
        prob = pr_ref[:, h * tokens : (h + 1) * tokens]
        vg = dot_tn(prob.astype(BF), ag)
        pgrad = dot_nt(ag, val_ref[:, h * DH : (h + 1) * DH])
        delta = jnp.sum(prob * pgrad, axis=-1, keepdims=True)
        sg = (prob * (pgrad - delta) * SCALE).astype(BF)
        late_ref[:, h * DH : (h + 1) * DH] = dot(
            sg, qk_ref[:, (H + h) * DH : (H + h + 1) * DH]
        ).astype(BF)
        late_ref[:, (H + h) * DH : (H + h + 1) * DH] = dot_tn(
            sg, qk_ref[:, h * DH : (h + 1) * DH]
        ).astype(BF)
        late_ref[:, COL_VG + h * DH : COL_VG + (h + 1) * DH] = vg.astype(BF)
        for e in range(EA):
            i = h * EA + e
            each = jnp.sum(va_ref[:, i * DH : (i + 1) * DH] * vg, axis=1, keepdims=True)
            logits = jnp.where(lane == i, each, logits)
            vag_ref[:, i * DH : (i + 1) * DH] = (col(gate, i) * vg).astype(BF)
    late_ref[:, COL_LG:COL_VG] = (logits * mask_ref[...] * sig * (1.0 - sig)).astype(BF)
    late_ref[:, COL_RG:] = rg_ref[...]


def back_token_kernel(grid, a_tags, idx, x_ref, rg_ref, late_ref, vag_ref, *rest):
    na = len(a_tags)
    a_refs = rest[:na]
    gt_ref, wa, wv, sem_a, sem_v = rest[na:]
    get_a = fetch_rows(grid, idx, a_refs, a_tags, wa, sem_a)
    get_v = fetch_rows(grid, idx, a_refs, a_tags, wv, sem_v, COL_VALUES)
    unit, inverse = norm_stats(x_ref[...].astype(F32))
    wait_all(get_a)
    n1g = dot_nt(late_ref[:, :COL_VG], wa[:, :COL_ROUTER])
    b = n1g * gain_row(wa[:, COL_SEL:COL_ROUTER], LANE_GAIN_ONE)
    wait_all(get_v)
    gt_ref[...] = rg_ref[...] + dot_nt(vag_ref[...], wv[...]) + norm_back(b, unit, inverse)


def stacked(refs, first=0, last=None):
    return jnp.concatenate([r[:, first:last] for r in refs], axis=0)


def in_order(grid, idx, ref, first=0, size=None):
    size = ref.shape[2] - first if size is None else size
    return jnp.concatenate(
        [ref[shard_at(grid, idx, k, r), :, pl.ds(first, size)] for k, r in dp_tags(grid)], axis=0
    )


def by_owner(grid, idx, out_refs, value, first=0):
    X, Z = grid.X, grid.Z
    mine = value.shape[0] // (X * Z)
    columns = pl.ds(first, value.shape[1])
    for z in range(Z):
        blocks = [value[(z * X + x) * mine : (z * X + x + 1) * mine] for x in range(X)]
        for j in range(X):
            chosen = blocks[0]
            for x in range(1, X):
                chosen = jnp.where(lax.rem(idx[3] + j, X) == x, blocks[x], chosen)
            out_refs[j][z, :, columns] = chosen.astype(BF)


def grad_out_kernel(grid, idx, early, *refs):
    nd = grid.nd
    bgs, out = refs[:nd], refs[nd:]
    wide = H * DH
    gate = in_order(grid, idx, early, wide)
    att = in_order(grid, idx, early, 0, wide)
    by_owner(grid, idx, out, dot_tn(stacked(bgs), mixed_of(gate, att, HE)))


def own_columns(grid, idx, cols, which):
    piece = cols.shape[2] // (3 * grid.nd)
    at = which * piece * grid.nd + shard_at(grid, idx, 0, 0) * piece
    return in_order(grid, idx, cols, pl.multiple_of(at, piece), piece)


def grad_rest_kernel(grid, idx, cols, early, a_ref, *refs):
    nd = grid.nd
    late, out = refs[:nd], refs[nd:]
    x, n1, n2 = [own_columns(grid, idx, cols, i) for i in range(3)]
    acts = stacked(late)
    both = dot_tn(n1, acts[:, :COL_VG])
    by_owner(grid, idx, out, both[:, :COL_SEL])
    misc = a_ref[:, COL_SEL:COL_ROUTER].astype(F32)
    stats = in_order(grid, idx, early, H * DH)
    unit = (x.astype(F32) - col(stats, LANE_MEAN)) * col(stats, LANE_INVERSE)
    n1_grad = dot_nt(acts[:, :COL_VG], a_ref[:, :COL_ROUTER])
    n2_grad = dot_nt(acts[:, COL_RG:], a_ref[:, COL_ROUTER:])
    one = jnp.sum(n1_grad * unit, axis=0, keepdims=True)
    gains = jnp.transpose(misc)[LANE_GAIN_TWO : LANE_GAIN_TWO + 1]
    two = jnp.sum(n2_grad * n2.astype(F32), axis=0, keepdims=True) / gains
    row = rows_of((LANES, one.shape[1]))
    extra = jnp.where(row == LANE_GAIN_ONE, one, 0.0)
    extra = jnp.where(row == LANE_GAIN_TWO, two, extra)
    by_owner(grid, idx, out, both[:, COL_SEL:] + jnp.transpose(extra), COL_SEL)
    by_owner(grid, idx, out, dot_tn(n2, acts[:, COL_RG:]), COL_ROUTER)
    mixed = mixed_of(stats, acts[:, COL_VG:COL_RG].astype(F32), 0)
    by_owner(grid, idx, out, dot_tn(x, mixed), COL_VALUES)


def finish_kernel(*refs):
    parts, (q, k, v, vs, os, router, one, two) = refs[:-8], refs[-8:]
    total = parts[0][...].astype(F32)
    for ref in parts[1:]:
        total = total + ref[...].astype(F32)
    wide = H * DH
    q[...] = total[:, :wide]
    k[...] = total[:, wide:COL_SEL]
    misc = total[:, COL_SEL:COL_ROUTER]
    turned = jnp.transpose(misc)
    vs[...] = turned[:HE]
    os[...] = turned[HE : 2 * HE]
    one[...] = turned[LANE_GAIN_ONE : LANE_GAIN_ONE + 1]
    two[...] = turned[LANE_GAIN_TWO : LANE_GAIN_TWO + 1]
    router[...] = total[:, COL_ROUTER:COL_VALUES]
    v[...] = total[:, COL_VALUES:]


def shape(dims, dtype):
    return jax.ShapeDtypeStruct(dims, dtype)


def call(name, kernel, operands, specs, outs, scratch=(), mib=58, us=5, aliases=None):
    outs = [o if isinstance(o, tuple) else (o, VMEM) for o in outs]
    operands = [
        o if s is SMEM else pltpu.with_memory_space_constraint(o, pltpu.HBM)
        for o, s in zip(operands, specs, strict=True)
    ]
    return pl.pallas_call(
        kernel,
        out_shape=tuple(pltpu.HBM(o[0].shape, o[0].dtype) for o in outs),
        in_specs=list(specs),
        out_specs=tuple(o[1] for o in outs),
        scratch_shapes=list(scratch),
        input_output_aliases=aliases or {},
        compiler_params=pltpu.CompilerParams(vmem_limit_bytes=mib * 1024 * 1024),
        cost_estimate=pl.CostEstimate(
            flops=us, bytes_accessed=us, transcendentals=0
        ),
        name=name,
    )(*operands)


def dma(n):
    return pltpu.SemaphoreType.DMA((n,))


def per_device(
    nd,
    ne,
    tokens,
    cotangent,
    segments,
    value_picks,
    output_picks,
    expert_picks,
    attn_gain,
    query_weight,
    key_weight,
    value_weight,
    output_expert_weight,
    value_select,
    output_select,
    moe_gain,
    router_weight,
    up_weight,
    down_weight,
):
    grid = Grid(nd, ne)
    X, Y, Z, C = grid.X, grid.Y, grid.Z, grid.C
    micros, length, width = tokens.shape
    rows = micros * length
    local = up_weight.shape[0]
    piece = width // nd
    wide = H * DH
    values_wide = HE * DH
    dp, ex = lax.axis_index("dp"), lax.axis_index("expert")
    idx = jnp.stack([dp // C, dp % C, ex // X, ex % X]).astype(jnp.int32)


    x_all = tokens.reshape(rows, width)
    g_all = cotangent.reshape(rows, width)

    ends = (*STARTS[1:], COL_A)
    block_w, block_a, *parts_a = call(
        "pack",
        functools.partial(pack_kernel, grid),
        (
            idx,
            query_weight,
            key_weight,
            value_select.T,
            output_select.T,
            attn_gain,
            moe_gain,
            router_weight,
            value_weight,
            output_expert_weight,
        ),
        [SMEM] + [VMEM] * 9,
        [shape((piece, COL_A), BF), shape((piece, COL_VALUES), BF)]
        + [shape((piece // X, high - low), BF) for low, high in zip(STARTS, ends)],
        [pltpu.VMEM((LANES, piece), F32)],
        us=3,
    )

    def to_y(v, *deps):
        v = after(v, *deps)
        return [grid.rot_y(v, k) for k in range(1, Y)]

    def over_x(got_y, *deps):
        return [[v] + [grid.rot_x(after(v, *deps), j) for j in range(1, X)] for v in got_y]

    def add_pieces(arrays, tags, v, tag, swapped=None):
        k, split, j, column = tag
        arrays.append(v)
        tags.append((k, 0, split, j, column))
        if C > 1:
            arrays.append(grid.swap(v) if swapped is None else swapped)
            tags.append((k, 1, split, j, column))

    def swap(v, *deps):
        return grid.swap(after(v, *deps)) if C > 1 else None

    def spread_x(got_y, *deps):
        return [[v] + [grid.rot_x(after(v, *deps), j) for j in range(1, X)] for v in got_y]

    def swap_all(values, *deps):
        return [swap(v, *deps) for v in values]

    def flat(by_k):
        return [v for by_j in by_k for v in by_j]

    g_gathered = lax.all_gather(g_all, "expert", axis=0, tiled=True)
    swap_w = swap(block_w)
    seg = segments.reshape(1, rows)
    v_picks, o_picks = value_picks.reshape(rows, 2 * H), output_picks.reshape(rows, 2 * H)
    e_picks = expert_picks.reshape(rows, -1)
    done = [swap_w, seg, v_picks, o_picks, e_picks]
    over_y, over_x_too, swap_y, swap_x = [to_y(parts_a[0])], [], [], []
    done.append(over_y[0])
    swap_d = swap_u = d_y = None
    for i in range(len(STARTS)):
        last_round = i == len(STARTS) - 1
        new = []
        if not last_round:
            over_y.append(to_y(parts_a[i + 1], *done))
            new += over_y[-1]
        else:
            d_y = to_y(down_weight, *done)
            swap_u = swap(up_weight, *done)
            new += [swap_u, g_gathered]
        if i == len(STARTS) - 2:
            swap_d = swap(down_weight, *done)
            new.append(swap_d)
        over_x_too.append(spread_x(over_y[i], *done))
        swap_y.append(swap_all(over_y[i], *done))
        new += flat(over_x_too[-1]) + swap_y[-1]
        if i:
            swap_x.append([swap_all(by_j[1:], *done) for by_j in over_x_too[i - 1]])
            new += flat(swap_x[-1])
        done = new
    def weight_pieces(own, swapped, chunks):
        arrays, tags = [own, swapped], [(0, 0, None, 0, 0), (0, 1, None, 0, 0)]
        for column, got, others in chunks:
            for k, (by_j, swaps) in enumerate(zip(got, others), 1):
                for j, (v, o) in enumerate(zip(by_j, swaps)):
                    split = "x" if len(by_j) > 1 else None
                    arrays += [v, o]
                    tags += [(k, 0, split, j, column), (k, 1, split, j, column)]
        return arrays, tags

    def all_chunks():
        return [
            (low, got, [[v] + more for v, more in zip(ys, xs)])
            for low, got, ys, xs in zip(STARTS, over_x_too, swap_y, swap_x)
        ]

    first_pieces, first_tags = weight_pieces(block_w, swap_w, all_chunks()[:1])

    n1, qk, sig, mask, probs, wmr = call(
        "attend",
        functools.partial(attend_kernel, grid, first_tags, length),
        (
            idx,
            x_all,
            seg,
            v_picks,
            o_picks,
            *first_pieces,
        ),
        [SMEM] + [VMEM] * 4 + [ANY] * len(first_pieces),
        [
            shape((rows, width), BF),
            shape((rows, 2 * wide), BF),
            shape((rows, LANES), F32),
            shape((rows, LANES), F32),
            shape((rows, H * rows), F32),
            shape((width, 2 * LANES), BF),
        ],
        [pltpu.VMEM((width, COL_VALUES), BF), dma(len(first_pieces))],
        us=4,
    )
    swap_x.append([swap_all(by_j[1:], n1, *done) for by_j in over_x_too[-1]])
    a_pieces, a_tags = weight_pieces(block_w, swap_w, all_chunks())
    v_pieces, v_tags = window(a_pieces, a_tags, COL_VALUES, COL_OUT)
    o_pieces, o_tags = window(a_pieces, a_tags, COL_OUT, COL_A)
    vals, va, early, res, router, picked, xg, cols = call(
        "route",
        functools.partial(route_kernel, grid, v_tags, o_tags),
        (idx, x_all, n1, sig, mask, probs, wmr, e_picks, *v_pieces, *o_pieces),
        [SMEM] + [VMEM] * 7 + [ANY] * (len(v_pieces) + len(o_pieces)),
        [
            shape((rows, wide), BF),
            shape((rows, values_wide), F32),
            shape((rows, wide + LANES), F32),
            shape((rows, width), F32),
            shape((rows, EXPERTS), F32),
            shape((rows, EXPERTS), F32),
            shape((rows, width + EXPERTS), BF),
            shape((rows, 3 * width), BF),
        ],
        [
            pltpu.VMEM((width, values_wide), BF),
            pltpu.VMEM((width, values_wide), BF),
            dma(len(v_pieces)),
            dma(len(o_pieces)),
        ],
        us=8,
    )

    group = ne * length
    ff = local * LANES
    swap_dy = swap_all(d_y, xg)
    u_y = to_y(up_weight, xg, *d_y)
    column, x_over, done = [xg], [], []
    for k in range(1, Z):
        held = after(column[-1], *done)
        column.append(grid.rot_z(held, 1))
        x_over.append([grid.rot_x(held, j) for j in range(1, X)])
        last_done, done = done, [column[-1], x_over[-1]]
    ring_done = done

    def expert_pieces(own, swapped, got, others):
        arrays, tags = [own, swapped], [(0, 0, 0), (0, 1, 0)]
        for k, (v, o) in enumerate(zip(got, others), 1):
            arrays += [v, o]
            tags += [(k, 0, 0), (k, 1, 0)]
        return arrays, tags

    d_pieces, d_tags = expert_pieces(down_weight, swap_d, d_y, swap_dy)
    g_rows = g_gathered.reshape(ne, micros, length, width)
    total = micros * group
    (ahead,) = call(
        "ahead",
        functools.partial(ahead_kernel, grid, d_tags),
        (idx, after(g_rows, *last_done), *d_pieces),
        [SMEM] + [ANY] * (1 + len(d_tags)),
        [(shape((total, ff), BF), ANY)],
        [
            pltpu.VMEM((ne, micros, length, width), BF),
            pltpu.VMEM((local, LANES, width), BF),
            pltpu.VMEM((total, ff), BF),
            dma(1),
            dma(len(d_tags)),
            dma(local // 2),
        ],
        us=9,
    )
    x_over.append([grid.rot_x(after(column[-1], ahead, *ring_done), j) for j in range(1, X)])
    x_pieces = column + [by_j[j] for j in range(X - 1) for by_j in x_over]
    swap_uy = swap_all(u_y, *flat(x_over))
    u_pieces, u_tags = expert_pieces(up_weight, swap_u, u_y, swap_uy)
    froms = []

    def over_x(parts):
        return [grid.rot_x(parts[j], -j) for j in range(1, X)]

    def fold(parts, others, *deps):
        return call(
            "fold",
            fold_kernel,
            (idx, after(parts[0], *deps), *others),
            [SMEM] + [VMEM] * X,
            [shape(parts[0].shape[1:], BF)] * Z,
            us=2,
        )

    sent, shared = [], []
    for m in range(micros):
        hg, pg, x_group, *back = call(
            "experts",
            functools.partial(expert_kernel, grid, u_tags, m, micros),
            (idx, ahead, *x_pieces, *u_pieces, *shared),
            [SMEM, ANY] + [ANY] * (ne + len(u_tags) + len(shared)),
            [
                (shape((total, ff), BF), ANY),
                (shape((total, ff), BF), ANY),
                (shape((total, width + EXPERTS), BF), ANY),
                *[shape((Z, length, width + EXPERTS), BF)] * X,
            ],
            [
                pltpu.VMEM((group, ff), BF),
                pltpu.VMEM((group, ff), BF),
                pltpu.VMEM((group, width + EXPERTS), BF),
                pltpu.VMEM((group, ff), BF),
                pltpu.VMEM((local, width, LANES), BF),
                pltpu.VMEM((group, EXPERTS), F32),
                pltpu.VMEM((group, max(piece, EXPERTS)), F32),
                dma(ne),
                dma(len(u_tags)),
                dma(1),
                dma(3),
            ],
            us=12,
            aliases={2 + ne + len(u_tags) + i: i for i in range(len(shared))},
        )
        shared = [hg, pg, x_group]
        sent.append(back)

    def out_rows(*deps):
        return call(
            "out",
            functools.partial(out_kernel, grid, d_tags, micros),
            (idx, after(hg, *deps), *d_pieces),
            [SMEM] + [ANY] * (1 + len(d_tags)),
            [shape((ne, rows, width), BF)],
            [
                pltpu.VMEM((total, ff), BF),
                pltpu.VMEM((local, LANES, width), BF),
                dma(1),
                dma(len(d_tags)),
            ],
            us=10,
        )

    def expert_grad(name, kernel, lhs, rhs, dims, *deps):
        halves = 2
        block = pl.BlockSpec((Y, local // halves, *dims), lambda h, idx: (0, h, 0, 0))
        if lhs.ndim == 4:
            whole = pl.BlockSpec((ne, micros, length, width), lambda h, idx: (0, 0, 0, 0))
        else:
            whole = pl.BlockSpec((total, width), lambda h, idx: (0, 0))
        part = (width, ff // halves) if lhs.ndim == 2 else (ff // halves, width)
        return pl.pallas_call(
            functools.partial(kernel, grid),
            out_shape=[pltpu.HBM((Y, local, *dims), BF)] * C,
            grid_spec=pltpu.PrefetchScalarGridSpec(
                num_scalar_prefetch=1,
                grid=(halves,),
                in_specs=[whole, pl.BlockSpec((total, ff // halves), lambda h, idx: (0, h))],
                out_specs=[block] * C,
                scratch_shapes=[pltpu.VMEM(part, F32)],
            ),
            compiler_params=pltpu.CompilerParams(vmem_limit_bytes=58 * 1024 * 1024),
            cost_estimate=pl.CostEstimate(flops=4, bytes_accessed=12, transcendentals=0),
            name=name,
        )(idx, *[pltpu.with_memory_space_constraint(v, pltpu.HBM) for v in (after(lhs, *deps), rhs)])

    def added_blocks(name, arrays, dtype, split):
        steps = 2
        dims = arrays[0].shape[1:] if split else arrays[0].shape
        some = (dims[0] // steps, *dims[1:])
        one = pl.BlockSpec(some, lambda i: (i, 0, 0))
        spec = pl.BlockSpec((Y, *some), lambda i: (0, i, 0, 0)) if split else one
        results = Y if split else 1

        def kernel(*refs):
            for k, out in enumerate(refs[len(arrays) :]):
                total = 0.0
                for ref in refs[: len(arrays)]:
                    total = total + (ref[k] if split else ref[...]).astype(F32)
                out[...] = total.astype(dtype)

        return pl.pallas_call(
            kernel,
            out_shape=[pltpu.HBM(dims, dtype)] * results,
            grid=(steps,),
            in_specs=[spec] * len(arrays),
            out_specs=[one] * results,
            compiler_params=pltpu.CompilerParams(vmem_limit_bytes=58 * 1024 * 1024),
            cost_estimate=pl.CostEstimate(flops=1, bytes_accessed=3, transcendentals=0),
            name=name,
        )(*[pltpu.with_memory_space_constraint(v, pltpu.HBM) for v in arrays])

    down_args = ("down_grad", down_grad_kernel, g_rows, hg, (LANES, piece))
    up_args = ("up_grad", up_grad_kernel, x_group, pg, (piece, LANES))

    def reduce_y(total, *deps):
        got = [grid.rot_y(after(total[k], *deps), k) for k in range(1, Y)]
        return lambda *more: added_blocks("last_sum", [after(total[0], *more), *got], F32, False)[0], got

    from_x = [over_x(v) for v in sent]
    sums = fold(sent[0], from_x[0], hg)
    froms.append(grid.send_z(sums))
    outs_sent = out_rows(sums[0])
    before, down_came, up_came = outs_sent[0], [], []
    for m in range(1, micros):
        sums = fold(sent[m], from_x[m], before, froms[-1])
        froms.append(grid.send_z(sums))
        before = sums[0]
    down_near, *down_far = expert_grad(*down_args, before)
    up_near, *up_far = expert_grad(*up_args, down_near)
    before = up_near

    early_all = lax.all_gather(after(early, u_pieces), "dp", axis=0)
    cols_all = lax.all_gather(after(cols, u_pieces), "dp", axis=0)
    res_grad, bg, rg, *bg_cols = call(
        "back_norm",
        functools.partial(back_norm_kernel, grid, micros),
        (
            idx,
            wmr,
            res,
            g_all,
            after(router, before, early_all, cols_all),
            picked,
            *[p for f in froms for p in f],
        ),
        [SMEM] + [VMEM] * (5 + micros * Z),
        [
            shape((rows, width), F32),
            shape((rows, width), BF),
            shape((rows, EXPERTS), BF),
            *[shape((rows, piece), BF)] * nd,
        ],
        us=3,
    )
    bgs = [v if t == (0, 0) else grid.rot_yc(v, *t) for v, t in zip(bg_cols, dp_tags(grid))]
    late, vag = call(
        "back_attend",
        functools.partial(back_attend_kernel, grid, o_tags),
        (idx, bg, rg, sig, mask, early, qk, vals, va, probs, *o_pieces),
        [SMEM] + [VMEM] * 9 + [ANY] * len(o_pieces),
        [shape((rows, COL_LATE), BF), shape((rows, values_wide), BF)],
        [pltpu.VMEM((width, values_wide), BF), dma(len(o_pieces))],
        us=8,
    )
    outs = lax.all_to_all(after(outs_sent[0], bg), "expert", 0, 0, tiled=True)
    down_came, up_came = swap_all(down_far, bg), swap_all(up_far, bg)
    late_swap = swap(late, bgs[1:], *down_came, *up_came)
    late_y = to_y(late, bgs[1:])

    mine = piece // ne

    def weight_grad(name, kernel, operands, columns):
        parts = call(
            name,
            functools.partial(kernel, grid),
            (idx, *operands),
            [SMEM] + [VMEM] * len(operands),
            [shape((Z, mine, columns), BF)] * X,
            us=3,
        )
        return parts, [grid.rot_x(parts[j], j) for j in range(1, X)]

    def fold_at(parts, others, *deps):
        sums = call(
            "fold_at",
            fold_at_kernel,
            (idx, after(parts[0], *deps), *others),
            [SMEM] + [VMEM] * X,
            [shape(parts[0].shape[1:], BF)] * Z,
            us=1,
        )
        return sums[0], grid.send_z(sums)

    def added(parts, *deps):
        return call(
            "sum",
            sum_kernel,
            (after(parts[0], *deps), *parts[1:]),
            [VMEM] * len(parts),
            [shape(parts[0].shape, F32)],
            us=1,
        )[0]

    down_sum = added_blocks("core_sum", [after(down_near, late), *down_came], BF, True)
    up_sum = added_blocks("core_sum", [after(up_near, down_sum), *up_came], BF, True)
    o_parts, o_others = weight_grad(
        "grad_out", grad_out_kernel, [after(early_all, up_sum), *bgs], values_wide
    )
    down_last, down_got = reduce_y(down_sum, late_y)
    up_last, up_got = reduce_y(up_sum, late_y)
    late_all = [late, *late_y, late_swap, *swap_all(late_y, o_parts[0])]
    r_parts, r_others = weight_grad(
        "grad_rest",
        grad_rest_kernel,
        [after(cols_all, o_parts[0]), early_all, block_a, *late_all],
        COL_OUT,
    )
    o_fold, o_sums = fold_at(o_parts, o_others, r_parts[0])
    r_fold, r_sums = fold_at(r_parts, r_others, o_sums, outs)
    grad_down = down_last(r_fold)
    grad_up = up_last(grad_down)
    (grad_tokens,) = call(
        "back_token",
        functools.partial(back_token_kernel, grid, a_tags),
        (idx, x_all, res_grad, after(late, r_fold), vag, *a_pieces),
        [SMEM] + [VMEM] * 4 + [ANY] * len(a_pieces),
        [shape((rows, width), F32)],
        [
            pltpu.VMEM((width, COL_VALUES), BF),
            pltpu.VMEM((width, values_wide), BF),
            dma(len(a_pieces)),
            dma(len(a_pieces)),
        ],
        us=8,
    )
    (output,) = call(
        "add_out",
        sum_places_kernel,
        (outs, after(res, grad_tokens)),
        [VMEM] * 2,
        [shape((rows, width), F32)],
        us=2,
    )
    grad_output = added(o_sums, output)
    q, k, grad_value, vs, os, r, one, two = call(
        "finish",
        finish_kernel,
        (after(r_sums[0], grad_tokens, output, grad_output, grad_up), *r_sums[1:]),
        [VMEM] * Z,
        [
            shape((mine, wide), F32),
            shape((mine, wide), F32),
            shape((mine, values_wide), F32),
            shape((HE, mine), F32),
            shape((HE, mine), F32),
            shape((mine, EXPERTS), F32),
            shape((1, mine), F32),
            shape((1, mine), F32),
        ],
        us=1,
    )
    return (
        output.reshape(micros, length, width),
        grad_tokens.reshape(micros, length, width),
        one.reshape(mine),
        q,
        k,
        grad_value,
        grad_output,
        vs.T,
        os.T,
        two.reshape(mine),
        r,
        grad_up,
        grad_down,
    )


def solution(mesh):
    rows = ("dp", "expert")
    placed = (
        P(None, rows, None),
        P(None, rows, None),
        P(None, rows, None),
        P(None, rows, None, None),
        P(None, rows, None, None),
        P(None, rows, None),
        P("dp"),
        P("dp", None),
        P("dp", None),
        P("dp", None),
        P("dp", None),
        P("dp", None),
        P("dp", None),
        P("dp"),
        P("dp", None),
        P("expert", "dp", None),
        P("expert", None, "dp"),
    )
    return jax.shard_map(
        functools.partial(per_device, mesh.shape["dp"], mesh.shape["expert"]),
        mesh=mesh,
        in_specs=placed,
        out_specs=(
            P(None, rows, None),
            P(None, rows, None),
            P(rows),
            P(rows, None),
            P(rows, None),
            P(rows, None),
            P(rows, None),
            P(rows, None),
            P(rows, None),
            P(rows),
            P(rows, None),
            P("expert", "dp", None),
            P("expert", None, "dp"),
        ),
        check_vma=False,
    )
```

```python
import functools

import jax
import jax.numpy as jnp
from jax import lax
from jax.experimental import pallas as pl
from jax.experimental.pallas import tpu as pltpu
from jax.sharding import PartitionSpec as P

H = 4
DH = 128
EA = 5
HE = H * EA
EXPERTS = 128
EPSILON = 1e-05
MASKED = -1e30
SCALE = DH ** (-0.5)
LANES = 128

BF = jnp.bfloat16
F32 = jnp.float32

COL_SEL = 2 * H * DH
COL_ROUTER = COL_SEL + LANES
COL_VALUES = COL_ROUTER + LANES
COL_OUT = COL_VALUES + HE * DH
COL_A = COL_OUT + HE * DH
STARTS = (0, 17 * LANES, 34 * LANES)
LANE_GAIN_ONE = 2 * HE
LANE_GAIN_TWO = 2 * HE + 1
LANE_MEAN = 2 * HE
LANE_INVERSE = 2 * HE + 1
COL_LG = 2 * H * DH
COL_VG = COL_LG + LANES
COL_RG = COL_VG + H * DH
COL_LATE = COL_RG + LANES

VMEM = pl.BlockSpec()
SMEM = pl.BlockSpec(memory_space=pltpu.SMEM)
ANY = pl.BlockSpec(memory_space=pltpu.HBM)


def dot(a, b):
    return jnp.dot(a, b, preferred_element_type=F32)


def dot_nt(a, b):
    return lax.dot_general(a, b, (((1,), (1,)), ((), ())), preferred_element_type=F32)


def dot_tn(a, b):
    return lax.dot_general(a, b, (((0,), (0,)), ((), ())), preferred_element_type=F32)


def sigmoid(v):
    return 1.0 / (1.0 + jnp.exp(-v))


class Grid:
    def __init__(self, nd, ne):
        self.nd, self.ne = nd, ne
        self.C = 2 if nd % 2 == 0 else 1
        self.Y = nd // self.C
        x = 1
        while (2 * x) * (2 * x) <= ne and ne % (2 * x) == 0:
            x *= 2
        self.X, self.Z = x, ne // x

    def _dp(self, v, go):
        C = self.C
        pairs = []
        for i in range(self.nd):
            y, c = go(i // C, i % C)
            pairs.append((i, y * C + c))
        return lax.ppermute(v, "dp", pairs)

    def _ex(self, v, go):
        X = self.X
        pairs = []
        for i in range(self.ne):
            z, x = go(i // X, i % X)
            pairs.append((i, z * X + x))
        return lax.ppermute(v, "expert", pairs)

    def rot_y(self, v, k):
        return self._dp(v, lambda y, c: ((y + k) % self.Y, c))

    def swap(self, v):
        return self._dp(v, lambda y, c: (y, c ^ 1))

    def rot_yc(self, v, k, r):
        return self._dp(v, lambda y, c: ((y + k) % self.Y, c ^ r))

    def rot_x(self, v, j):
        return self._ex(v, lambda z, x: (z, (x + j) % self.X))

    def rot_z(self, v, k):
        return self._ex(v, lambda z, x: ((z + k) % self.Z, x))

    def lines_z(self):
        return [[z * self.X + x for z in range(self.Z)] for x in range(self.X)]

    def gather_z(self, v):
        return lax.all_gather(v, "expert", axis=0, tiled=True, axis_index_groups=self.lines_z())

    def swap_z(self, v):
        return lax.all_to_all(v, "expert", 0, 0, tiled=True, axis_index_groups=self.lines_z())

    def send_z(self, parts):
        return [parts[0]] + [self.rot_z(parts[k], k) for k in range(1, self.Z)]

    def swap_dp(self, v):
        return lax.all_to_all(v, "dp", 0, 0, tiled=True)


def after(v, *deps):
    flat = [d for dep in deps for d in (dep if isinstance(dep, (list, tuple)) else [dep])]
    if not flat:
        return v
    return lax.optimization_barrier((v, *flat))[0]


def gather_dp(grid, w, over_y, swapped=None):
    got = [w] + list(over_y)
    if grid.C > 1:
        got = got + [grid.swap(w) if swapped is None else swapped] + [grid.swap(v) for v in over_y]
    return got


def dp_tags(grid):
    return [(k, r) for r in range(grid.C) for k in range(grid.Y)]


def shard_at(grid, idx, k, r):
    return lax.rem(idx[0] + (grid.Y - k), grid.Y) * grid.C + lax.rem(idx[1] + r, grid.C)


def fetch_rows(grid, idx, refs, tags, dst, sems, first=0):
    copies = []
    width, last = dst.shape[0] // grid.nd, first + dst.shape[1]
    for i, (ref, (k, r, split, j, column)) in enumerate(zip(refs, tags)):
        low, high = max(first, column), min(last, column + ref.shape[1])
        if low >= high:
            continue
        at = shard_at(grid, idx, k, r) * width
        n = width
        if split is not None:
            size, mine = (grid.X, idx[3]) if split == "x" else (grid.Z, idx[2])
            n = width // size
            at = at + lax.rem(mine + (size - j), size) * n
        at = pl.multiple_of(at, n)
        copy = pltpu.make_async_copy(
            ref.at[:, pl.ds(low - column, high - low)],
            dst.at[pl.ds(at, n), pl.ds(low - first, high - low)],
            sems.at[i],
        )
        copy.start()
        copies.append(copy)
    return copies


def fetch_experts(grid, idx, refs, tags, dst, axis, sems):
    copies = []
    n = dst.shape[axis] // grid.nd
    for i, (ref, (k, r, first)) in enumerate(zip(refs, tags)):
        at = pl.ds(pl.multiple_of(shard_at(grid, idx, k, r) * n, n), n)
        held = pl.ds(first, ref.shape[0])
        place = dst.at[held, at, :] if axis == 1 else dst.at[held, :, at]
        copy = pltpu.make_async_copy(ref, place, sems.at[i])
        copy.start()
        copies.append(copy)
    return copies


def wait_all(copies):
    for copy in copies:
        copy.wait()


def lanes_of(dims):
    return lax.broadcasted_iota(jnp.int32, dims, 1)


def rows_of(dims):
    return lax.broadcasted_iota(jnp.int32, dims, 0)


def norm_stats(v):
    centered = v - jnp.mean(v, axis=-1, keepdims=True)
    inverse = lax.rsqrt(jnp.mean(centered * centered, axis=-1, keepdims=True) + EPSILON)
    return centered * inverse, inverse


def window(pieces, tags, low, high):
    held = [(p, t) for p, t in zip(pieces, tags) if t[4] < high and t[4] + p.shape[1] > low]
    return [p for p, _ in held], [t for _, t in held]


def norm_back(grad, unit, inverse):
    return inverse * (
        grad
        - jnp.mean(grad, axis=-1, keepdims=True)
        - unit * jnp.mean(grad * unit, axis=-1, keepdims=True)
    )


def gain_row(block, lane):
    return jnp.transpose(block.astype(F32))[lane : lane + 1, :]


def col(v, i):
    return v[:, i : i + 1]


def head(v, i):
    return v[:, i * DH : (i + 1) * DH]


def mixed_of(gate, vectors, first):
    return jnp.concatenate(
        [
            (col(gate, first + h * EA + e) * head(vectors, h)).astype(BF)
            for h in range(H)
            for e in range(EA)
        ],
        axis=1,
    )


def pack_kernel(grid, idx, q, k, vs, os, gain_one, gain_two, router, v_ref, o_ref, w_ref, a_ref, *rest):
    parts, misc = rest[:-1], rest[-1]
    piece = q.shape[0]
    nx = piece // grid.X
    at_x = pl.ds(pl.multiple_of(idx[3] * nx, nx), nx)
    misc[...] = jnp.zeros_like(misc)
    misc[:HE, :] = vs[...].astype(F32)
    misc[HE : 2 * HE, :] = os[...].astype(F32)
    misc[LANE_GAIN_ONE : LANE_GAIN_ONE + 1, :] = gain_one[...].astype(F32).reshape(1, piece)
    misc[LANE_GAIN_TWO : LANE_GAIN_TWO + 1, :] = gain_two[...].astype(F32).reshape(1, piece)
    wide = H * DH
    a_ref[:, :wide] = q[...]
    a_ref[:, wide:COL_SEL] = k[...]
    a_ref[:, COL_SEL:COL_ROUTER] = jnp.transpose(misc[...]).astype(BF)
    a_ref[:, COL_ROUTER:] = router[...]
    w_ref[:, :COL_VALUES] = a_ref[...]
    w_ref[:, COL_VALUES:COL_OUT] = v_ref[...]
    w_ref[:, COL_OUT:] = o_ref[...]
    for part, low in zip(parts, STARTS):
        part[...] = w_ref[at_x, low : low + part.shape[1]]


def attend_kernel(grid, tags, length, idx, x_ref, seg_ref, vp, op, *rest):
    n = len(tags)
    a_refs = rest[:n]
    n1_ref, qk_ref, sig_ref, mask_ref, pr_ref, wmr_ref, wa, sem_a = rest[n:]
    get_a = fetch_rows(grid, idx, a_refs, tags, wa, sem_a)
    unit, _ = norm_stats(x_ref[...].astype(F32))
    tokens = unit.shape[0]
    lane = lanes_of((tokens, LANES))
    mask = jnp.zeros((tokens, LANES), F32)
    for h in range(H):
        for k in range(2):
            mask = mask + (lane == col(vp, 2 * h + k) + EA * h).astype(F32)
            mask = mask + (lane == col(op, 2 * h + k) + (EA * h + HE)).astype(F32)
    mask_ref[...] = mask
    square = (tokens, tokens)
    row, lane = rows_of(square), lanes_of(square)
    seg = jnp.broadcast_to(seg_ref[...].astype(F32), square)
    allowed = (seg == jnp.transpose(seg)) & (lane <= row) & (lane // length == row // length)
    wait_all(get_a)
    n1 = (unit * gain_row(wa[:, COL_SEL:COL_ROUTER], LANE_GAIN_ONE)).astype(BF)
    n1_ref[...] = n1
    qks = dot(n1, wa[:, :COL_ROUTER])
    qk = qks[:, :COL_SEL].astype(BF)
    qk_ref[...] = qk
    sig_ref[...] = sigmoid(qks[:, COL_SEL:])
    wmr_ref[...] = wa[:, COL_SEL:]
    for h in range(H):
        scores = dot_nt(head(qk, h), head(qk, H + h))
        scaled = jnp.where(allowed, scores * SCALE, MASKED)
        top = jnp.max(scaled, axis=-1, keepdims=True)
        expo = jnp.where(allowed, jnp.exp(scaled - top), 0.0)
        pr_ref[:, h * tokens : (h + 1) * tokens] = expo / jnp.sum(expo, axis=-1, keepdims=True)


def route_kernel(grid, v_tags, o_tags, idx, x_ref, n1_ref, sig_ref, mask_ref, pr_ref, wmr_ref, ep, *rest):
    nv, no = len(v_tags), len(o_tags)
    v_refs, o_refs = rest[:nv], rest[nv : nv + no]
    rest = rest[nv + no :]
    val_ref, va_ref, early_ref, res_ref, router_ref, picked_ref = rest[:6]
    xg_ref, col_ref, wv, wo, sem_v, sem_o = rest[6:]
    get_v = fetch_rows(grid, idx, v_refs, v_tags, wv, sem_v, COL_VALUES)
    get_o = fetch_rows(grid, idx, o_refs, o_tags, wo, sem_o, COL_OUT)
    gate = sig_ref[...] * mask_ref[...]
    tokens, width = x_ref.shape
    lane = lanes_of((tokens, EXPERTS))
    picked = jnp.zeros((tokens, EXPERTS), F32)
    for k in range(ep.shape[1]):
        picked = picked + (lane == col(ep, k)).astype(F32)
    picked_ref[...] = picked
    x_bf = x_ref[...]
    wait_all(get_v)
    atts = []
    for h in range(H):
        va = dot(x_bf, wv[:, h * EA * DH : (h + 1) * EA * DH])
        va_ref[:, h * EA * DH : (h + 1) * EA * DH] = va
        total = col(gate, h * EA) * head(va, 0)
        for e in range(1, EA):
            total = total + col(gate, h * EA + e) * head(va, e)
        value = total.astype(BF)
        val_ref[:, h * DH : (h + 1) * DH] = value
        atts.append(dot(pr_ref[:, h * tokens : (h + 1) * tokens].astype(BF), value))
    att = jnp.concatenate(atts, axis=1)
    early_ref[:, : H * DH] = att
    mean = jnp.mean(x_bf.astype(F32), axis=-1, keepdims=True)
    centered = x_bf.astype(F32) - mean
    inverse = lax.rsqrt(jnp.mean(centered * centered, axis=-1, keepdims=True) + EPSILON)
    lane = lanes_of((tokens, LANES))
    early_ref[:, H * DH :] = jnp.where(
        lane == LANE_MEAN, mean, jnp.where(lane == LANE_INVERSE, inverse, gate)
    )
    mixed = mixed_of(gate, att, HE)
    wait_all(get_o)
    res = x_bf.astype(F32) + dot_nt(mixed, wo[...])
    res_ref[...] = res
    unit, _ = norm_stats(res)
    n2 = (unit * gain_row(wmr_ref[:, :LANES], LANE_GAIN_TWO)).astype(BF)
    router = sigmoid(dot(n2, wmr_ref[:, LANES:]))
    router_ref[...] = router
    xg_ref[:, :width] = res.astype(BF)
    xg_ref[:, width:] = (router * picked).astype(BF)
    col_ref[:, :width] = x_bf
    col_ref[:, width : 2 * width] = n1_ref[...]
    col_ref[:, 2 * width :] = n2


def ahead_kernel(grid, tags, idx, g_ref, *rest):
    d_refs, (gh_ref, g, down, gh, sem_g, sem_d, sem_o) = rest[: len(tags)], rest[len(tags) :]
    local, width = down.shape[0], down.shape[2]
    micros = g.shape[1]
    get_g = pltpu.make_async_copy(g_ref, g, sem_g.at[0])
    get_g.start()
    get_d = fetch_experts(grid, idx, d_refs, tags, down, 2, sem_d)
    get_g.wait()
    wait_all(get_d)
    group = g.shape[0] * g.shape[2]
    copies = []
    for p in range(local // 2):
        d2 = down[2 * p : 2 * p + 2].reshape(2 * LANES, width)
        columns = pl.ds(p * 2 * LANES, 2 * LANES)
        for m in range(micros):
            gh[m * group : (m + 1) * group, columns] = dot_nt(g[:, m].reshape(group, width), d2).astype(BF)
        copies.append(pltpu.make_async_copy(gh.at[:, columns], gh_ref.at[:, columns], sem_o.at[p]))
        copies[-1].start()
    wait_all(copies)


def place_of(grid, idx, j, k):
    return lax.rem(idx[2] + (grid.Z - k), grid.Z) * grid.X + lax.rem(idx[3] + (grid.X - j), grid.X)


def expert_kernel(grid, tags, micro, micros, idx, gh_ref, *rest):
    n, X, Z, nd, nt = grid.ne, grid.X, grid.Z, grid.nd, len(tags)
    x_refs, u_refs = rest[:n], rest[n : n + nt]
    rest = rest[n + nt + (3 if micro else 0) :]
    hg_ref, pg_ref, xg_ref = rest[:3]
    from_refs = rest[3 : 3 + X]
    hg, pg, xg, gh, up, gg, back, sem_x, sem_u, sem_g, sem_o = rest[3 + X :]
    local, width = up.shape[0], up.shape[1]
    tokens = xg.shape[0]
    rows = tokens // n
    mine = pl.ds(micro * tokens, tokens)
    get_x = []
    for j in range(X):
        for k in range(Z):
            at = pl.multiple_of(place_of(grid, idx, j, k) * rows, rows)
            i = j * Z + k
            get_x.append(
                pltpu.make_async_copy(
                    x_refs[i].at[pl.ds(micro * rows, rows), :], xg.at[pl.ds(at, rows), :], sem_x.at[i]
                )
            )
            get_x[-1].start()
    get_u = fetch_experts(grid, idx, u_refs, tags, up, 1, sem_u)
    get_g = pltpu.make_async_copy(gh_ref.at[mine, :], gh, sem_g.at[0])
    get_g.start()
    first = (idx[2] * X + idx[3]) * local
    gg[...] = jnp.zeros_like(gg)
    lane = lanes_of((tokens, EXPERTS))
    wait_all(get_x)
    copies = [pltpu.make_async_copy(xg, xg_ref.at[mine, :], sem_o.at[0])]
    copies[0].start()
    wait_all(get_u)
    get_g.wait()

    def pair(p, carry):
        w2 = jnp.concatenate([up[2 * p], up[2 * p + 1]], axis=1)
        pre = dot(xg[:, :width], w2)
        columns = pl.ds(pl.multiple_of(p * 2 * LANES, 2 * LANES), 2 * LANES)
        grad = gh[:, columns].astype(F32)
        at = first + 2 * p
        gates = pltpu.roll(xg[:, width:].astype(F32), EXPERTS - at, 1)
        gate = jnp.concatenate(
            [jnp.broadcast_to(col(gates, i), (tokens, LANES)) for i in range(2)], axis=1
        )
        sig = sigmoid(pre)
        hidden = (pre * sig).astype(BF).astype(F32)
        part = hidden * grad
        total = gg[...]
        for i in range(2):
            each = jnp.sum(head(part, i), axis=1, keepdims=True)
            total = total + jnp.where(lane == at + i, each, 0.0)
        gg[...] = total
        hg[:, columns] = (gate * hidden).astype(BF)
        pg[:, columns] = (gate * grad * sig * (1.0 + pre * (1.0 - sig))).astype(BF)
        return carry

    lax.fori_loop(0, local // 2, pair, 0)
    for i, (src, dst) in enumerate(((hg, hg_ref), (pg, pg_ref)), 1):
        copies.append(pltpu.make_async_copy(src, dst.at[mine, :], sem_o.at[i]))
        copies[-1].start()
    piece = width // nd

    def blocks(columns):
        for j in range(X):
            for k in range(Z):
                at = pl.multiple_of(place_of(grid, idx, j, k) * rows, rows)
                from_refs[j][k, :, columns] = back[pl.ds(at, rows), : columns.size].astype(BF)

    for q in range(nd):
        columns = pl.ds(q * piece, piece)
        w = jnp.concatenate([up[e, columns, :] for e in range(local)], axis=1)
        back[:, :piece] = dot_nt(pg[...], w)
        blocks(columns)
    back[:, :EXPERTS] = gg[...]
    blocks(pl.ds(width, EXPERTS))
    wait_all(copies)


def out_kernel(grid, tags, micros, idx, hg_ref, *rest):
    nd, nt = grid.nd, len(tags)
    d_refs, (out_ref, hg, down, sem_g, sem_d) = rest[:nt], rest[nt:]
    local, width = down.shape[0], down.shape[2]
    group = hg.shape[0] // micros
    rows = group // grid.ne
    piece = width // nd
    get_d = fetch_experts(grid, idx, d_refs, tags, down, 2, sem_d)
    get_g = pltpu.make_async_copy(hg_ref, hg, sem_g.at[0])
    get_g.start()
    wait_all(get_d)
    get_g.wait()
    for q in range(nd):
        columns = pl.ds(q * piece, piece)
        back = dot(hg[...], down[:, :, columns].reshape(local * LANES, piece)).astype(BF)
        for e in range(grid.ne):
            for m in range(micros):
                at = m * group + e * rows
                out_ref[e, m * rows : (m + 1) * rows, columns] = back[at : at + rows]


def to_dp_place(grid, idx, k, r, piece):
    at = lax.rem(idx[0] + k, grid.Y) * grid.C + lax.rem(idx[1] + r, grid.C)
    return pl.ds(pl.multiple_of(at * piece, piece), piece)


def up_grad_kernel(grid, idx, x_ref, pg_ref, *rest):
    outs, acc = rest[:-1], rest[-1]
    acc[...] = dot_tn(x_ref[...], pg_ref[...])
    piece = outs[0].shape[2]
    for k, r in dp_tags(grid):
        rows = to_dp_place(grid, idx, k, r, piece)
        for e in range(outs[r].shape[1]):
            outs[r][k, e] = acc[rows, e * LANES : (e + 1) * LANES].astype(BF)


def down_grad_kernel(grid, idx, g_ref, hg_ref, *rest):
    outs, acc = rest[:-1], rest[-1]
    places, micros, rows, width = g_ref.shape
    g = jnp.concatenate([g_ref[:, m].reshape(places * rows, width) for m in range(micros)], axis=0)
    acc[...] = dot_tn(hg_ref[...], g)
    piece = outs[0].shape[3]
    for k, r in dp_tags(grid):
        columns = to_dp_place(grid, idx, k, r, piece)
        for e in range(outs[r].shape[1]):
            outs[r][k, e] = acc[e * LANES : (e + 1) * LANES, columns].astype(BF)


def fold_kernel(idx, own, *refs):
    Z = own.shape[0]
    others, out = refs[:-Z], refs[-Z:]
    del idx
    for k in range(Z):
        at = (Z - k) % Z
        total = own[at].astype(F32)
        for ref in others:
            total = total + ref[at].astype(F32)
        out[k][...] = total.astype(BF)


def fold_at_kernel(idx, own, *refs):
    Z = own.shape[0]
    others, out = refs[:-Z], refs[-Z:]
    for k in range(Z):
        at = lax.rem(idx[2] + k, Z)
        total = own[at].astype(F32)
        for ref in others:
            total = total + ref[at].astype(F32)
        out[k][...] = total.astype(BF)


def sum_kernel(*refs):
    total = refs[0][...].astype(F32)
    for ref in refs[1:-1]:
        total = total + ref[...].astype(F32)
    refs[-1][...] = total


def sum_places_kernel(parts, own, out):
    total = own[...]
    for z in range(parts.shape[0]):
        total = total + parts[z].astype(F32)
    out[...] = total


def back_norm_kernel(grid, micros, idx, wmr_ref, res_ref, g_ref, router_ref, picked_ref, *rest):
    nd, Z = grid.nd, grid.Z
    n = micros * Z
    rg_ref, bg_ref, late_ref = rest[n : n + 3]
    cols = rest[n + 3 :]
    width = res_ref.shape[1]
    parts = []
    for m in range(micros):
        total = rest[m * Z][...].astype(F32)
        for ref in rest[m * Z + 1 : (m + 1) * Z]:
            total = total + ref[...].astype(F32)
        parts.append(total)
    back = jnp.concatenate(parts, axis=0)
    router = router_ref[...]
    late = (back[:, width:] * picked_ref[...] * router * (1.0 - router)).astype(BF)
    late_ref[...] = late
    unit, inverse = norm_stats(res_ref[...])
    n2g = dot_nt(late, wmr_ref[:, LANES:])
    a = n2g * gain_row(wmr_ref[:, :LANES], LANE_GAIN_TWO)
    res_grad = g_ref[...].astype(F32) + back[:, :width] + norm_back(a, unit, inverse)
    rg_ref[...] = res_grad
    bg_ref[...] = res_grad.astype(BF)
    piece = width // nd
    for ref, (k, r) in zip(cols, dp_tags(grid)):
        at = lax.rem(idx[0] + k, grid.Y) * grid.C + lax.rem(idx[1] + r, grid.C)
        ref[...] = bg_ref[:, pl.ds(pl.multiple_of(at * piece, piece), piece)]


def back_attend_kernel(grid, tags, idx, bg_ref, rg_ref, sig_ref, mask_ref, early_ref, qk_ref, val_ref, va_ref,
                       pr_ref, *rest):
    n = len(tags)
    o_refs = rest[:n]
    late_ref, vag_ref, wo, sem_o = rest[n:]
    get_o = fetch_rows(grid, idx, o_refs, tags, wo, sem_o, COL_OUT)
    bg = bg_ref[...]
    tokens = bg.shape[0]
    sig, gate = sig_ref[...], early_ref[:, H * DH :]
    lane = lanes_of((tokens, LANES))
    logits = jnp.zeros((tokens, LANES), F32)
    wait_all(get_o)
    for h in range(H):
        att = early_ref[:, h * DH : (h + 1) * DH]
        mg = dot(bg, wo[:, h * EA * DH : (h + 1) * EA * DH])
        ag = jnp.zeros((tokens, DH), F32)
        for e in range(EA):
            i = HE + h * EA + e
            ag = ag + col(gate, i) * head(mg, e)
            each = jnp.sum(head(mg, e) * att, axis=1, keepdims=True)
            logits = jnp.where(lane == i, each, logits)
        ag = ag.astype(BF)
        prob = pr_ref[:, h * tokens : (h + 1) * tokens]
        vg = dot_tn(prob.astype(BF), ag)
        pgrad = dot_nt(ag, val_ref[:, h * DH : (h + 1) * DH])
        delta = jnp.sum(prob * pgrad, axis=-1, keepdims=True)
        sg = (prob * (pgrad - delta) * SCALE).astype(BF)
        late_ref[:, h * DH : (h + 1) * DH] = dot(
            sg, qk_ref[:, (H + h) * DH : (H + h + 1) * DH]
        ).astype(BF)
        late_ref[:, (H + h) * DH : (H + h + 1) * DH] = dot_tn(
            sg, qk_ref[:, h * DH : (h + 1) * DH]
        ).astype(BF)
        late_ref[:, COL_VG + h * DH : COL_VG + (h + 1) * DH] = vg.astype(BF)
        for e in range(EA):
            i = h * EA + e
            each = jnp.sum(va_ref[:, i * DH : (i + 1) * DH] * vg, axis=1, keepdims=True)
            logits = jnp.where(lane == i, each, logits)
            vag_ref[:, i * DH : (i + 1) * DH] = (col(gate, i) * vg).astype(BF)
    late_ref[:, COL_LG:COL_VG] = (logits * mask_ref[...] * sig * (1.0 - sig)).astype(BF)
    late_ref[:, COL_RG:] = rg_ref[...]


def back_token_kernel(grid, a_tags, idx, x_ref, rg_ref, late_ref, vag_ref, *rest):
    na = len(a_tags)
    a_refs = rest[:na]
    gt_ref, wa, wv, sem_a, sem_v = rest[na:]
    get_a = fetch_rows(grid, idx, a_refs, a_tags, wa, sem_a)
    get_v = fetch_rows(grid, idx, a_refs, a_tags, wv, sem_v, COL_VALUES)
    unit, inverse = norm_stats(x_ref[...].astype(F32))
    wait_all(get_a)
    n1g = dot_nt(late_ref[:, :COL_VG], wa[:, :COL_ROUTER])
    b = n1g * gain_row(wa[:, COL_SEL:COL_ROUTER], LANE_GAIN_ONE)
    wait_all(get_v)
    gt_ref[...] = rg_ref[...] + dot_nt(vag_ref[...], wv[...]) + norm_back(b, unit, inverse)


def stacked(refs, first=0, last=None):
    return jnp.concatenate([r[:, first:last] for r in refs], axis=0)


def in_order(grid, idx, ref, first=0, size=None):
    size = ref.shape[2] - first if size is None else size
    return jnp.concatenate(
        [ref[shard_at(grid, idx, k, r), :, pl.ds(first, size)] for k, r in dp_tags(grid)], axis=0
    )


def by_owner(grid, idx, out_refs, value, first=0):
    X, Z = grid.X, grid.Z
    mine = value.shape[0] // (X * Z)
    columns = pl.ds(first, value.shape[1])
    for z in range(Z):
        blocks = [value[(z * X + x) * mine : (z * X + x + 1) * mine] for x in range(X)]
        for j in range(X):
            chosen = blocks[0]
            for x in range(1, X):
                chosen = jnp.where(lax.rem(idx[3] + j, X) == x, blocks[x], chosen)
            out_refs[j][z, :, columns] = chosen.astype(BF)


def grad_out_kernel(grid, idx, early, *refs):
    nd = grid.nd
    bgs, out = refs[:nd], refs[nd:]
    wide = H * DH
    gate = in_order(grid, idx, early, wide)
    att = in_order(grid, idx, early, 0, wide)
    by_owner(grid, idx, out, dot_tn(stacked(bgs), mixed_of(gate, att, HE)))


def own_columns(grid, idx, cols, which):
    piece = cols.shape[2] // (3 * grid.nd)
    at = which * piece * grid.nd + shard_at(grid, idx, 0, 0) * piece
    return in_order(grid, idx, cols, pl.multiple_of(at, piece), piece)


def grad_rest_kernel(grid, idx, cols, early, a_ref, *refs):
    nd = grid.nd
    late, out = refs[:nd], refs[nd:]
    x, n1, n2 = [own_columns(grid, idx, cols, i) for i in range(3)]
    acts = stacked(late)
    both = dot_tn(n1, acts[:, :COL_VG])
    by_owner(grid, idx, out, both[:, :COL_SEL])
    misc = a_ref[:, COL_SEL:COL_ROUTER].astype(F32)
    stats = in_order(grid, idx, early, H * DH)
    unit = (x.astype(F32) - col(stats, LANE_MEAN)) * col(stats, LANE_INVERSE)
    n1_grad = dot_nt(acts[:, :COL_VG], a_ref[:, :COL_ROUTER])
    n2_grad = dot_nt(acts[:, COL_RG:], a_ref[:, COL_ROUTER:])
    one = jnp.sum(n1_grad * unit, axis=0, keepdims=True)
    gains = jnp.transpose(misc)[LANE_GAIN_TWO : LANE_GAIN_TWO + 1]
    two = jnp.sum(n2_grad * n2.astype(F32), axis=0, keepdims=True) / gains
    row = rows_of((LANES, one.shape[1]))
    extra = jnp.where(row == LANE_GAIN_ONE, one, 0.0)
    extra = jnp.where(row == LANE_GAIN_TWO, two, extra)
    by_owner(grid, idx, out, both[:, COL_SEL:] + jnp.transpose(extra), COL_SEL)
    by_owner(grid, idx, out, dot_tn(n2, acts[:, COL_RG:]), COL_ROUTER)
    mixed = mixed_of(stats, acts[:, COL_VG:COL_RG].astype(F32), 0)
    by_owner(grid, idx, out, dot_tn(x, mixed), COL_VALUES)


def finish_kernel(*refs):
    parts, (q, k, v, vs, os, router, one, two) = refs[:-8], refs[-8:]
    total = parts[0][...].astype(F32)
    for ref in parts[1:]:
        total = total + ref[...].astype(F32)
    wide = H * DH
    q[...] = total[:, :wide]
    k[...] = total[:, wide:COL_SEL]
    misc = total[:, COL_SEL:COL_ROUTER]
    turned = jnp.transpose(misc)
    vs[...] = turned[:HE]
    os[...] = turned[HE : 2 * HE]
    one[...] = turned[LANE_GAIN_ONE : LANE_GAIN_ONE + 1]
    two[...] = turned[LANE_GAIN_TWO : LANE_GAIN_TWO + 1]
    router[...] = total[:, COL_ROUTER:COL_VALUES]
    v[...] = total[:, COL_VALUES:]


def shape(dims, dtype):
    return jax.ShapeDtypeStruct(dims, dtype)


def call(name, kernel, operands, specs, outs, scratch=(), mib=58, us=5, aliases=None):
    outs = [o if isinstance(o, tuple) else (o, VMEM) for o in outs]
    operands = [
        o if s is SMEM else pltpu.with_memory_space_constraint(o, pltpu.HBM)
        for o, s in zip(operands, specs, strict=True)
    ]
    return pl.pallas_call(
        kernel,
        out_shape=tuple(pltpu.HBM(o[0].shape, o[0].dtype) for o in outs),
        in_specs=list(specs),
        out_specs=tuple(o[1] for o in outs),
        scratch_shapes=list(scratch),
        input_output_aliases=aliases or {},
        compiler_params=pltpu.CompilerParams(vmem_limit_bytes=mib * 1024 * 1024),
        cost_estimate=pl.CostEstimate(
            flops=us, bytes_accessed=us, transcendentals=0
        ),
        name=name,
    )(*operands)


def dma(n):
    return pltpu.SemaphoreType.DMA((n,))


def per_device(
    nd,
    ne,
    tokens,
    cotangent,
    segments,
    value_picks,
    output_picks,
    expert_picks,
    attn_gain,
    query_weight,
    key_weight,
    value_weight,
    output_expert_weight,
    value_select,
    output_select,
    moe_gain,
    router_weight,
    up_weight,
    down_weight,
):
    grid = Grid(nd, ne)
    X, Y, Z, C = grid.X, grid.Y, grid.Z, grid.C
    micros, length, width = tokens.shape
    rows = micros * length
    local = up_weight.shape[0]
    piece = width // nd
    wide = H * DH
    values_wide = HE * DH
    dp, ex = lax.axis_index("dp"), lax.axis_index("expert")
    idx = jnp.stack([dp // C, dp % C, ex // X, ex % X]).astype(jnp.int32)


    x_all = tokens.reshape(rows, width)
    g_all = cotangent.reshape(rows, width)

    ends = (*STARTS[1:], COL_A)
    block_w, block_a, *parts_a = call(
        "pack",
        functools.partial(pack_kernel, grid),
        (
            idx,
            query_weight,
            key_weight,
            value_select.T,
            output_select.T,
            attn_gain,
            moe_gain,
            router_weight,
            value_weight,
            output_expert_weight,
        ),
        [SMEM] + [VMEM] * 9,
        [shape((piece, COL_A), BF), shape((piece, COL_VALUES), BF)]
        + [shape((piece // X, high - low), BF) for low, high in zip(STARTS, ends)],
        [pltpu.VMEM((LANES, piece), F32)],
        us=3,
    )

    def to_y(v, *deps):
        v = after(v, *deps)
        return [grid.rot_y(v, k) for k in range(1, Y)]

    def over_x(got_y, *deps):
        return [[v] + [grid.rot_x(after(v, *deps), j) for j in range(1, X)] for v in got_y]

    def add_pieces(arrays, tags, v, tag, swapped=None):
        k, split, j, column = tag
        arrays.append(v)
        tags.append((k, 0, split, j, column))
        if C > 1:
            arrays.append(grid.swap(v) if swapped is None else swapped)
            tags.append((k, 1, split, j, column))

    def swap(v, *deps):
        return grid.swap(after(v, *deps)) if C > 1 else None

    def spread_x(got_y, *deps):
        return [[v] + [grid.rot_x(after(v, *deps), j) for j in range(1, X)] for v in got_y]

    def swap_all(values, *deps):
        return [swap(v, *deps) for v in values]

    def flat(by_k):
        return [v for by_j in by_k for v in by_j]

    g_gathered = lax.all_gather(g_all, "expert", axis=0, tiled=True)
    swap_w = swap(block_w)
    seg = segments.reshape(1, rows)
    v_picks, o_picks = value_picks.reshape(rows, 2 * H), output_picks.reshape(rows, 2 * H)
    e_picks = expert_picks.reshape(rows, -1)
    done = [swap_w, seg, v_picks, o_picks, e_picks]
    over_y, over_x_too, swap_y, swap_x = [to_y(parts_a[0])], [], [], []
    done.append(over_y[0])
    swap_d = swap_u = d_y = None
    for i in range(len(STARTS)):
        last_round = i == len(STARTS) - 1
        new = []
        if not last_round:
            over_y.append(to_y(parts_a[i + 1], *done))
            new += over_y[-1]
        else:
            d_y = to_y(down_weight, *done)
            swap_u = swap(up_weight, *done)
            new += [swap_u, g_gathered]
        if i == len(STARTS) - 2:
            swap_d = swap(down_weight, *done)
            new.append(swap_d)
        over_x_too.append(spread_x(over_y[i], *done))
        swap_y.append(swap_all(over_y[i], *done))
        new += flat(over_x_too[-1]) + swap_y[-1]
        if i:
            swap_x.append([swap_all(by_j[1:], *done) for by_j in over_x_too[i - 1]])
            new += flat(swap_x[-1])
        done = new
    def weight_pieces(own, swapped, chunks):
        arrays, tags = [own, swapped], [(0, 0, None, 0, 0), (0, 1, None, 0, 0)]
        for column, got, others in chunks:
            for k, (by_j, swaps) in enumerate(zip(got, others), 1):
                for j, (v, o) in enumerate(zip(by_j, swaps)):
                    split = "x" if len(by_j) > 1 else None
                    arrays += [v, o]
                    tags += [(k, 0, split, j, column), (k, 1, split, j, column)]
        return arrays, tags

    def all_chunks():
        return [
            (low, got, [[v] + more for v, more in zip(ys, xs)])
            for low, got, ys, xs in zip(STARTS, over_x_too, swap_y, swap_x)
        ]

    first_pieces, first_tags = weight_pieces(block_w, swap_w, all_chunks()[:1])

    n1, qk, sig, mask, probs, wmr = call(
        "attend",
        functools.partial(attend_kernel, grid, first_tags, length),
        (
            idx,
            x_all,
            seg,
            v_picks,
            o_picks,
            *first_pieces,
        ),
        [SMEM] + [VMEM] * 4 + [ANY] * len(first_pieces),
        [
            shape((rows, width), BF),
            shape((rows, 2 * wide), BF),
            shape((rows, LANES), F32),
            shape((rows, LANES), F32),
            shape((rows, H * rows), F32),
            shape((width, 2 * LANES), BF),
        ],
        [pltpu.VMEM((width, COL_VALUES), BF), dma(len(first_pieces))],
        us=4,
    )
    swap_x.append([swap_all(by_j[1:], n1, *done) for by_j in over_x_too[-1]])
    a_pieces, a_tags = weight_pieces(block_w, swap_w, all_chunks())
    v_pieces, v_tags = window(a_pieces, a_tags, COL_VALUES, COL_OUT)
    o_pieces, o_tags = window(a_pieces, a_tags, COL_OUT, COL_A)
    vals, va, early, res, router, picked, xg, cols = call(
        "route",
        functools.partial(route_kernel, grid, v_tags, o_tags),
        (idx, x_all, n1, sig, mask, probs, wmr, e_picks, *v_pieces, *o_pieces),
        [SMEM] + [VMEM] * 7 + [ANY] * (len(v_pieces) + len(o_pieces)),
        [
            shape((rows, wide), BF),
            shape((rows, values_wide), F32),
            shape((rows, wide + LANES), F32),
            shape((rows, width), F32),
            shape((rows, EXPERTS), F32),
            shape((rows, EXPERTS), F32),
            shape((rows, width + EXPERTS), BF),
            shape((rows, 3 * width), BF),
        ],
        [
            pltpu.VMEM((width, values_wide), BF),
            pltpu.VMEM((width, values_wide), BF),
            dma(len(v_pieces)),
            dma(len(o_pieces)),
        ],
        us=8,
    )

    group = ne * length
    ff = local * LANES
    swap_dy = swap_all(d_y, xg)
    u_y = to_y(up_weight, xg, *d_y)
    column, x_over, done = [xg], [], []
    for k in range(1, Z):
        held = after(column[-1], *done)
        column.append(grid.rot_z(held, 1))
        x_over.append([grid.rot_x(held, j) for j in range(1, X)])
        last_done, done = done, [column[-1], x_over[-1]]
    ring_done = done

    def expert_pieces(own, swapped, got, others):
        arrays, tags = [own, swapped], [(0, 0, 0), (0, 1, 0)]
        for k, (v, o) in enumerate(zip(got, others), 1):
            arrays += [v, o]
            tags += [(k, 0, 0), (k, 1, 0)]
        return arrays, tags

    d_pieces, d_tags = expert_pieces(down_weight, swap_d, d_y, swap_dy)
    g_rows = g_gathered.reshape(ne, micros, length, width)
    total = micros * group
    (ahead,) = call(
        "ahead",
        functools.partial(ahead_kernel, grid, d_tags),
        (idx, after(g_rows, *last_done), *d_pieces),
        [SMEM] + [ANY] * (1 + len(d_tags)),
        [(shape((total, ff), BF), ANY)],
        [
            pltpu.VMEM((ne, micros, length, width), BF),
            pltpu.VMEM((local, LANES, width), BF),
            pltpu.VMEM((total, ff), BF),
            dma(1),
            dma(len(d_tags)),
            dma(local // 2),
        ],
        us=9,
    )
    x_over.append([grid.rot_x(after(column[-1], ahead, *ring_done), j) for j in range(1, X)])
    x_pieces = column + [by_j[j] for j in range(X - 1) for by_j in x_over]
    swap_uy = swap_all(u_y, *flat(x_over))
    u_pieces, u_tags = expert_pieces(up_weight, swap_u, u_y, swap_uy)
    froms = []

    def over_x(parts):
        return [grid.rot_x(parts[j], -j) for j in range(1, X)]

    def fold(parts, others, *deps):
        return call(
            "fold",
            fold_kernel,
            (idx, after(parts[0], *deps), *others),
            [SMEM] + [VMEM] * X,
            [shape(parts[0].shape[1:], BF)] * Z,
            us=2,
        )

    sent, shared = [], []
    for m in range(micros):
        hg, pg, x_group, *back = call(
            "experts",
            functools.partial(expert_kernel, grid, u_tags, m, micros),
            (idx, ahead, *x_pieces, *u_pieces, *shared),
            [SMEM, ANY] + [ANY] * (ne + len(u_tags) + len(shared)),
            [
                (shape((total, ff), BF), ANY),
                (shape((total, ff), BF), ANY),
                (shape((total, width + EXPERTS), BF), ANY),
                *[shape((Z, length, width + EXPERTS), BF)] * X,
            ],
            [
                pltpu.VMEM((group, ff), BF),
                pltpu.VMEM((group, ff), BF),
                pltpu.VMEM((group, width + EXPERTS), BF),
                pltpu.VMEM((group, ff), BF),
                pltpu.VMEM((local, width, LANES), BF),
                pltpu.VMEM((group, EXPERTS), F32),
                pltpu.VMEM((group, max(piece, EXPERTS)), F32),
                dma(ne),
                dma(len(u_tags)),
                dma(1),
                dma(3),
            ],
            us=12,
            aliases={2 + ne + len(u_tags) + i: i for i in range(len(shared))},
        )
        shared = [hg, pg, x_group]
        sent.append(back)

    def out_rows(*deps):
        return call(
            "out",
            functools.partial(out_kernel, grid, d_tags, micros),
            (idx, after(hg, *deps), *d_pieces),
            [SMEM] + [ANY] * (1 + len(d_tags)),
            [shape((ne, rows, width), BF)],
            [
                pltpu.VMEM((total, ff), BF),
                pltpu.VMEM((local, LANES, width), BF),
                dma(1),
                dma(len(d_tags)),
            ],
            us=10,
        )

    def expert_grad(name, kernel, lhs, rhs, dims, *deps):
        halves = 2
        block = pl.BlockSpec((Y, local // halves, *dims), lambda h, idx: (0, h, 0, 0))
        if lhs.ndim == 4:
            whole = pl.BlockSpec((ne, micros, length, width), lambda h, idx: (0, 0, 0, 0))
        else:
            whole = pl.BlockSpec((total, width), lambda h, idx: (0, 0))
        part = (width, ff // halves) if lhs.ndim == 2 else (ff // halves, width)
        return pl.pallas_call(
            functools.partial(kernel, grid),
            out_shape=[pltpu.HBM((Y, local, *dims), BF)] * C,
            grid_spec=pltpu.PrefetchScalarGridSpec(
                num_scalar_prefetch=1,
                grid=(halves,),
                in_specs=[whole, pl.BlockSpec((total, ff // halves), lambda h, idx: (0, h))],
                out_specs=[block] * C,
                scratch_shapes=[pltpu.VMEM(part, F32)],
            ),
            compiler_params=pltpu.CompilerParams(vmem_limit_bytes=58 * 1024 * 1024),
            cost_estimate=pl.CostEstimate(flops=4, bytes_accessed=12, transcendentals=0),
            name=name,
        )(idx, *[pltpu.with_memory_space_constraint(v, pltpu.HBM) for v in (after(lhs, *deps), rhs)])

    def added_blocks(name, arrays, dtype, split):
        steps = 2
        dims = arrays[0].shape[1:] if split else arrays[0].shape
        some = (dims[0] // steps, *dims[1:])
        one = pl.BlockSpec(some, lambda i: (i, 0, 0))
        spec = pl.BlockSpec((Y, *some), lambda i: (0, i, 0, 0)) if split else one
        results = Y if split else 1

        def kernel(*refs):
            for k, out in enumerate(refs[len(arrays) :]):
                total = 0.0
                for ref in refs[: len(arrays)]:
                    total = total + (ref[k] if split else ref[...]).astype(F32)
                out[...] = total.astype(dtype)

        return pl.pallas_call(
            kernel,
            out_shape=[pltpu.HBM(dims, dtype)] * results,
            grid=(steps,),
            in_specs=[spec] * len(arrays),
            out_specs=[one] * results,
            compiler_params=pltpu.CompilerParams(vmem_limit_bytes=58 * 1024 * 1024),
            cost_estimate=pl.CostEstimate(flops=1, bytes_accessed=3, transcendentals=0),
            name=name,
        )(*[pltpu.with_memory_space_constraint(v, pltpu.HBM) for v in arrays])

    down_args = ("down_grad", down_grad_kernel, g_rows, hg, (LANES, piece))
    up_args = ("up_grad", up_grad_kernel, x_group, pg, (piece, LANES))

    def reduce_y(total, *deps):
        got = [grid.rot_y(after(total[k], *deps), k) for k in range(1, Y)]
        return lambda *more: added_blocks("last_sum", [after(total[0], *more), *got], F32, False)[0], got

    from_x = [over_x(v) for v in sent]
    sums = fold(sent[0], from_x[0], hg)
    froms.append(grid.send_z(sums))
    outs_sent = out_rows(sums[0])
    before, down_came, up_came = outs_sent[0], [], []
    for m in range(1, micros):
        sums = fold(sent[m], from_x[m], before, froms[-1])
        froms.append(grid.send_z(sums))
        before = sums[0]
    down_near, *down_far = expert_grad(*down_args, before)
    up_near, *up_far = expert_grad(*up_args, down_near)
    before = up_near

    early_all = lax.all_gather(after(early, u_pieces), "dp", axis=0)
    cols_all = lax.all_gather(after(cols, u_pieces), "dp", axis=0)
    res_grad, bg, rg, *bg_cols = call(
        "back_norm",
        functools.partial(back_norm_kernel, grid, micros),
        (
            idx,
            wmr,
            res,
            g_all,
            after(router, before, early_all, cols_all),
            picked,
            *[p for f in froms for p in f],
        ),
        [SMEM] + [VMEM] * (5 + micros * Z),
        [
            shape((rows, width), F32),
            shape((rows, width), BF),
            shape((rows, EXPERTS), BF),
            *[shape((rows, piece), BF)] * nd,
        ],
        us=3,
    )
    bgs = [v if t == (0, 0) else grid.rot_yc(v, *t) for v, t in zip(bg_cols, dp_tags(grid))]
    late, vag = call(
        "back_attend",
        functools.partial(back_attend_kernel, grid, o_tags),
        (idx, bg, rg, sig, mask, early, qk, vals, va, probs, *o_pieces),
        [SMEM] + [VMEM] * 9 + [ANY] * len(o_pieces),
        [shape((rows, COL_LATE), BF), shape((rows, values_wide), BF)],
        [pltpu.VMEM((width, values_wide), BF), dma(len(o_pieces))],
        us=8,
    )
    outs = lax.all_to_all(after(outs_sent[0], bg), "expert", 0, 0, tiled=True)
    down_came, up_came = swap_all(down_far, bg), swap_all(up_far, bg)
    late_swap = swap(late, bgs[1:], *down_came, *up_came)
    late_y = to_y(late, bgs[1:])

    mine = piece // ne

    def weight_grad(name, kernel, operands, columns):
        parts = call(
            name,
            functools.partial(kernel, grid),
            (idx, *operands),
            [SMEM] + [VMEM] * len(operands),
            [shape((Z, mine, columns), BF)] * X,
            us=3,
        )
        return parts, [grid.rot_x(parts[j], j) for j in range(1, X)]

    def fold_at(parts, others, *deps):
        sums = call(
            "fold_at",
            fold_at_kernel,
            (idx, after(parts[0], *deps), *others),
            [SMEM] + [VMEM] * X,
            [shape(parts[0].shape[1:], BF)] * Z,
            us=1,
        )
        return sums[0], grid.send_z(sums)

    def added(parts, *deps):
        return call(
            "sum",
            sum_kernel,
            (after(parts[0], *deps), *parts[1:]),
            [VMEM] * len(parts),
            [shape(parts[0].shape, F32)],
            us=1,
        )[0]

    down_sum = added_blocks("core_sum", [after(down_near, late), *down_came], BF, True)
    up_sum = added_blocks("core_sum", [after(up_near, down_sum), *up_came], BF, True)
    o_parts, o_others = weight_grad(
        "grad_out", grad_out_kernel, [after(early_all, up_sum), *bgs], values_wide
    )
    down_last, down_got = reduce_y(down_sum, late_y)
    up_last, up_got = reduce_y(up_sum, late_y)
    late_all = [late, *late_y, late_swap, *swap_all(late_y, o_parts[0])]
    r_parts, r_others = weight_grad(
        "grad_rest",
        grad_rest_kernel,
        [after(cols_all, o_parts[0]), early_all, block_a, *late_all],
        COL_OUT,
    )
    (grad_tokens,) = call(
        "back_token",
        functools.partial(back_token_kernel, grid, a_tags),
        (idx, x_all, res_grad, after(late, r_parts[0]), vag, *a_pieces),
        [SMEM] + [VMEM] * 4 + [ANY] * len(a_pieces),
        [shape((rows, width), F32)],
        [
            pltpu.VMEM((width, COL_VALUES), BF),
            pltpu.VMEM((width, values_wide), BF),
            dma(len(a_pieces)),
            dma(len(a_pieces)),
        ],
        us=8,
    )
    o_fold, o_sums = fold_at(o_parts, o_others, grad_tokens)
    r_fold, r_sums = fold_at(r_parts, r_others, o_sums, outs)
    grad_down = down_last(r_fold)
    grad_up = up_last(grad_down)
    (output,) = call(
        "add_out",
        sum_places_kernel,
        (outs, after(res, r_fold)),
        [VMEM] * 2,
        [shape((rows, width), F32)],
        us=2,
    )
    grad_output = added(o_sums, output)
    q, k, grad_value, vs, os, r, one, two = call(
        "finish",
        finish_kernel,
        (after(r_sums[0], grad_tokens, output, grad_output, grad_up), *r_sums[1:]),
        [VMEM] * Z,
        [
            shape((mine, wide), F32),
            shape((mine, wide), F32),
            shape((mine, values_wide), F32),
            shape((HE, mine), F32),
            shape((HE, mine), F32),
            shape((mine, EXPERTS), F32),
            shape((1, mine), F32),
            shape((1, mine), F32),
        ],
        us=1,
    )
    return (
        output.reshape(micros, length, width),
        grad_tokens.reshape(micros, length, width),
        one.reshape(mine),
        q,
        k,
        grad_value,
        grad_output,
        vs.T,
        os.T,
        two.reshape(mine),
        r,
        grad_up,
        grad_down,
    )


def solution(mesh):
    rows = ("dp", "expert")
    placed = (
        P(None, rows, None),
        P(None, rows, None),
        P(None, rows, None),
        P(None, rows, None, None),
        P(None, rows, None, None),
        P(None, rows, None),
        P("dp"),
        P("dp", None),
        P("dp", None),
        P("dp", None),
        P("dp", None),
        P("dp", None),
        P("dp", None),
        P("dp"),
        P("dp", None),
        P("expert", "dp", None),
        P("expert", None, "dp"),
    )
    return jax.shard_map(
        functools.partial(per_device, mesh.shape["dp"], mesh.shape["expert"]),
        mesh=mesh,
        in_specs=placed,
        out_specs=(
            P(None, rows, None),
            P(None, rows, None),
            P(rows),
            P(rows, None),
            P(rows, None),
            P(rows, None),
            P(rows, None),
            P(rows, None),
            P(rows, None),
            P(rows),
            P(rows, None),
            P("expert", "dp", None),
            P("expert", None, "dp"),
        ),
        check_vma=False,
    )
```

```python
import functools

import jax
import jax.numpy as jnp
from jax import lax
from jax.experimental import pallas as pl
from jax.experimental.pallas import tpu as pltpu
from jax.sharding import PartitionSpec as P

H = 4
DH = 128
EA = 5
HE = H * EA
EXPERTS = 128
EPSILON = 1e-05
MASKED = -1e30
SCALE = DH ** (-0.5)
LANES = 128

BF = jnp.bfloat16
F32 = jnp.float32

COL_SEL = 2 * H * DH
COL_ROUTER = COL_SEL + LANES
COL_VALUES = COL_ROUTER + LANES
COL_OUT = COL_VALUES + HE * DH
COL_A = COL_OUT + HE * DH
STARTS = (0, 17 * LANES, 34 * LANES)
LANE_GAIN_ONE = 2 * HE
LANE_GAIN_TWO = 2 * HE + 1
LANE_MEAN = 2 * HE
LANE_INVERSE = 2 * HE + 1
COL_LG = 2 * H * DH
COL_VG = COL_LG + LANES
COL_RG = COL_VG + H * DH
COL_LATE = COL_RG + LANES

VMEM = pl.BlockSpec()
SMEM = pl.BlockSpec(memory_space=pltpu.SMEM)
ANY = pl.BlockSpec(memory_space=pltpu.HBM)


def dot(a, b):
    return jnp.dot(a, b, preferred_element_type=F32)


def dot_nt(a, b):
    return lax.dot_general(a, b, (((1,), (1,)), ((), ())), preferred_element_type=F32)


def dot_tn(a, b):
    return lax.dot_general(a, b, (((0,), (0,)), ((), ())), preferred_element_type=F32)


def sigmoid(v):
    return 1.0 / (1.0 + jnp.exp(-v))


class Grid:
    def __init__(self, nd, ne):
        self.nd, self.ne = nd, ne
        self.C = 2 if nd % 2 == 0 else 1
        self.Y = nd // self.C
        x = 1
        while (2 * x) * (2 * x) <= ne and ne % (2 * x) == 0:
            x *= 2
        self.X, self.Z = x, ne // x

    def _dp(self, v, go):
        C = self.C
        pairs = []
        for i in range(self.nd):
            y, c = go(i // C, i % C)
            pairs.append((i, y * C + c))
        return lax.ppermute(v, "dp", pairs)

    def _ex(self, v, go):
        X = self.X
        pairs = []
        for i in range(self.ne):
            z, x = go(i // X, i % X)
            pairs.append((i, z * X + x))
        return lax.ppermute(v, "expert", pairs)

    def rot_y(self, v, k):
        return self._dp(v, lambda y, c: ((y + k) % self.Y, c))

    def swap(self, v):
        return self._dp(v, lambda y, c: (y, c ^ 1))

    def rot_yc(self, v, k, r):
        return self._dp(v, lambda y, c: ((y + k) % self.Y, c ^ r))

    def rot_x(self, v, j):
        return self._ex(v, lambda z, x: (z, (x + j) % self.X))

    def rot_z(self, v, k):
        return self._ex(v, lambda z, x: ((z + k) % self.Z, x))

    def lines_z(self):
        return [[z * self.X + x for z in range(self.Z)] for x in range(self.X)]

    def gather_z(self, v):
        return lax.all_gather(v, "expert", axis=0, tiled=True, axis_index_groups=self.lines_z())

    def swap_z(self, v):
        return lax.all_to_all(v, "expert", 0, 0, tiled=True, axis_index_groups=self.lines_z())

    def send_z(self, parts):
        far = [self.rot_z(parts[k], k) for k in range(self.Z - 1, 0, -1)]
        return [parts[0]] + far[::-1]

    def swap_dp(self, v):
        return lax.all_to_all(v, "dp", 0, 0, tiled=True)


def after(v, *deps):
    flat = [d for dep in deps for d in (dep if isinstance(dep, (list, tuple)) else [dep])]
    if not flat:
        return v
    return lax.optimization_barrier((v, *flat))[0]


def gather_dp(grid, w, over_y, swapped=None):
    got = [w] + list(over_y)
    if grid.C > 1:
        got = got + [grid.swap(w) if swapped is None else swapped] + [grid.swap(v) for v in over_y]
    return got


def dp_tags(grid):
    return [(k, r) for r in range(grid.C) for k in range(grid.Y)]


def shard_at(grid, idx, k, r):
    return lax.rem(idx[0] + (grid.Y - k), grid.Y) * grid.C + lax.rem(idx[1] + r, grid.C)


def fetch_rows(grid, idx, refs, tags, dst, sems, first=0):
    copies = []
    width, last = dst.shape[0] // grid.nd, first + dst.shape[1]
    for i, (ref, (k, r, split, j, column)) in enumerate(zip(refs, tags)):
        low, high = max(first, column), min(last, column + ref.shape[1])
        if low >= high:
            continue
        at = shard_at(grid, idx, k, r) * width
        n = width
        if split is not None:
            size, mine = (grid.X, idx[3]) if split == "x" else (grid.Z, idx[2])
            n = width // size
            at = at + lax.rem(mine + (size - j), size) * n
        at = pl.multiple_of(at, n)
        copy = pltpu.make_async_copy(
            ref.at[:, pl.ds(low - column, high - low)],
            dst.at[pl.ds(at, n), pl.ds(low - first, high - low)],
            sems.at[i],
        )
        copy.start()
        copies.append(copy)
    return copies


def fetch_experts(grid, idx, refs, tags, dst, axis, sems):
    copies = []
    n = dst.shape[axis] // grid.nd
    for i, (ref, (k, r, first)) in enumerate(zip(refs, tags)):
        at = pl.ds(pl.multiple_of(shard_at(grid, idx, k, r) * n, n), n)
        held = pl.ds(first, ref.shape[0])
        place = dst.at[held, at, :] if axis == 1 else dst.at[held, :, at]
        copy = pltpu.make_async_copy(ref, place, sems.at[i])
        copy.start()
        copies.append(copy)
    return copies


def wait_all(copies):
    for copy in copies:
        copy.wait()


def lanes_of(dims):
    return lax.broadcasted_iota(jnp.int32, dims, 1)


def rows_of(dims):
    return lax.broadcasted_iota(jnp.int32, dims, 0)


def norm_stats(v):
    centered = v - jnp.mean(v, axis=-1, keepdims=True)
    inverse = lax.rsqrt(jnp.mean(centered * centered, axis=-1, keepdims=True) + EPSILON)
    return centered * inverse, inverse


def window(pieces, tags, low, high):
    held = [(p, t) for p, t in zip(pieces, tags) if t[4] < high and t[4] + p.shape[1] > low]
    return [p for p, _ in held], [t for _, t in held]


def norm_back(grad, unit, inverse):
    return inverse * (
        grad
        - jnp.mean(grad, axis=-1, keepdims=True)
        - unit * jnp.mean(grad * unit, axis=-1, keepdims=True)
    )


def gain_row(block, lane):
    return jnp.transpose(block.astype(F32))[lane : lane + 1, :]


def col(v, i):
    return v[:, i : i + 1]


def head(v, i):
    return v[:, i * DH : (i + 1) * DH]


def mixed_of(gate, vectors, first):
    return jnp.concatenate(
        [
            (col(gate, first + h * EA + e) * head(vectors, h)).astype(BF)
            for h in range(H)
            for e in range(EA)
        ],
        axis=1,
    )


def pack_kernel(grid, idx, q, k, vs, os, gain_one, gain_two, router, v_ref, o_ref, w_ref, a_ref, *rest):
    parts, misc = rest[:-1], rest[-1]
    piece = q.shape[0]
    nx = piece // grid.X
    at_x = pl.ds(pl.multiple_of(idx[3] * nx, nx), nx)
    misc[...] = jnp.zeros_like(misc)
    misc[:HE, :] = vs[...].astype(F32)
    misc[HE : 2 * HE, :] = os[...].astype(F32)
    misc[LANE_GAIN_ONE : LANE_GAIN_ONE + 1, :] = gain_one[...].astype(F32).reshape(1, piece)
    misc[LANE_GAIN_TWO : LANE_GAIN_TWO + 1, :] = gain_two[...].astype(F32).reshape(1, piece)
    wide = H * DH
    a_ref[:, :wide] = q[...]
    a_ref[:, wide:COL_SEL] = k[...]
    a_ref[:, COL_SEL:COL_ROUTER] = jnp.transpose(misc[...]).astype(BF)
    a_ref[:, COL_ROUTER:] = router[...]
    w_ref[:, :COL_VALUES] = a_ref[...]
    w_ref[:, COL_VALUES:COL_OUT] = v_ref[...]
    w_ref[:, COL_OUT:] = o_ref[...]
    for part, low in zip(parts, STARTS):
        part[...] = w_ref[at_x, low : low + part.shape[1]]


def attend_kernel(grid, tags, length, idx, x_ref, seg_ref, vp, op, *rest):
    n = len(tags)
    a_refs = rest[:n]
    n1_ref, qk_ref, sig_ref, mask_ref, pr_ref, wmr_ref, wa, sem_a = rest[n:]
    get_a = fetch_rows(grid, idx, a_refs, tags, wa, sem_a)
    unit, _ = norm_stats(x_ref[...].astype(F32))
    tokens = unit.shape[0]
    lane = lanes_of((tokens, LANES))
    mask = jnp.zeros((tokens, LANES), F32)
    for h in range(H):
        for k in range(2):
            mask = mask + (lane == col(vp, 2 * h + k) + EA * h).astype(F32)
            mask = mask + (lane == col(op, 2 * h + k) + (EA * h + HE)).astype(F32)
    mask_ref[...] = mask
    square = (tokens, tokens)
    row, lane = rows_of(square), lanes_of(square)
    seg = jnp.broadcast_to(seg_ref[...].astype(F32), square)
    allowed = (seg == jnp.transpose(seg)) & (lane <= row) & (lane // length == row // length)
    wait_all(get_a)
    n1 = (unit * gain_row(wa[:, COL_SEL:COL_ROUTER], LANE_GAIN_ONE)).astype(BF)
    n1_ref[...] = n1
    qks = dot(n1, wa[:, :COL_ROUTER])
    qk = qks[:, :COL_SEL].astype(BF)
    qk_ref[...] = qk
    sig_ref[...] = sigmoid(qks[:, COL_SEL:])
    wmr_ref[...] = wa[:, COL_SEL:]
    for h in range(H):
        scores = dot_nt(head(qk, h), head(qk, H + h))
        scaled = jnp.where(allowed, scores * SCALE, MASKED)
        top = jnp.max(scaled, axis=-1, keepdims=True)
        expo = jnp.where(allowed, jnp.exp(scaled - top), 0.0)
        pr_ref[:, h * tokens : (h + 1) * tokens] = expo / jnp.sum(expo, axis=-1, keepdims=True)


def route_kernel(grid, v_tags, o_tags, idx, x_ref, n1_ref, sig_ref, mask_ref, pr_ref, wmr_ref, ep, *rest):
    nv, no = len(v_tags), len(o_tags)
    v_refs, o_refs = rest[:nv], rest[nv : nv + no]
    rest = rest[nv + no :]
    val_ref, va_ref, early_ref, res_ref, router_ref, picked_ref = rest[:6]
    xg_ref, col_ref, wv, wo, sem_v, sem_o = rest[6:]
    get_v = fetch_rows(grid, idx, v_refs, v_tags, wv, sem_v, COL_VALUES)
    get_o = fetch_rows(grid, idx, o_refs, o_tags, wo, sem_o, COL_OUT)
    gate = sig_ref[...] * mask_ref[...]
    tokens, width = x_ref.shape
    lane = lanes_of((tokens, EXPERTS))
    picked = jnp.zeros((tokens, EXPERTS), F32)
    for k in range(ep.shape[1]):
        picked = picked + (lane == col(ep, k)).astype(F32)
    picked_ref[...] = picked
    x_bf = x_ref[...]
    wait_all(get_v)
    atts = []
    for h in range(H):
        va = dot(x_bf, wv[:, h * EA * DH : (h + 1) * EA * DH])
        va_ref[:, h * EA * DH : (h + 1) * EA * DH] = va
        total = col(gate, h * EA) * head(va, 0)
        for e in range(1, EA):
            total = total + col(gate, h * EA + e) * head(va, e)
        value = total.astype(BF)
        val_ref[:, h * DH : (h + 1) * DH] = value
        atts.append(dot(pr_ref[:, h * tokens : (h + 1) * tokens].astype(BF), value))
    att = jnp.concatenate(atts, axis=1)
    early_ref[:, : H * DH] = att
    mean = jnp.mean(x_bf.astype(F32), axis=-1, keepdims=True)
    centered = x_bf.astype(F32) - mean
    inverse = lax.rsqrt(jnp.mean(centered * centered, axis=-1, keepdims=True) + EPSILON)
    lane = lanes_of((tokens, LANES))
    early_ref[:, H * DH :] = jnp.where(
        lane == LANE_MEAN, mean, jnp.where(lane == LANE_INVERSE, inverse, gate)
    )
    mixed = mixed_of(gate, att, HE)
    wait_all(get_o)
    res = x_bf.astype(F32) + dot_nt(mixed, wo[...])
    res_ref[...] = res
    unit, _ = norm_stats(res)
    n2 = (unit * gain_row(wmr_ref[:, :LANES], LANE_GAIN_TWO)).astype(BF)
    router = sigmoid(dot(n2, wmr_ref[:, LANES:]))
    router_ref[...] = router
    xg_ref[:, :width] = res.astype(BF)
    xg_ref[:, width:] = (router * picked).astype(BF)
    col_ref[:, :width] = x_bf
    col_ref[:, width : 2 * width] = n1_ref[...]
    col_ref[:, 2 * width :] = n2


def ahead_kernel(grid, tags, idx, g_ref, *rest):
    d_refs, (gh_ref, g, down, gh, sem_g, sem_d, sem_o) = rest[: len(tags)], rest[len(tags) :]
    local, width = down.shape[0], down.shape[2]
    micros = g.shape[1]
    get_g = pltpu.make_async_copy(g_ref, g, sem_g.at[0])
    get_g.start()
    get_d = fetch_experts(grid, idx, d_refs, tags, down, 2, sem_d)
    get_g.wait()
    wait_all(get_d)
    group = g.shape[0] * g.shape[2]
    copies = []
    for p in range(local // 2):
        d2 = down[2 * p : 2 * p + 2].reshape(2 * LANES, width)
        columns = pl.ds(p * 2 * LANES, 2 * LANES)
        for m in range(micros):
            gh[m * group : (m + 1) * group, columns] = dot_nt(g[:, m].reshape(group, width), d2).astype(BF)
        copies.append(pltpu.make_async_copy(gh.at[:, columns], gh_ref.at[:, columns], sem_o.at[p]))
        copies[-1].start()
    wait_all(copies)


def place_of(grid, idx, j, k):
    return lax.rem(idx[2] + (grid.Z - k), grid.Z) * grid.X + lax.rem(idx[3] + (grid.X - j), grid.X)


def expert_kernel(grid, tags, micro, micros, idx, gh_ref, *rest):
    n, X, Z, nd, nt = grid.ne, grid.X, grid.Z, grid.nd, len(tags)
    x_refs, u_refs = rest[:n], rest[n : n + nt]
    rest = rest[n + nt + (3 if micro else 0) :]
    hg_ref, pg_ref, xg_ref = rest[:3]
    from_refs = rest[3 : 3 + X]
    hg, pg, xg, gh, up, gg, back, sem_x, sem_u, sem_g, sem_o = rest[3 + X :]
    local, width = up.shape[0], up.shape[1]
    tokens = xg.shape[0]
    rows = tokens // n
    mine = pl.ds(micro * tokens, tokens)
    get_x = []
    for j in range(X):
        for k in range(Z):
            at = pl.multiple_of(place_of(grid, idx, j, k) * rows, rows)
            i = j * Z + k
            get_x.append(
                pltpu.make_async_copy(
                    x_refs[i].at[pl.ds(micro * rows, rows), :], xg.at[pl.ds(at, rows), :], sem_x.at[i]
                )
            )
            get_x[-1].start()
    get_u = fetch_experts(grid, idx, u_refs, tags, up, 1, sem_u)
    get_g = pltpu.make_async_copy(gh_ref.at[mine, :], gh, sem_g.at[0])
    get_g.start()
    first = (idx[2] * X + idx[3]) * local
    gg[...] = jnp.zeros_like(gg)
    lane = lanes_of((tokens, EXPERTS))
    wait_all(get_x)
    copies = [pltpu.make_async_copy(xg, xg_ref.at[mine, :], sem_o.at[0])]
    copies[0].start()
    wait_all(get_u)
    get_g.wait()

    def pair(p, carry):
        w2 = jnp.concatenate([up[2 * p], up[2 * p + 1]], axis=1)
        pre = dot(xg[:, :width], w2)
        columns = pl.ds(pl.multiple_of(p * 2 * LANES, 2 * LANES), 2 * LANES)
        grad = gh[:, columns].astype(F32)
        at = first + 2 * p
        gates = pltpu.roll(xg[:, width:].astype(F32), EXPERTS - at, 1)
        gate = jnp.concatenate(
            [jnp.broadcast_to(col(gates, i), (tokens, LANES)) for i in range(2)], axis=1
        )
        sig = sigmoid(pre)
        hidden = (pre * sig).astype(BF).astype(F32)
        part = hidden * grad
        total = gg[...]
        for i in range(2):
            each = jnp.sum(head(part, i), axis=1, keepdims=True)
            total = total + jnp.where(lane == at + i, each, 0.0)
        gg[...] = total
        hg[:, columns] = (gate * hidden).astype(BF)
        pg[:, columns] = (gate * grad * sig * (1.0 + pre * (1.0 - sig))).astype(BF)
        return carry

    lax.fori_loop(0, local // 2, pair, 0)
    for i, (src, dst) in enumerate(((hg, hg_ref), (pg, pg_ref)), 1):
        copies.append(pltpu.make_async_copy(src, dst.at[mine, :], sem_o.at[i]))
        copies[-1].start()
    piece = width // nd

    def blocks(columns):
        for j in range(X):
            for k in range(Z):
                at = pl.multiple_of(place_of(grid, idx, j, k) * rows, rows)
                from_refs[j][k, :, columns] = back[pl.ds(at, rows), : columns.size].astype(BF)

    for q in range(nd):
        columns = pl.ds(q * piece, piece)
        w = jnp.concatenate([up[e, columns, :] for e in range(local)], axis=1)
        back[:, :piece] = dot_nt(pg[...], w)
        blocks(columns)
    back[:, :EXPERTS] = gg[...]
    blocks(pl.ds(width, EXPERTS))
    wait_all(copies)


def out_kernel(grid, tags, micros, idx, hg_ref, *rest):
    nd, nt = grid.nd, len(tags)
    d_refs, (out_ref, hg, down, sem_g, sem_d) = rest[:nt], rest[nt:]
    local, width = down.shape[0], down.shape[2]
    group = hg.shape[0] // micros
    rows = group // grid.ne
    piece = width // nd
    get_d = fetch_experts(grid, idx, d_refs, tags, down, 2, sem_d)
    get_g = pltpu.make_async_copy(hg_ref, hg, sem_g.at[0])
    get_g.start()
    wait_all(get_d)
    get_g.wait()
    for q in range(nd):
        columns = pl.ds(q * piece, piece)
        back = dot(hg[...], down[:, :, columns].reshape(local * LANES, piece)).astype(BF)
        for e in range(grid.ne):
            for m in range(micros):
                at = m * group + e * rows
                out_ref[e, m * rows : (m + 1) * rows, columns] = back[at : at + rows]


def to_dp_place(grid, idx, k, r, piece):
    at = lax.rem(idx[0] + k, grid.Y) * grid.C + lax.rem(idx[1] + r, grid.C)
    return pl.ds(pl.multiple_of(at * piece, piece), piece)


def up_grad_kernel(grid, idx, x_ref, pg_ref, *rest):
    outs, acc = rest[:-1], rest[-1]
    acc[...] = dot_tn(x_ref[...], pg_ref[...])
    piece = outs[0].shape[2]
    for k, r in dp_tags(grid):
        rows = to_dp_place(grid, idx, k, r, piece)
        for e in range(outs[r].shape[1]):
            outs[r][k, e] = acc[rows, e * LANES : (e + 1) * LANES].astype(BF)


def down_grad_kernel(grid, idx, g_ref, hg_ref, *rest):
    outs, acc = rest[:-1], rest[-1]
    places, micros, rows, width = g_ref.shape
    g = jnp.concatenate([g_ref[:, m].reshape(places * rows, width) for m in range(micros)], axis=0)
    acc[...] = dot_tn(hg_ref[...], g)
    piece = outs[0].shape[3]
    for k, r in dp_tags(grid):
        columns = to_dp_place(grid, idx, k, r, piece)
        for e in range(outs[r].shape[1]):
            outs[r][k, e] = acc[e * LANES : (e + 1) * LANES, columns].astype(BF)


def fold_kernel(idx, own, *refs):
    Z = own.shape[0]
    others, out = refs[:-Z], refs[-Z:]
    del idx
    for k in range(Z):
        at = (Z - k) % Z
        total = own[at].astype(F32)
        for ref in others:
            total = total + ref[at].astype(F32)
        out[k][...] = total.astype(BF)


def fold_at_kernel(idx, own, *refs):
    Z = own.shape[0]
    others, out = refs[:-Z], refs[-Z:]
    for k in range(Z):
        at = lax.rem(idx[2] + k, Z)
        total = own[at].astype(F32)
        for ref in others:
            total = total + ref[at].astype(F32)
        out[k][...] = total.astype(BF)


def sum_kernel(*refs):
    total = refs[0][...].astype(F32)
    for ref in refs[1:-1]:
        total = total + ref[...].astype(F32)
    refs[-1][...] = total


def sum_places_kernel(parts, own, out):
    total = own[...]
    for z in range(parts.shape[0]):
        total = total + parts[z].astype(F32)
    out[...] = total


def back_norm_kernel(grid, micros, idx, wmr_ref, res_ref, g_ref, router_ref, picked_ref, *rest):
    nd, Z = grid.nd, grid.Z
    n = micros * Z
    rg_ref, bg_ref, late_ref = rest[n : n + 3]
    cols = rest[n + 3 :]
    width = res_ref.shape[1]
    parts = []
    for m in range(micros):
        total = rest[m * Z][...].astype(F32)
        for ref in rest[m * Z + 1 : (m + 1) * Z]:
            total = total + ref[...].astype(F32)
        parts.append(total)
    back = jnp.concatenate(parts, axis=0)
    router = router_ref[...]
    late = (back[:, width:] * picked_ref[...] * router * (1.0 - router)).astype(BF)
    late_ref[...] = late
    unit, inverse = norm_stats(res_ref[...])
    n2g = dot_nt(late, wmr_ref[:, LANES:])
    a = n2g * gain_row(wmr_ref[:, :LANES], LANE_GAIN_TWO)
    res_grad = g_ref[...].astype(F32) + back[:, :width] + norm_back(a, unit, inverse)
    rg_ref[...] = res_grad
    bg_ref[...] = res_grad.astype(BF)
    piece = width // nd
    for ref, (k, r) in zip(cols, dp_tags(grid)):
        at = lax.rem(idx[0] + k, grid.Y) * grid.C + lax.rem(idx[1] + r, grid.C)
        ref[...] = bg_ref[:, pl.ds(pl.multiple_of(at * piece, piece), piece)]


def back_attend_kernel(grid, tags, idx, bg_ref, rg_ref, sig_ref, mask_ref, early_ref, qk_ref, val_ref, va_ref,
                       pr_ref, *rest):
    n = len(tags)
    o_refs = rest[:n]
    late_ref, vag_ref, wo, sem_o = rest[n:]
    get_o = fetch_rows(grid, idx, o_refs, tags, wo, sem_o, COL_OUT)
    bg = bg_ref[...]
    tokens = bg.shape[0]
    sig, gate = sig_ref[...], early_ref[:, H * DH :]
    lane = lanes_of((tokens, LANES))
    logits = jnp.zeros((tokens, LANES), F32)
    wait_all(get_o)
    for h in range(H):
        att = early_ref[:, h * DH : (h + 1) * DH]
        mg = dot(bg, wo[:, h * EA * DH : (h + 1) * EA * DH])
        ag = jnp.zeros((tokens, DH), F32)
        for e in range(EA):
            i = HE + h * EA + e
            ag = ag + col(gate, i) * head(mg, e)
            each = jnp.sum(head(mg, e) * att, axis=1, keepdims=True)
            logits = jnp.where(lane == i, each, logits)
        ag = ag.astype(BF)
        prob = pr_ref[:, h * tokens : (h + 1) * tokens]
        vg = dot_tn(prob.astype(BF), ag)
        pgrad = dot_nt(ag, val_ref[:, h * DH : (h + 1) * DH])
        delta = jnp.sum(prob * pgrad, axis=-1, keepdims=True)
        sg = (prob * (pgrad - delta) * SCALE).astype(BF)
        late_ref[:, h * DH : (h + 1) * DH] = dot(
            sg, qk_ref[:, (H + h) * DH : (H + h + 1) * DH]
        ).astype(BF)
        late_ref[:, (H + h) * DH : (H + h + 1) * DH] = dot_tn(
            sg, qk_ref[:, h * DH : (h + 1) * DH]
        ).astype(BF)
        late_ref[:, COL_VG + h * DH : COL_VG + (h + 1) * DH] = vg.astype(BF)
        for e in range(EA):
            i = h * EA + e
            each = jnp.sum(va_ref[:, i * DH : (i + 1) * DH] * vg, axis=1, keepdims=True)
            logits = jnp.where(lane == i, each, logits)
            vag_ref[:, i * DH : (i + 1) * DH] = (col(gate, i) * vg).astype(BF)
    late_ref[:, COL_LG:COL_VG] = (logits * mask_ref[...] * sig * (1.0 - sig)).astype(BF)
    late_ref[:, COL_RG:] = rg_ref[...]


def back_token_kernel(grid, a_tags, idx, x_ref, rg_ref, late_ref, vag_ref, *rest):
    na = len(a_tags)
    a_refs = rest[:na]
    gt_ref, wa, wv, sem_a, sem_v = rest[na:]
    get_a = fetch_rows(grid, idx, a_refs, a_tags, wa, sem_a)
    get_v = fetch_rows(grid, idx, a_refs, a_tags, wv, sem_v, COL_VALUES)
    unit, inverse = norm_stats(x_ref[...].astype(F32))
    wait_all(get_a)
    n1g = dot_nt(late_ref[:, :COL_VG], wa[:, :COL_ROUTER])
    b = n1g * gain_row(wa[:, COL_SEL:COL_ROUTER], LANE_GAIN_ONE)
    wait_all(get_v)
    gt_ref[...] = rg_ref[...] + dot_nt(vag_ref[...], wv[...]) + norm_back(b, unit, inverse)


def stacked(refs, first=0, last=None):
    return jnp.concatenate([r[:, first:last] for r in refs], axis=0)


def in_order(grid, idx, ref, first=0, size=None):
    size = ref.shape[2] - first if size is None else size
    return jnp.concatenate(
        [ref[shard_at(grid, idx, k, r), :, pl.ds(first, size)] for k, r in dp_tags(grid)], axis=0
    )


def by_owner(grid, idx, out_refs, value, first=0):
    X, Z = grid.X, grid.Z
    mine = value.shape[0] // (X * Z)
    columns = pl.ds(first, value.shape[1])
    for z in range(Z):
        blocks = [value[(z * X + x) * mine : (z * X + x + 1) * mine] for x in range(X)]
        for j in range(X):
            chosen = blocks[0]
            for x in range(1, X):
                chosen = jnp.where(lax.rem(idx[3] + j, X) == x, blocks[x], chosen)
            out_refs[j][z, :, columns] = chosen.astype(BF)


def grad_out_kernel(grid, idx, early, *refs):
    nd = grid.nd
    bgs, out = refs[:nd], refs[nd:]
    wide = H * DH
    gate = in_order(grid, idx, early, wide)
    att = in_order(grid, idx, early, 0, wide)
    by_owner(grid, idx, out, dot_tn(stacked(bgs), mixed_of(gate, att, HE)))


def own_columns(grid, idx, cols, which):
    piece = cols.shape[2] // (3 * grid.nd)
    at = which * piece * grid.nd + shard_at(grid, idx, 0, 0) * piece
    return in_order(grid, idx, cols, pl.multiple_of(at, piece), piece)


def grad_rest_kernel(grid, idx, cols, early, a_ref, *refs):
    nd = grid.nd
    late, out = refs[:nd], refs[nd:]
    x, n1, n2 = [own_columns(grid, idx, cols, i) for i in range(3)]
    acts = stacked(late)
    both = dot_tn(n1, acts[:, :COL_VG])
    by_owner(grid, idx, out, both[:, :COL_SEL])
    misc = a_ref[:, COL_SEL:COL_ROUTER].astype(F32)
    stats = in_order(grid, idx, early, H * DH)
    unit = (x.astype(F32) - col(stats, LANE_MEAN)) * col(stats, LANE_INVERSE)
    n1_grad = dot_nt(acts[:, :COL_VG], a_ref[:, :COL_ROUTER])
    n2_grad = dot_nt(acts[:, COL_RG:], a_ref[:, COL_ROUTER:])
    one = jnp.sum(n1_grad * unit, axis=0, keepdims=True)
    gains = jnp.transpose(misc)[LANE_GAIN_TWO : LANE_GAIN_TWO + 1]
    two = jnp.sum(n2_grad * n2.astype(F32), axis=0, keepdims=True) / gains
    row = rows_of((LANES, one.shape[1]))
    extra = jnp.where(row == LANE_GAIN_ONE, one, 0.0)
    extra = jnp.where(row == LANE_GAIN_TWO, two, extra)
    by_owner(grid, idx, out, both[:, COL_SEL:] + jnp.transpose(extra), COL_SEL)
    by_owner(grid, idx, out, dot_tn(n2, acts[:, COL_RG:]), COL_ROUTER)
    mixed = mixed_of(stats, acts[:, COL_VG:COL_RG].astype(F32), 0)
    by_owner(grid, idx, out, dot_tn(x, mixed), COL_VALUES)


def finish_kernel(*refs):
    parts, (q, k, v, vs, os, router, one, two) = refs[:-8], refs[-8:]
    total = parts[0][...].astype(F32)
    for ref in parts[1:]:
        total = total + ref[...].astype(F32)
    wide = H * DH
    q[...] = total[:, :wide]
    k[...] = total[:, wide:COL_SEL]
    misc = total[:, COL_SEL:COL_ROUTER]
    turned = jnp.transpose(misc)
    vs[...] = turned[:HE]
    os[...] = turned[HE : 2 * HE]
    one[...] = turned[LANE_GAIN_ONE : LANE_GAIN_ONE + 1]
    two[...] = turned[LANE_GAIN_TWO : LANE_GAIN_TWO + 1]
    router[...] = total[:, COL_ROUTER:COL_VALUES]
    v[...] = total[:, COL_VALUES:]


def shape(dims, dtype):
    return jax.ShapeDtypeStruct(dims, dtype)


def call(name, kernel, operands, specs, outs, scratch=(), mib=58, us=5, aliases=None):
    outs = [o if isinstance(o, tuple) else (o, VMEM) for o in outs]
    operands = [
        o if s is SMEM else pltpu.with_memory_space_constraint(o, pltpu.HBM)
        for o, s in zip(operands, specs, strict=True)
    ]
    return pl.pallas_call(
        kernel,
        out_shape=tuple(pltpu.HBM(o[0].shape, o[0].dtype) for o in outs),
        in_specs=list(specs),
        out_specs=tuple(o[1] for o in outs),
        scratch_shapes=list(scratch),
        input_output_aliases=aliases or {},
        compiler_params=pltpu.CompilerParams(vmem_limit_bytes=mib * 1024 * 1024),
        cost_estimate=pl.CostEstimate(
            flops=us, bytes_accessed=us, transcendentals=0
        ),
        name=name,
    )(*operands)


def dma(n):
    return pltpu.SemaphoreType.DMA((n,))


def per_device(
    nd,
    ne,
    tokens,
    cotangent,
    segments,
    value_picks,
    output_picks,
    expert_picks,
    attn_gain,
    query_weight,
    key_weight,
    value_weight,
    output_expert_weight,
    value_select,
    output_select,
    moe_gain,
    router_weight,
    up_weight,
    down_weight,
):
    grid = Grid(nd, ne)
    X, Y, Z, C = grid.X, grid.Y, grid.Z, grid.C
    micros, length, width = tokens.shape
    rows = micros * length
    local = up_weight.shape[0]
    piece = width // nd
    wide = H * DH
    values_wide = HE * DH
    dp, ex = lax.axis_index("dp"), lax.axis_index("expert")
    idx = jnp.stack([dp // C, dp % C, ex // X, ex % X]).astype(jnp.int32)


    x_all = tokens.reshape(rows, width)
    g_all = cotangent.reshape(rows, width)

    ends = (*STARTS[1:], COL_A)
    block_w, block_a, *parts_a = call(
        "pack",
        functools.partial(pack_kernel, grid),
        (
            idx,
            query_weight,
            key_weight,
            value_select.T,
            output_select.T,
            attn_gain,
            moe_gain,
            router_weight,
            value_weight,
            output_expert_weight,
        ),
        [SMEM] + [VMEM] * 9,
        [shape((piece, COL_A), BF), shape((piece, COL_VALUES), BF)]
        + [shape((piece // X, high - low), BF) for low, high in zip(STARTS, ends)],
        [pltpu.VMEM((LANES, piece), F32)],
        us=3,
    )

    def to_y(v, *deps):
        v = after(v, *deps)
        return [grid.rot_y(v, k) for k in range(1, Y)]

    def over_x(got_y, *deps):
        return [[v] + [grid.rot_x(after(v, *deps), j) for j in range(1, X)] for v in got_y]

    def add_pieces(arrays, tags, v, tag, swapped=None):
        k, split, j, column = tag
        arrays.append(v)
        tags.append((k, 0, split, j, column))
        if C > 1:
            arrays.append(grid.swap(v) if swapped is None else swapped)
            tags.append((k, 1, split, j, column))

    def swap(v, *deps):
        return grid.swap(after(v, *deps)) if C > 1 else None

    def spread_x(got_y, *deps):
        return [[v] + [grid.rot_x(after(v, *deps), j) for j in range(1, X)] for v in got_y]

    def swap_all(values, *deps):
        return [swap(v, *deps) for v in values]

    def flat(by_k):
        return [v for by_j in by_k for v in by_j]

    g_gathered = lax.all_gather(g_all, "expert", axis=0, tiled=True)
    swap_w = swap(block_w)
    seg = segments.reshape(1, rows)
    v_picks, o_picks = value_picks.reshape(rows, 2 * H), output_picks.reshape(rows, 2 * H)
    e_picks = expert_picks.reshape(rows, -1)
    done = [swap_w, seg, v_picks, o_picks, e_picks]
    over_y, over_x_too, swap_y, swap_x = [to_y(parts_a[0])], [], [], []
    done.append(over_y[0])
    swap_d = swap_u = d_y = None
    for i in range(len(STARTS)):
        last_round = i == len(STARTS) - 1
        new = []
        if not last_round:
            over_y.append(to_y(parts_a[i + 1], *done))
            new += over_y[-1]
        else:
            d_y = to_y(down_weight, *done)
            swap_u = swap(up_weight, *done)
            new += [swap_u, g_gathered]
        if i == len(STARTS) - 2:
            swap_d = swap(down_weight, *done)
            new.append(swap_d)
        over_x_too.append(spread_x(over_y[i], *done))
        swap_y.append(swap_all(over_y[i], *done))
        new += flat(over_x_too[-1]) + swap_y[-1]
        if i:
            swap_x.append([swap_all(by_j[1:], *done) for by_j in over_x_too[i - 1]])
            new += flat(swap_x[-1])
        done = new
    def weight_pieces(own, swapped, chunks):
        arrays, tags = [own, swapped], [(0, 0, None, 0, 0), (0, 1, None, 0, 0)]
        for column, got, others in chunks:
            for k, (by_j, swaps) in enumerate(zip(got, others), 1):
                for j, (v, o) in enumerate(zip(by_j, swaps)):
                    split = "x" if len(by_j) > 1 else None
                    arrays += [v, o]
                    tags += [(k, 0, split, j, column), (k, 1, split, j, column)]
        return arrays, tags

    def all_chunks():
        return [
            (low, got, [[v] + more for v, more in zip(ys, xs)])
            for low, got, ys, xs in zip(STARTS, over_x_too, swap_y, swap_x)
        ]

    first_pieces, first_tags = weight_pieces(block_w, swap_w, all_chunks()[:1])

    n1, qk, sig, mask, probs, wmr = call(
        "attend",
        functools.partial(attend_kernel, grid, first_tags, length),
        (
            idx,
            x_all,
            seg,
            v_picks,
            o_picks,
            *first_pieces,
        ),
        [SMEM] + [VMEM] * 4 + [ANY] * len(first_pieces),
        [
            shape((rows, width), BF),
            shape((rows, 2 * wide), BF),
            shape((rows, LANES), F32),
            shape((rows, LANES), F32),
            shape((rows, H * rows), F32),
            shape((width, 2 * LANES), BF),
        ],
        [pltpu.VMEM((width, COL_VALUES), BF), dma(len(first_pieces))],
        us=4,
    )
    swap_x.append([swap_all(by_j[1:], n1, *done) for by_j in over_x_too[-1]])
    a_pieces, a_tags = weight_pieces(block_w, swap_w, all_chunks())
    v_pieces, v_tags = window(a_pieces, a_tags, COL_VALUES, COL_OUT)
    o_pieces, o_tags = window(a_pieces, a_tags, COL_OUT, COL_A)
    vals, va, early, res, router, picked, xg, cols = call(
        "route",
        functools.partial(route_kernel, grid, v_tags, o_tags),
        (idx, x_all, n1, sig, mask, probs, wmr, e_picks, *v_pieces, *o_pieces),
        [SMEM] + [VMEM] * 7 + [ANY] * (len(v_pieces) + len(o_pieces)),
        [
            shape((rows, wide), BF),
            shape((rows, values_wide), F32),
            shape((rows, wide + LANES), F32),
            shape((rows, width), F32),
            shape((rows, EXPERTS), F32),
            shape((rows, EXPERTS), F32),
            shape((rows, width + EXPERTS), BF),
            shape((rows, 3 * width), BF),
        ],
        [
            pltpu.VMEM((width, values_wide), BF),
            pltpu.VMEM((width, values_wide), BF),
            dma(len(v_pieces)),
            dma(len(o_pieces)),
        ],
        us=8,
    )

    group = ne * length
    ff = local * LANES
    swap_dy = swap_all(d_y, xg)
    u_y = to_y(up_weight, xg, *d_y)
    column, x_over, done = [xg], [], []
    for k in range(1, Z):
        held = after(column[-1], *done)
        column.append(grid.rot_z(held, 1))
        x_over.append([grid.rot_x(held, j) for j in range(1, X)])
        last_done, done = done, [column[-1], x_over[-1]]
    ring_done = done

    def expert_pieces(own, swapped, got, others):
        arrays, tags = [own, swapped], [(0, 0, 0), (0, 1, 0)]
        for k, (v, o) in enumerate(zip(got, others), 1):
            arrays += [v, o]
            tags += [(k, 0, 0), (k, 1, 0)]
        return arrays, tags

    d_pieces, d_tags = expert_pieces(down_weight, swap_d, d_y, swap_dy)
    g_rows = g_gathered.reshape(ne, micros, length, width)
    total = micros * group
    (ahead,) = call(
        "ahead",
        functools.partial(ahead_kernel, grid, d_tags),
        (idx, after(g_rows, *last_done), *d_pieces),
        [SMEM] + [ANY] * (1 + len(d_tags)),
        [(shape((total, ff), BF), ANY)],
        [
            pltpu.VMEM((ne, micros, length, width), BF),
            pltpu.VMEM((local, LANES, width), BF),
            pltpu.VMEM((total, ff), BF),
            dma(1),
            dma(len(d_tags)),
            dma(local // 2),
        ],
        us=9,
    )
    x_over.append([grid.rot_x(after(column[-1], ahead, *ring_done), j) for j in range(1, X)])
    x_pieces = column + [by_j[j] for j in range(X - 1) for by_j in x_over]
    swap_uy = swap_all(u_y, *flat(x_over))
    u_pieces, u_tags = expert_pieces(up_weight, swap_u, u_y, swap_uy)
    froms = []

    def over_x(parts):
        return [grid.rot_x(parts[j], -j) for j in range(1, X)]

    def fold(parts, others, *deps):
        return call(
            "fold",
            fold_kernel,
            (idx, after(parts[0], *deps), *others),
            [SMEM] + [VMEM] * X,
            [shape(parts[0].shape[1:], BF)] * Z,
            us=2,
        )

    sent, shared = [], []
    for m in range(micros):
        hg, pg, x_group, *back = call(
            "experts",
            functools.partial(expert_kernel, grid, u_tags, m, micros),
            (idx, ahead, *x_pieces, *u_pieces, *shared),
            [SMEM, ANY] + [ANY] * (ne + len(u_tags) + len(shared)),
            [
                (shape((total, ff), BF), ANY),
                (shape((total, ff), BF), ANY),
                (shape((total, width + EXPERTS), BF), ANY),
                *[shape((Z, length, width + EXPERTS), BF)] * X,
            ],
            [
                pltpu.VMEM((group, ff), BF),
                pltpu.VMEM((group, ff), BF),
                pltpu.VMEM((group, width + EXPERTS), BF),
                pltpu.VMEM((group, ff), BF),
                pltpu.VMEM((local, width, LANES), BF),
                pltpu.VMEM((group, EXPERTS), F32),
                pltpu.VMEM((group, max(piece, EXPERTS)), F32),
                dma(ne),
                dma(len(u_tags)),
                dma(1),
                dma(3),
            ],
            us=12,
            aliases={2 + ne + len(u_tags) + i: i for i in range(len(shared))},
        )
        shared = [hg, pg, x_group]
        sent.append(back)

    def out_rows(*deps):
        return call(
            "out",
            functools.partial(out_kernel, grid, d_tags, micros),
            (idx, after(hg, *deps), *d_pieces),
            [SMEM] + [ANY] * (1 + len(d_tags)),
            [shape((ne, rows, width), BF)],
            [
                pltpu.VMEM((total, ff), BF),
                pltpu.VMEM((local, LANES, width), BF),
                dma(1),
                dma(len(d_tags)),
            ],
            us=10,
        )

    def expert_grad(name, kernel, lhs, rhs, dims, *deps):
        halves = 2
        block = pl.BlockSpec((Y, local // halves, *dims), lambda h, idx: (0, h, 0, 0))
        if lhs.ndim == 4:
            whole = pl.BlockSpec((ne, micros, length, width), lambda h, idx: (0, 0, 0, 0))
        else:
            whole = pl.BlockSpec((total, width), lambda h, idx: (0, 0))
        part = (width, ff // halves) if lhs.ndim == 2 else (ff // halves, width)
        return pl.pallas_call(
            functools.partial(kernel, grid),
            out_shape=[pltpu.HBM((Y, local, *dims), BF)] * C,
            grid_spec=pltpu.PrefetchScalarGridSpec(
                num_scalar_prefetch=1,
                grid=(halves,),
                in_specs=[whole, pl.BlockSpec((total, ff // halves), lambda h, idx: (0, h))],
                out_specs=[block] * C,
                scratch_shapes=[pltpu.VMEM(part, F32)],
            ),
            compiler_params=pltpu.CompilerParams(vmem_limit_bytes=58 * 1024 * 1024),
            cost_estimate=pl.CostEstimate(flops=4, bytes_accessed=12, transcendentals=0),
            name=name,
        )(idx, *[pltpu.with_memory_space_constraint(v, pltpu.HBM) for v in (after(lhs, *deps), rhs)])

    def added_blocks(name, arrays, dtype, split):
        steps = 2
        dims = arrays[0].shape[1:] if split else arrays[0].shape
        some = (dims[0] // steps, *dims[1:])
        one = pl.BlockSpec(some, lambda i: (i, 0, 0))
        spec = pl.BlockSpec((Y, *some), lambda i: (0, i, 0, 0)) if split else one
        results = Y if split else 1

        def kernel(*refs):
            for k, out in enumerate(refs[len(arrays) :]):
                total = 0.0
                for ref in refs[: len(arrays)]:
                    total = total + (ref[k] if split else ref[...]).astype(F32)
                out[...] = total.astype(dtype)

        return pl.pallas_call(
            kernel,
            out_shape=[pltpu.HBM(dims, dtype)] * results,
            grid=(steps,),
            in_specs=[spec] * len(arrays),
            out_specs=[one] * results,
            compiler_params=pltpu.CompilerParams(vmem_limit_bytes=58 * 1024 * 1024),
            cost_estimate=pl.CostEstimate(flops=1, bytes_accessed=3, transcendentals=0),
            name=name,
        )(*[pltpu.with_memory_space_constraint(v, pltpu.HBM) for v in arrays])

    down_args = ("down_grad", down_grad_kernel, g_rows, hg, (LANES, piece))
    up_args = ("up_grad", up_grad_kernel, x_group, pg, (piece, LANES))

    def reduce_y(total, *deps):
        got = [grid.rot_y(after(total[k], *deps), k) for k in range(1, Y)]
        return lambda *more: added_blocks("last_sum", [after(total[0], *more), *got], F32, False)[0], got

    from_x = [over_x(v) for v in sent]
    sums = fold(sent[0], from_x[0], hg)
    froms.append(grid.send_z(sums))
    outs_sent = out_rows(sums[0])
    before, down_came, up_came = outs_sent[0], [], []
    for m in range(1, micros):
        sums = fold(sent[m], from_x[m], before, froms[-1])
        froms.append(grid.send_z(sums))
        before = sums[0]
    down_near, *down_far = expert_grad(*down_args, before)
    up_near, *up_far = expert_grad(*up_args, down_near)
    before = up_near

    early_all = lax.all_gather(after(early, u_pieces), "dp", axis=0)
    cols_all = lax.all_gather(after(cols, u_pieces), "dp", axis=0)
    res_grad, bg, rg, *bg_cols = call(
        "back_norm",
        functools.partial(back_norm_kernel, grid, micros),
        (
            idx,
            wmr,
            res,
            g_all,
            after(router, before, early_all, cols_all),
            picked,
            *[p for f in froms for p in f],
        ),
        [SMEM] + [VMEM] * (5 + micros * Z),
        [
            shape((rows, width), F32),
            shape((rows, width), BF),
            shape((rows, EXPERTS), BF),
            *[shape((rows, piece), BF)] * nd,
        ],
        us=3,
    )
    bgs = [v if t == (0, 0) else grid.rot_yc(v, *t) for v, t in zip(bg_cols, dp_tags(grid))]
    late, vag = call(
        "back_attend",
        functools.partial(back_attend_kernel, grid, o_tags),
        (idx, bg, rg, sig, mask, early, qk, vals, va, probs, *o_pieces),
        [SMEM] + [VMEM] * 9 + [ANY] * len(o_pieces),
        [shape((rows, COL_LATE), BF), shape((rows, values_wide), BF)],
        [pltpu.VMEM((width, values_wide), BF), dma(len(o_pieces))],
        us=8,
    )
    outs = lax.all_to_all(after(outs_sent[0], bg), "expert", 0, 0, tiled=True)
    down_came, up_came = swap_all(down_far, bg), swap_all(up_far, bg)
    late_swap = swap(late, bgs[1:], *down_came, *up_came)
    late_y = to_y(late, bgs[1:])

    mine = piece // ne

    def weight_grad(name, kernel, operands, columns):
        parts = call(
            name,
            functools.partial(kernel, grid),
            (idx, *operands),
            [SMEM] + [VMEM] * len(operands),
            [shape((Z, mine, columns), BF)] * X,
            us=3,
        )
        return parts, [grid.rot_x(parts[j], j) for j in range(1, X)]

    def fold_at(parts, others, *deps):
        sums = call(
            "fold_at",
            fold_at_kernel,
            (idx, after(parts[0], *deps), *others),
            [SMEM] + [VMEM] * X,
            [shape(parts[0].shape[1:], BF)] * Z,
            us=1,
        )
        return sums[0], grid.send_z(sums)

    def added(parts, *deps):
        return call(
            "sum",
            sum_kernel,
            (after(parts[0], *deps), *parts[1:]),
            [VMEM] * len(parts),
            [shape(parts[0].shape, F32)],
            us=1,
        )[0]

    down_sum = added_blocks("core_sum", [after(down_near, late), *down_came], BF, True)
    up_sum = added_blocks("core_sum", [after(up_near, down_sum), *up_came], BF, True)
    o_parts, o_others = weight_grad(
        "grad_out", grad_out_kernel, [after(early_all, up_sum), *bgs], values_wide
    )
    down_last, down_got = reduce_y(down_sum, late_y)
    up_last, up_got = reduce_y(up_sum, late_y)
    late_all = [late, *late_y, late_swap, *swap_all(late_y, o_parts[0])]
    r_parts, r_others = weight_grad(
        "grad_rest",
        grad_rest_kernel,
        [after(cols_all, o_parts[0]), early_all, block_a, *late_all],
        COL_OUT,
    )
    (grad_tokens,) = call(
        "back_token",
        functools.partial(back_token_kernel, grid, a_tags),
        (idx, x_all, res_grad, after(late, r_parts[0]), vag, *a_pieces),
        [SMEM] + [VMEM] * 4 + [ANY] * len(a_pieces),
        [shape((rows, width), F32)],
        [
            pltpu.VMEM((width, COL_VALUES), BF),
            pltpu.VMEM((width, values_wide), BF),
            dma(len(a_pieces)),
            dma(len(a_pieces)),
        ],
        us=8,
    )
    o_fold, o_sums = fold_at(o_parts, o_others, grad_tokens)
    r_fold, r_sums = fold_at(r_parts, r_others, o_sums, outs)
    grad_down = down_last(r_fold)
    grad_up = up_last(grad_down)
    (output,) = call(
        "add_out",
        sum_places_kernel,
        (outs, after(res, r_fold)),
        [VMEM] * 2,
        [shape((rows, width), F32)],
        us=2,
    )
    grad_output = added(o_sums, output)
    q, k, grad_value, vs, os, r, one, two = call(
        "finish",
        finish_kernel,
        (after(r_sums[0], grad_tokens, output, grad_output, grad_up), *r_sums[1:]),
        [VMEM] * Z,
        [
            shape((mine, wide), F32),
            shape((mine, wide), F32),
            shape((mine, values_wide), F32),
            shape((HE, mine), F32),
            shape((HE, mine), F32),
            shape((mine, EXPERTS), F32),
            shape((1, mine), F32),
            shape((1, mine), F32),
        ],
        us=1,
    )
    return (
        output.reshape(micros, length, width),
        grad_tokens.reshape(micros, length, width),
        one.reshape(mine),
        q,
        k,
        grad_value,
        grad_output,
        vs.T,
        os.T,
        two.reshape(mine),
        r,
        grad_up,
        grad_down,
    )


def solution(mesh):
    rows = ("dp", "expert")
    placed = (
        P(None, rows, None),
        P(None, rows, None),
        P(None, rows, None),
        P(None, rows, None, None),
        P(None, rows, None, None),
        P(None, rows, None),
        P("dp"),
        P("dp", None),
        P("dp", None),
        P("dp", None),
        P("dp", None),
        P("dp", None),
        P("dp", None),
        P("dp"),
        P("dp", None),
        P("expert", "dp", None),
        P("expert", None, "dp"),
    )
    return jax.shard_map(
        functools.partial(per_device, mesh.shape["dp"], mesh.shape["expert"]),
        mesh=mesh,
        in_specs=placed,
        out_specs=(
            P(None, rows, None),
            P(None, rows, None),
            P(rows),
            P(rows, None),
            P(rows, None),
            P(rows, None),
            P(rows, None),
            P(rows, None),
            P(rows, None),
            P(rows),
            P(rows, None),
            P("expert", "dp", None),
            P("expert", None, "dp"),
        ),
        check_vma=False,
    )
```
